32 devices in a mesh: canvas: 4 (over y, x), rows: 8 (over z, core).
Axes of the slice: x: 2, y: 2, z: 4, core: 2. Of those that a mesh axis runs over, the one named last changes fastest.
Arguments:
- inputs: bfloat16 [4, 32, 384, 64], P('canvas', 'rows'), may hold values from -6 to 6
- coarse: bfloat16 [4, 16, 192, 256], P('canvas', 'rows'), may hold values from -6 to 6
- row_cuts: int32 [4, 32], P('canvas'), may hold values 0 or 1
- col_cuts: int32 [4, 384], P('canvas'), may hold values 0 or 1
- w_first: bfloat16 [3, 3, 64, 128], replicated, may hold values from -0.25 to 0.25
- b_first: bfloat16 [128], replicated, may hold values from -3 to 3
- w_second: bfloat16 [3, 3, 128, 128], replicated, may hold values from -0.1875 to 0.1875
- b_second: bfloat16 [128], replicated, may hold values from -3 to 3
- w_up: bfloat16 [2, 2, 256, 128], replicated, may hold values from -0.375 to 0.375
- b_up: bfloat16 [128], replicated, may hold values from -3 to 3
- w_third: bfloat16 [3, 3, 256, 128], replicated, may hold values from -0.125 to 0.125
- b_third: bfloat16 [128], replicated, may hold values from -3 to 3
- w_fourth: bfloat16 [3, 3, 128, 128], replicated, may hold values from -0.1875 to 0.1875
- b_fourth: bfloat16 [128], replicated, may hold values from -3 to 3
- cot_out: bfloat16 [4, 32, 384, 128], P('canvas', 'rows'), may hold values from -6 to 6
- cot_pool: bfloat16 [4, 16, 192, 128], P('canvas', 'rows'), may hold values from -12 to 12
Outputs:
- activations: bfloat16 [4, 32, 384, 128], P('canvas', 'rows')
- pooled: bfloat16 [4, 16, 192, 128], P('canvas', 'rows')
- grad_inputs: bfloat16 [4, 32, 384, 64], P('canvas', 'rows')
- grad_coarse: bfloat16 [4, 16, 192, 256], P('canvas', 'rows')
- grad_w_first: float32 [3, 3, 64, 128], P(None, None, None, 'rows')
- grad_b_first: float32 [128], P('rows')
- grad_w_second: float32 [3, 3, 128, 128], P(None, None, None, 'rows')
- grad_b_second: float32 [128], P('rows')
- grad_w_up: float32 [2, 2, 256, 128], P(None, None, None, 'rows')
- grad_b_up: float32 [128], P('rows')
- grad_w_third: float32 [3, 3, 256, 128], P(None, None, None, 'rows')
- grad_b_third: float32 [128], P('rows')
- grad_w_fourth: float32 [3, 3, 128, 128], P(None, None, None, 'rows')
- grad_b_fourth: float32 [128], P('rows')
The draws below stay inside these ranges and needn't reach their ends.
All inputs are finite; a program needn't handle non-finite values. No bound on the sum of `row_cuts` or of `col_cuts` on one device may be relied on, other than what follows from the above.
Results may differ from the reference program's by a relative error of at most 0.013.
Values may be sent and summed in bfloat16 or wider, within the bound.
A program may use at most 64 MiB of HBM per device.

```python
import jax
import jax.numpy as jnp
from jax import lax

C_IN = 64
CH = 128
C_COARSE = 256
W = 384
CANVASES = 4
H = 32


def touch_ends(result, rng, low, high):
    longest = result.shape.index(max(result.shape))
    spots = []
    for shift in (0, 1):
        where = [jax.random.randint(jax.random.fold_in(rng, axis), (), 0, length) for axis, length in enumerate(result.shape)]
        where[longest] = (where[longest] + shift) % result.shape[longest]
        spots.append(tuple(where))
    return result.at[spots[0]].set(low).at[spots[1]].set(high)


def with_spikes(array, stream_key, source, target, parts, factor):
    owner, partner = [(jnp.arange(array.shape[position]) // (array.shape[position] // parts)).reshape([-1 if axis == position else 1 for axis in range(array.ndim)]) for position in (source, target)]
    chosen = jax.random.permutation(stream_key, parts)[partner]
    strong = (owner == chosen) | (owner == (partner + parts // 2) % parts)
    return jnp.where(strong, factor * array, array)


def block_scale(own_key, dims, shards, low, high):
    def one(dim, shards_of):
        draws = jax.random.uniform(jax.random.fold_in(jax.random.fold_in(own_key, 6), dim), (shards_of,), jnp.float32, low / len(shards), high / len(shards))
        return jnp.repeat(jnp.exp(draws), dims[dim] // shards_of).reshape((-1,) + (1,) * (len(dims) - dim - 1))

    gain = one(*shards[0])
    for cut in shards[1:]:
        gain = gain * one(*cut)
    return gain


def centred(key, shape, scale, bound, shards=(), kind=jnp.bfloat16):
    factor_of = block_scale(key, shape, shards, -0.22, 0.18) if shards else 1.0
    array = jax.random.normal(key, shape, jnp.float32) * scale * factor_of
    return jnp.minimum(jnp.maximum(array, -bound), bound).astype(kind)


def heavy_noise(own_key, extent, scale, reach, split, heavy, kind=jnp.bfloat16):
    array = scale * jax.random.normal(own_key, extent, jnp.float32)
    if split:
        array = array * block_scale(own_key, extent, split, -0.22, 0.18)
    return jnp.clip(with_spikes(array, jax.random.fold_in(own_key, 3), *heavy), -reach, reach).astype(kind)


def setup_inputs(seed: int = 0) -> dict:
    keys = jax.random.split(jax.random.key(seed), 17)
    return {
        "inputs": centred(keys[0], (CANVASES, H, W, C_IN), 1.0, 6.0, ((0, 4), (1, 8))),
        "coarse": centred(keys[1], (CANVASES, H // 2, W // 2, C_COARSE), 1.0, 6.0, ((0, 4), (1, 8))),
        "row_cuts": touch_ends((jax.random.randint(keys[2], (CANVASES, H), 0, 8) < 1).astype(jnp.int32), jax.random.fold_in(keys[2], 1), 0, 1),
        "col_cuts": touch_ends((jax.random.randint(keys[3], (CANVASES, W), 0, 8) < 1).astype(jnp.int32), jax.random.fold_in(keys[3], 1), 0, 1),
        "w_first": centred(keys[4], (3, 3, C_IN, CH), (9 * C_IN) ** -0.5, 0.25),
        "b_first": centred(keys[5], (CH,), 0.5, 3.0),
        "w_second": centred(keys[6], (3, 3, CH, CH), (9 * CH) ** -0.5, 0.1875),
        "b_second": centred(keys[7], (CH,), 0.5, 3.0),
        "w_up": centred(keys[8], (2, 2, C_COARSE, CH), C_COARSE ** -0.5, 0.375),
        "b_up": centred(keys[9], (CH,), 0.5, 3.0),
        "w_third": centred(keys[10], (3, 3, 2 * CH, CH), (18 * CH) ** -0.5, 0.125),
        "b_third": centred(keys[11], (CH,), 0.5, 3.0),
        "w_fourth": centred(keys[12], (3, 3, CH, CH), (9 * CH) ** -0.5, 0.1875),
        "b_fourth": centred(keys[13], (CH,), 0.5, 3.0),
        "cot_out": heavy_noise(keys[14], (CANVASES, H, W, CH), 1.0, 6.0, ((0, 4), (1, 8)), (1, 3, 8, 2.0)),
        "cot_pool": centred(keys[15], (CANVASES, H // 2, W // 2, CH), 2.0, 12.0, ((0, 4), (1, 8))),
    }


@jax.custom_vjp
def low(v):
    return lax.optimization_barrier(v.astype(jnp.bfloat16)).astype(jnp.float32)

@jax.custom_vjp
def low_back(v):
    return v

def low_keep(v):
    return (low(v), None)

def low_pass(kept, grad):
    return (grad,)

def back_keep(v):
    return (v, None)

def back_low(kept, grad):
    return (low(grad),)
low.defvjp(low_keep, low_pass)
low_back.defvjp(back_keep, back_low)

def row_valid(cut_flags, first_row, length):
    padded = jnp.pad(cut_flags, ((0, 0), (1, 2)))
    segment = lax.dynamic_slice_in_dim(padded, first_row + 1, length + 1, 1).astype(jnp.float32)
    above_ok = 1.0 - segment[:, :length]
    below_ok = 1.0 - segment[:, 1:]
    return jnp.stack([above_ok, jnp.ones_like(above_ok), below_ok])

def column_shift(tensor, step):
    if step == 0:
        return tensor
    zero_col = jnp.zeros_like(tensor[:, :, :1])
    if step > 0:
        return jnp.concatenate([tensor[:, :, 1:], zero_col], 2)
    return jnp.concatenate([zero_col, tensor[:, :, :-1]], 2)

def tap_stack(padded, col_gates, row_step, length):
    slab = padded[:, 1 + row_step:1 + row_step + length]
    shifted = [column_shift(slab, col_step) * col_gates[col_step + 1][:, None, :, None].astype(slab.dtype) for col_step in (-1, 0, 1)]
    return jnp.concatenate(shifted, 3)

def conv_layer(values, kernel, bias, row_gates, col_gates):
    padded = jnp.pad(values, ((0, 0), (1, 1), (0, 0), (0, 0)))
    length = values.shape[1]
    outputs = kernel.shape[3]
    running = jnp.zeros(values.shape[:3] + (outputs,), jnp.float32) + bias
    for row_step in (-1, 0, 1):
        stacked = tap_stack(padded, col_gates, row_step, length)
        product = jnp.dot(stacked, kernel[row_step + 1].reshape(-1, outputs), precision=lax.Precision.HIGHEST, preferred_element_type=jnp.float32)
        running = running + row_gates[row_step + 1][:, :, None, None] * product
    return running

def unet_level(canvas_map, coarse_map, params, row_gates, col_gates):
    w_first, b_first, w_second, b_second, w_up, b_up, w_third, b_third, w_fourth, b_fourth = params
    pre_first = low_back(conv_layer(canvas_map, w_first, b_first, row_gates, col_gates))
    act_first = low(jax.nn.silu(pre_first))
    pre_second = low_back(conv_layer(act_first, w_second, b_second, row_gates, col_gates))
    act_second = low(jax.nn.silu(pre_second))
    batch, height, col_count, channels = act_second.shape
    pooled_map = lax.optimization_barrier(jnp.mean(act_second.reshape(batch, height // 2, 2, col_count // 2, 2, channels), axis=(2, 4)))
    spread = jnp.einsum('nijk,abko->niajbo', coarse_map, w_up, precision=lax.Precision.HIGHEST)
    up_map = spread.reshape(batch, height, col_count, w_up.shape[3]) + b_up
    up_map = low(low_back(up_map))
    joined = jnp.concatenate([up_map, act_second], 3)
    pre_third = low_back(conv_layer(joined, w_third, b_third, row_gates, col_gates))
    act_third = low(jax.nn.silu(pre_third))
    pre_fourth = low_back(conv_layer(act_third, w_fourth, b_fourth, row_gates, col_gates))
    return (jax.nn.silu(pre_fourth), pooled_map)

def reference(inputs, coarse, row_cuts, col_cuts, w_first, b_first, w_second, b_second, w_up, b_up, w_third, b_third, w_fourth, b_fourth, cot_out, cot_pool):
    params = tuple((member.astype(jnp.float32) for member in (w_first, b_first, w_second, b_second, w_up, b_up, w_third, b_third, w_fourth, b_fourth)))

    def per_canvas(totals, canvas_items):
        canvas_map, coarse_map, row_flags, col_flags, cot_act, cot_low = canvas_items
        row_gates = row_valid(row_flags[None], 0, row_flags.shape[0])
        col_gates = row_valid(col_flags[None], 0, col_flags.shape[0])

        def forward(canvas_in, coarse_in, weights):
            return unet_level(canvas_in, coarse_in, weights, row_gates, col_gates)
        results, pullback = jax.vjp(forward, canvas_map[None].astype(jnp.float32), coarse_map[None].astype(jnp.float32), params)
        gradients = pullback((cot_act[None].astype(jnp.float32), cot_low[None].astype(jnp.float32)))
        totals = tuple((running + member for running, member in zip(totals, gradients[2])))
        return (totals, (results[0][0].astype(jnp.bfloat16), results[1][0].astype(jnp.bfloat16), gradients[0][0].astype(jnp.bfloat16), gradients[1][0].astype(jnp.bfloat16)))
    start_sums = tuple((jnp.zeros(member.shape, jnp.float32) for member in params))
    totals, mapped = lax.scan(per_canvas, start_sums, (inputs, coarse, row_cuts, col_cuts, cot_out, cot_pool))
    return (mapped[0], mapped[1], mapped[2], mapped[3], totals[0], totals[1], totals[2], totals[3], totals[4], totals[5], totals[6], totals[7], totals[8], totals[9])
```

```python
import functools

import jax
import jax.numpy as jnp
from jax import lax
from jax.experimental import pallas as pl
from jax.experimental.pallas import tpu as pltpu
from jax.sharding import PartitionSpec as P

MESH = pl.DeviceIdType.MESH
BF = jnp.bfloat16
F32 = jnp.float32
VMEM_BYTES = 58 * 2**20

OPERANDS = (
    "inputs",
    "coarse",
    "row_cuts",
    "col_cuts",
    "w_first",
    "b_first",
    "w_second",
    "b_second",
    "w_up",
    "b_up",
    "w_third",
    "b_third",
    "w_fourth",
    "b_fourth",
    "cot_out",
    "cot_pool",
)
LAYERS = ("fourth", "third", "up", "second", "first")


def dot_nn(a, b):
    return lax.dot_general(a, b, (((1,), (0,)), ((), ())), preferred_element_type=F32)


def dot_tn(a, b):
    return lax.dot_general(a, b, (((0,), (0,)), ((), ())), preferred_element_type=F32)


def dot_nt(a, b):
    return lax.dot_general(a, b, (((1,), (1,)), ((), ())), preferred_element_type=F32)


def silu_and_slope(values):
    sigma = 0.5 * jnp.tanh(0.5 * values) + 0.5
    act = values * sigma
    return act, sigma + act * (1.0 - sigma)


def level_kernel(names, sizes, *refs):
    ref = dict(zip(names, refs))
    width, ch, c_in, c_coarse, rows_n, canvas_n, fused = sizes
    half = width // 2
    c = lax.axis_index("canvas")
    r = lax.axis_index("rows")
    z, k = r // 2, lax.rem(r, 2)
    up_id, down_id = (c, r - 1), (c, r + 1)
    has_up, has_down = r > 0, r < rows_n - 1
    z_n = rows_n // 2

    barrier = pltpu.get_barrier_semaphore()

    def greet(device):
        pl.semaphore_signal(barrier, inc=1, device_id=device, device_id_type=MESH)

    pl.when(has_up)(lambda: greet(up_id))
    pl.when(has_down)(lambda: greet(down_id))
    if fused:
        for step in range(1, z_n):
            greet((c, lax.rem(z + step, z_n) * 2 + k))
        for step in range(1, canvas_n):
            greet((lax.rem(c + step, canvas_n), r))

    local_sem = ref["local_sem"]
    used = [0]

    def fetch(src, dst):
        copy = pltpu.make_async_copy(src, dst, local_sem.at[used[0]])
        used[0] += 1
        copy.start()
        return copy

    X, CO = ref["X"], ref["CO"]
    in_x = fetch(ref["inputs"].at[0], X.at[pl.ds(4, 4)])
    in_w1 = fetch(ref["w_first"], ref["KB1"].at[pl.ds(1, 3)])
    in_co = fetch(ref["coarse"].at[0], CO.at[pl.ds(1, 2)])
    in_up = [
        fetch(ref["w_up"].at[a, b], ref["WU"].at[:, pl.ds((2 * a + b) * ch, ch)])
        for a in (0, 1)
        for b in (0, 1)
    ]
    in_w2 = fetch(ref["w_second"], ref["KB2"].at[pl.ds(1, 3)])
    in_w3 = fetch(ref["w_third"], ref["KB3"].at[pl.ds(1, 3)])
    in_w4 = fetch(ref["w_fourth"], ref["KB4"].at[pl.ds(1, 3)])
    in_cot = fetch(ref["cot_out"].at[0], ref["COT"])
    in_cp = fetch(ref["cot_pool"].at[0], ref["CP"])

    first, total_rows = r * 4, rows_n * 4

    def link(h):
        row = first + h
        inside = jnp.logical_and(row > 0, row < total_rows)
        cut = ref["row_cuts"][0, jnp.clip(row, 0, total_rows - 1)]
        return jnp.where(inside, 1 - cut, 0)

    open_row = 1.0 - ref["col_cuts"][...].astype(F32)
    open_row = jnp.where(lax.broadcasted_iota(jnp.int32, (1, width), 1) > 0, open_row, 0.0)
    left_gate = jnp.broadcast_to(open_row, (128, width))
    right_gate = pltpu.roll(left_gate, width - 1, 1)
    GL, GR = ref["GL"], ref["GR"]
    GL[...] = left_gate.T
    GR[...] = right_gate.T
    left_row, right_row = left_gate[:c_in], right_gate[:c_in]

    for name in ("KB1", "KB2", "KB3", "KB4"):
        ref[name][0] = jnp.zeros(ref[name].shape[1:], BF)
    for name in ("KT1", "KT2", "KT4", "VA", "VJ", "VC"):
        ref[name][0] = jnp.zeros(ref[name].shape[1:], BF)
    ref["KT3"][0] = jnp.zeros(ref["KT3"].shape[1:], BF)
    X[12] = jnp.zeros(X.shape[1:], BF)

    halo_send, halo_recv = ref["halo_send"], ref["halo_recv"]

    def remote(src, dst, send, recv, device):
        return pltpu.make_async_remote_copy(
            src_ref=src, dst_ref=dst, send_sem=send, recv_sem=recv, device_id=device, device_id_type=MESH
        )

    def pair_exchange(index, src_up, dst_up, src_down, dst_down):
        to_up = remote(src_up, dst_up, halo_send.at[index, 0], halo_recv.at[index, 0], up_id)
        to_down = remote(src_down, dst_down, halo_send.at[index, 1], halo_recv.at[index, 1], down_id)
        return to_up, to_down

    def start_exchange(pair):
        pl.when(has_up)(lambda: pair[0].start())
        pl.when(has_down)(lambda: pair[1].start())

    def receive(pair):
        pl.when(has_down)(lambda: pair[0].wait_recv())
        pl.when(has_up)(lambda: pair[1].wait_recv())

    def sent(pair):
        pl.when(has_up)(lambda: pair[0].wait_send())
        pl.when(has_down)(lambda: pair[1].wait_send())

    G4, G2 = ref["G4"], ref["G2"]
    x_halo = pair_exchange(0, ref["inputs"].at[0], X.at[pl.ds(8, 4)], ref["inputs"].at[0], X.at[pl.ds(0, 4)])
    co_halo = pair_exchange(1, ref["coarse"].at[0, 0], CO.at[3], ref["coarse"].at[0, 1], CO.at[0])
    g4_halo = pair_exchange(2, G4.at[pl.ds(2, 2)], G4.at[pl.ds(6, 2)], G4.at[pl.ds(4, 2)], G4.at[pl.ds(0, 2)])
    g2_halo = pair_exchange(3, G2.at[pl.ds(2, 2)], G2.at[pl.ds(6, 2)], G2.at[pl.ds(4, 2)], G2.at[pl.ds(0, 2)])

    @pl.when(jnp.logical_not(has_up))
    def _():
        X[0:4] = jnp.zeros((4,) + X.shape[1:], BF)
        CO[0] = jnp.zeros(CO.shape[1:], BF)
        G4[0:2] = jnp.zeros((2,) + G4.shape[1:], BF)
        G2[0:2] = jnp.zeros((2,) + G2.shape[1:], BF)

    @pl.when(jnp.logical_not(has_down))
    def _():
        X[8:12] = jnp.zeros((4,) + X.shape[1:], BF)
        CO[3] = jnp.zeros(CO.shape[1:], BF)
        G4[6:8] = jnp.zeros((2,) + G4.shape[1:], BF)
        G2[6:8] = jnp.zeros((2,) + G2.shape[1:], BF)

    peers = (z_n - 1 + canvas_n - 1) if fused else 0
    pl.semaphore_wait(barrier, peers + has_up.astype(jnp.int32) + has_down.astype(jnp.int32))
    start_exchange(x_halo)
    start_exchange(co_halo)

    def widen(value):
        left = (pltpu.roll(value, 1, 0) * GL[...]).astype(BF)
        right = (pltpu.roll(value, width - 1, 0) * GR[...]).astype(BF)
        return left, value.astype(BF), right

    def put_wide(dst, row, value, base=0, stride=ch):
        for place, piece in enumerate(widen(value)):
            lo = base + place * stride
            dst[row, :, lo : lo + ch] = piece

    def taps(bank, h):
        ga, gb, gc = link(h), link(h + 1), link(h + 2)
        return bank[0], bank[ga], bank[2], bank[gb * 3], bank[gb], bank[gc * 3]

    def conv_pair(src, at, bank, h):
        band = jnp.concatenate([src[at + d] for d in (-1, 0, 1, 2)], axis=1)
        zero, up0, mid, down0, up1, down1 = taps(bank, h)
        weights = jnp.concatenate(
            [
                jnp.concatenate([up0, mid, down0, zero], axis=0),
                jnp.concatenate([zero, up1, mid, down1], axis=0),
            ],
            axis=1,
        )
        return dot_nn(band, weights)

    def back_weights(bank, h):
        zero, up0, mid, down0, up1, down1 = taps(bank, h)
        return jnp.concatenate(
            [
                jnp.concatenate([up0, mid, down0, zero], axis=1),
                jnp.concatenate([zero, up1, mid, down1], axis=1),
            ],
            axis=0,
        )

    def back_pair(src, at, bank, h):
        band = jnp.concatenate([src[at + d] for d in (-1, 0, 1, 2)], axis=1)
        return dot_nt(band, back_weights(bank, h))

    def bias(name):
        return ref[name][...].astype(F32).reshape(1, ch)

    V3X, V3A, V3J, V3C = ref["V3X"], ref["V3A"], ref["V3J"], ref["V3C"]
    VA, VJ, VC = ref["VA"], ref["VJ"], ref["VC"]
    S1, S2, S3 = ref["S1"], ref["S2"], ref["S3"]
    KB1, KB2, KB3, KB4 = ref["KB1"], ref["KB2"], ref["KB3"], ref["KB4"]
    KT1, KT2, KT3, KT4 = ref["KT1"], ref["KT2"], ref["KT3"], ref["KT4"]

    def widen_input(row):
        value = X[row].astype(F32)
        V3X[row, 0:c_in] = (pltpu.roll(value, 1, 1) * left_row).astype(BF)
        V3X[row, c_in : 2 * c_in] = X[row]
        V3X[row, 2 * c_in : 3 * c_in] = (pltpu.roll(value, width - 1, 1) * right_row).astype(BF)

    b_first, b_second, b_up, b_third, b_fourth = (
        bias("b_" + name) for name in ("first", "second", "up", "third", "fourth")
    )

    def first_pair(h):
        at = h + 4
        band = V3X[pl.ds(at - 1, 4)].reshape(4 * 3 * c_in, width)
        zero, up0, mid, down0, up1, down1 = [t.reshape(3 * c_in, ch) for t in taps(KB1, h)]
        weights = jnp.concatenate(
            [
                jnp.concatenate([up0, mid, down0, zero], axis=0),
                jnp.concatenate([zero, up1, mid, down1], axis=0),
            ],
            axis=1,
        )
        both = dot_tn(band, weights)
        for j in (0, 1):
            act, slope = silu_and_slope(both[:, j * ch : (j + 1) * ch] + b_first)
            S1[h + j + 3] = slope
            put_wide(V3A, h + j + 3, act)
            VA[h + j + 4] = act.astype(BF)

    in_x.wait()
    in_w1.wait()
    for row in (4, 5, 6, 7):
        widen_input(row)
    first_pair(1)

    SA, SB = ref["SA"], ref["SB"]
    WU = ref["WU"]

    def up_rows(i):
        fine = dot_nn(CO[i], WU[...])
        for a in (0, 1):
            for b in (0, 1):
                lo = (2 * a + b) * ch
                piece = (fine[:, lo : lo + ch] + b_up).astype(BF).astype(F32)
                SA[a, pl.ds(b, half, stride=2), :] = piece
        for a in (0, 1):
            value = SA[a]
            put_wide(V3J, 2 * i + a, value, base=0, stride=2 * ch)
            VJ[2 * i + a + 1, :, :ch] = value.astype(BF)

    in_co.wait()
    for copy in in_up:
        copy.wait()
    up_rows(1)
    up_rows(2)

    in_w2.wait()
    in_w3.wait()
    in_w4.wait()
    for bank, back, part in ((KB1, KT1, c_in), (KB2, KT2, ch), (KB3, KT3, 2 * ch), (KB4, KT4, ch)):
        for row_tap in range(3):
            for col_tap in range(3):
                back[1 + (2 - row_tap), :, (2 - col_tap) * ch : (3 - col_tap) * ch] = bank[
                    1 + row_tap, col_tap * part : (col_tap + 1) * part
                ]

    receive(x_halo)
    for row in (0, 1, 2, 3, 8, 9, 10, 11):
        widen_input(row)
    for h in (-1, 3, -3, 5):
        first_pair(h)

    pooled_buf = ref["POOL"]

    def second_pair(h):
        both = conv_pair(V3A, h + 3, KB2, h)
        acts = []
        for j in (0, 1):
            act, slope = silu_and_slope(both[:, j * ch : (j + 1) * ch] + b_second)
            if 0 <= h + j < 4:
                S2[h + j] = slope
            put_wide(V3J, h + j + 2, act, base=ch, stride=2 * ch)
            rounded = act.astype(BF)
            VJ[h + j + 3, :, ch:] = rounded
            acts.append(rounded.astype(F32))
        if 0 <= h < 4:
            SB[...] = acts[0] + acts[1]
            pooled_buf[h // 2] = (
                (SB[pl.ds(0, half, stride=2), :] + SB[pl.ds(1, half, stride=2), :]) * 0.25
            ).astype(BF)

    for h in (0, 2, -2, 4):
        second_pair(h)
    out_pool = fetch(pooled_buf, ref["pooled"].at[0])

    receive(co_halo)
    up_rows(0)
    up_rows(3)

    def third_pair(h):
        both = conv_pair(V3J, h + 2, KB3, h)
        for j in (0, 1):
            act, slope = silu_and_slope(both[:, j * ch : (j + 1) * ch] + b_third)
            S3[h + j + 1] = slope
            put_wide(V3C, h + j + 1, act)
            VC[h + j + 2] = act.astype(BF)

    for h in (1, -1, 3):
        third_pair(h)

    G34, G33, G32, G31 = ref["G34"], ref["G33"], ref["G32"], ref["G31"]
    DB = ref["DB"]
    COT, ACT = ref["COT"], ref["ACT"]
    in_cot.wait()
    in_cp.wait()
    sums = {}

    def add_sum(name, value):
        part = jnp.sum(value.reshape(-1, 8, ch), axis=0)
        sums[name] = part if name not in sums else sums[name] + part

    def fourth_pair(h):
        both = conv_pair(V3C, h + 1, KB4, h)
        for j in (0, 1):
            act, slope = silu_and_slope(both[:, j * ch : (j + 1) * ch] + b_fourth)
            ACT[h + j] = act.astype(BF)
            g = (COT[h + j].astype(F32) * slope).astype(BF)
            G4[h + j + 2] = g
            g = g.astype(F32)
            add_sum("fourth", g)
            put_wide(G34, h + j + 2, g)

    fourth_pair(0)
    pl.when(has_up)(lambda: g4_halo[0].start())
    fourth_pair(2)
    pl.when(has_down)(lambda: g4_halo[1].start())
    out_act = fetch(ACT, ref["activations"].at[0])

    partner = (c, r + 1 - 2 * k)

    class Reduction:
        def __init__(self, index, name):
            self.index, self.name = index, name
            self.part, self.twin = ref["P_" + name], ref["RA_" + name]
            self.sums, self.along = ref["Q_" + name], ref["RB_" + name]
            self.slots = ref["RC_" + name]
            self.send, self.recv = ref["red_send"], ref["red_recv"]

        def copies_z(self):
            found = []
            for step in range(1, z_n):
                other = lax.rem(z + step, z_n)
                source = lax.rem(z + z_n - step, z_n)
                found.append(
                    remote(
                        self.sums.at[other], self.along.at[z], self.send.at[self.index, step],
                        self.recv.at[self.index, step], (c, other * 2 + k),
                    )
                )
            return found

        def copies_canvas(self):
            found = []
            for step in range(1, canvas_n):
                other = lax.rem(c + step, canvas_n)
                found.append(
                    remote(
                        self.along.at[z], self.slots.at[c], self.send.at[self.index, z_n + step],
                        self.recv.at[self.index, z_n + step], (other, r),
                    )
                )
            return found

        def start_core(self):
            if not fused:
                return
            self.core = remote(
                self.part.at[1 - k], self.twin, self.send.at[self.index, 0], self.recv.at[self.index, 0], partner
            )
            self.core.start()

        def start_z(self):
            if not fused:
                return
            self.core.wait_recv()
            self.sums[...] = (self.part[k].astype(F32) + self.twin[...].astype(F32)).astype(self.sums.dtype)
            self.along_copies = self.copies_z()
            for copy in self.along_copies:
                copy.start()

        def start_canvas(self):
            if not fused:
                return
            for copy in self.along_copies:
                copy.wait()
            self.along[z] = self.sums[z]
            total = self.along[0].astype(F32)
            for place in range(1, z_n):
                total = total + self.along[place].astype(F32)
            self.along[z] = total.astype(self.along.dtype)
            self.canvas = self.copies_canvas()
            for copy in self.canvas:
                copy.start()
            self.own = fetch(self.along.at[z], self.slots.at[c])

        def finish(self):
            if not fused:
                fetch(self.part, self.slots).wait()
                return
            self.core.wait_send()
            for copy in self.canvas:
                copy.wait()
            self.own.wait()

    red = {name: Reduction(index, name) for index, name in enumerate(LAYERS + ("bias",))}

    def put_parts(name, value):
        part = ref["P_" + name]
        blocks, share = part.shape[2], part.shape[3]
        for block in range(blocks):
            place = block if name == "up" else blocks - 1 - block
            for owner in range(8):
                lo = block * ch + owner * share
                part[owner % 2, owner // 2, place] = value[lo : lo + share].astype(BF)

    def row_stack(src, off, h):
        return jnp.concatenate(
            [src[link(h) * (h - 1 + off)], src[h + off], src[link(h + 1) * (h + 1 + off)]], axis=1
        )

    def weight_grad(grad3, at, src, off):
        band = grad3[pl.ds(at, 4)].reshape(4 * width, 3 * ch)
        stacked = jnp.concatenate([row_stack(src, off, h) for h in range(4)], axis=0)
        return dot_tn(band, stacked)

    def load_wide(dst, row, src):
        put_wide(dst, row, src.astype(F32))

    def third_back(h):
        both = back_pair(G34, h + 2, KT4, h)
        for j in (0, 1):
            g = (both[:, j * ch : (j + 1) * ch] * S3[h + j + 1]).astype(BF).astype(F32)
            if 0 <= h + j < 4:
                add_sum("third", g)
            put_wide(G33, h + j + 1, g)

    put_parts("fourth", weight_grad(G34, 2, VC, 2))
    red["fourth"].start_core()
    third_back(1)
    receive(g4_halo)
    for row in (0, 1, 6, 7):
        load_wide(G34, row, G4[row])
    third_back(-1)
    third_back(3)
    red["fourth"].start_z()

    GB, CP = ref["GB"], ref["CP"]

    def joined_back(h):
        band = jnp.concatenate([G33[h + 1 + d] for d in (-1, 0, 1)], axis=1)
        weights = jnp.concatenate([KT3[link(h)], KT3[2], KT3[link(h + 1) * 3]], axis=1)
        d_joined = dot_nt(band, weights)
        g_up = d_joined[:, :ch].astype(BF).astype(F32)
        add_sum("up", g_up)
        a = h % 2
        SA[a] = g_up
        for b in (0, 1):
            lo = (2 * a + b) * ch
            GB[h // 2, :, lo : lo + ch] = SA[a, pl.ds(b, half, stride=2), :].astype(BF)
        if a == 0:
            spread = CP[h // 2].astype(F32) * 0.25
            SB[pl.ds(0, half, stride=2), :] = spread
            SB[pl.ds(1, half, stride=2), :] = spread
        g = ((d_joined[:, ch:] + SB[...]) * S2[h]).astype(BF)
        G2[h + 2] = g
        g = g.astype(F32)
        add_sum("second", g)
        put_wide(G32, h + 2, g)

    joined_back(0)
    joined_back(1)
    pl.when(has_up)(lambda: g2_halo[0].start())
    joined_back(2)
    joined_back(3)
    pl.when(has_down)(lambda: g2_halo[1].start())

    put_parts("third", weight_grad(G33, 1, VJ, 3))
    red["third"].start_core()
    red["fourth"].start_canvas()
    bands = GB[...].reshape(2 * half, 4 * ch)
    put_parts("up", dot_tn(bands, CO[1:3].reshape(2 * half, c_coarse)))
    red["up"].start_core()
    red["third"].start_z()
    put_parts("second", weight_grad(G32, 2, VA, 4))
    red["second"].start_core()
    red["up"].start_z()

    def first_back(h):
        both = back_pair(G32, h + 2, KT2, h)
        for j in (0, 1):
            g = (both[:, j * ch : (j + 1) * ch] * S1[h + j + 3]).astype(BF).astype(F32)
            if 0 <= h + j < 4:
                add_sum("first", g)
            put_wide(G31, h + j + 1, g)

    first_back(1)
    receive(g2_halo)
    for row in (0, 1, 6, 7):
        load_wide(G32, row, G2[row])
    first_back(-1)
    first_back(3)

    def pick(h, joined):
        return X[12 + joined * (h - 8)]

    stacked = jnp.concatenate(
        [
            jnp.concatenate([pick(h - 1, link(h)), X[h + 4], pick(h + 1, link(h + 1))], axis=0)
            for h in range(4)
        ],
        axis=1,
    )
    put_parts("first", dot_nn(stacked, G31[1:5].reshape(4 * width, 3 * ch)).T)
    red["first"].start_core()
    for place, name in enumerate(("first", "second", "up", "third", "fourth")):
        DB[place : place + 1] = jnp.sum(sums[name], axis=0, keepdims=True)
    if fused:
        ref["P_bias"][0] = DB[...]
        ref["P_bias"][1] = DB[...]
    else:
        ref["P_bias"][0] = DB[...]
    red["bias"].start_core()
    red["second"].start_z()

    GI = ref["GI"]

    def input_back(h):
        weights = back_weights(KT1, h)
        band = jnp.concatenate([G31[h + 1 + d] for d in (-1, 0, 1, 2)], axis=1)
        both = dot_nt(weights, band).astype(BF)
        GI[h] = both[:c_in]
        GI[h + 1] = both[c_in:]

    red["first"].start_z()
    input_back(0)
    input_back(2)
    out_gi = fetch(GI, ref["grad_inputs"].at[0])
    GC = ref["GC"]
    for i in (0, 1):
        GC[i] = dot_nt(GB[i], WU[...]).astype(BF)
    out_gc = fetch(GC, ref["grad_coarse"].at[0])
    red["third"].start_canvas()
    red["up"].start_canvas()
    red["second"].start_canvas()

    if fused:
        bias_red = red["bias"]
        bias_red.core.wait_recv()
        bias_red.sums[z] = bias_red.part[k] + bias_red.twin[...]
        bias_red.along_copies = []
        for step in range(1, z_n):
            other = lax.rem(z + step, z_n)
            bias_red.along_copies.append(
                remote(
                    bias_red.sums.at[z], bias_red.along.at[z], bias_red.send.at[bias_red.index, step],
                    bias_red.recv.at[bias_red.index, step], (c, other * 2 + k),
                )
            )
        for copy in bias_red.along_copies:
            copy.start()
    red["first"].start_canvas()
    red["bias"].start_canvas()

    for name in LAYERS + ("bias",):
        red[name].finish()
    for pair in (x_halo, co_halo, g4_halo, g2_halo):
        sent(pair)
    for copy in (out_pool, out_act, out_gi, out_gc):
        copy.wait()


def finish_kernel(names, sizes, *refs):
    ref = dict(zip(names, refs))
    ch, share = sizes
    r = lax.axis_index("rows")
    copies = []
    for place, name in enumerate(("activations", "pooled", "grad_inputs", "grad_coarse")):
        copy = pltpu.make_async_copy(ref[name], ref["out_" + name], ref["sem"].at[place])
        copy.start()
        copies.append(copy)

    def total(slots):
        value = slots[0].astype(F32)
        for place in range(1, slots.shape[0]):
            value = value + slots[place].astype(F32)
        return value

    for name in ("first", "second", "third", "fourth"):
        value = total(ref["RC_" + name])
        out = ref["out_w_" + name]
        part = out.shape[3]
        for row_tap in range(3):
            out[row_tap] = value[:, :, row_tap * part : (row_tap + 1) * part]
    value = total(ref["RC_up"])
    for a in (0, 1):
        for b in (0, 1):
            ref["out_w_up"][a, b] = value[2 * a + b]
    sums = pltpu.roll(total(ref["RC_bias"]), lax.rem(ch - r * share, ch), 1)
    for place, name in enumerate(("first", "second", "up", "third", "fourth")):
        ref["out_b_" + name][...] = sums[place : place + 1, :share]
    for copy in copies:
        copy.wait()


def on_device(fused, rows_n, canvas_n, *args):
    arg = dict(zip(OPERANDS, args))
    _, length, width, c_in = arg["inputs"].shape
    ch = arg["w_first"].shape[3]
    c_coarse = arg["coarse"].shape[3]
    half = width // 2
    assert length == 4
    arg["inputs"] = jnp.swapaxes(arg["inputs"], 2, 3)
    arg["w_first"] = arg["w_first"].reshape(3, 3 * c_in, ch)
    arg["w_second"] = arg["w_second"].reshape(3, 3 * ch, ch)
    arg["w_third"] = arg["w_third"].reshape(3, 6 * ch, ch)
    arg["w_fourth"] = arg["w_fourth"].reshape(3, 3 * ch, ch)
    for name in ("b_first", "b_second", "b_up", "b_third", "b_fourth"):
        arg[name] = arg[name].reshape(1, ch)

    any_spec = pl.BlockSpec(memory_space=pl.ANY)
    vmem_spec = pl.BlockSpec(memory_space=pltpu.VMEM)
    in_specs = []
    for name in OPERANDS:
        if name == "row_cuts":
            in_specs.append(pl.BlockSpec(memory_space=pltpu.SMEM))
        elif name == "col_cuts" or name.startswith("b_"):
            in_specs.append(vmem_spec)
        else:
            in_specs.append(any_spec)

    owners, z_n = 8, 4
    share = ch // owners
    pieces = {
        "fourth": ((3, share, 3 * ch), BF),
        "third": ((3, share, 6 * ch), BF),
        "up": ((4, share, c_coarse), BF),
        "second": ((3, share, 3 * ch), BF),
        "first": ((3, share, 3 * c_in), BF),
        "bias": ((8, ch), F32),
    }
    outs = {
        "activations": jax.ShapeDtypeStruct((1, 4, width, ch), BF),
        "pooled": jax.ShapeDtypeStruct((1, 2, half, ch), BF),
        "grad_inputs": jax.ShapeDtypeStruct((1, 4, c_in, width), BF),
        "grad_coarse": jax.ShapeDtypeStruct((1, 2, half, c_coarse), BF),
    }
    scratch = {
        "X": pltpu.VMEM((13, c_in, width), BF),
        "CO": pltpu.VMEM((4, half, c_coarse), BF),
        "COT": pltpu.VMEM((4, width, ch), BF),
        "CP": pltpu.VMEM((2, half, ch), BF),
        "WU": pltpu.VMEM((c_coarse, 4 * ch), BF),
        "GL": pltpu.VMEM((width, ch), F32),
        "GR": pltpu.VMEM((width, ch), F32),
        "KB1": pltpu.VMEM((4, 3 * c_in, ch), BF),
        "KB2": pltpu.VMEM((4, 3 * ch, ch), BF),
        "KB3": pltpu.VMEM((4, 6 * ch, ch), BF),
        "KB4": pltpu.VMEM((4, 3 * ch, ch), BF),
        "KT1": pltpu.VMEM((4, c_in, 3 * ch), BF),
        "KT2": pltpu.VMEM((4, ch, 3 * ch), BF),
        "KT3": pltpu.VMEM((4, 2 * ch, 3 * ch), BF),
        "KT4": pltpu.VMEM((4, ch, 3 * ch), BF),
        "V3X": pltpu.VMEM((12, 3 * c_in, width), BF),
        "V3A": pltpu.VMEM((10, width, 3 * ch), BF),
        "V3J": pltpu.VMEM((8, width, 6 * ch), BF),
        "V3C": pltpu.VMEM((6, width, 3 * ch), BF),
        "VA": pltpu.VMEM((11, width, ch), BF),
        "VJ": pltpu.VMEM((9, width, 2 * ch), BF),
        "VC": pltpu.VMEM((7, width, ch), BF),
        "S1": pltpu.VMEM((10, width, ch), F32),
        "S2": pltpu.VMEM((4, width, ch), F32),
        "S3": pltpu.VMEM((6, width, ch), F32),
        "G4": pltpu.VMEM((8, width, ch), BF),
        "G2": pltpu.VMEM((8, width, ch), BF),
        "G34": pltpu.VMEM((8, width, 3 * ch), BF),
        "G33": pltpu.VMEM((6, width, 3 * ch), BF),
        "G32": pltpu.VMEM((8, width, 3 * ch), BF),
        "G31": pltpu.VMEM((6, width, 3 * ch), BF),
        "GB": pltpu.VMEM((2, half, 4 * ch), BF),
        "SA": pltpu.VMEM((2, width, ch), F32),
        "SB": pltpu.VMEM((width, ch), F32),
        "DB": pltpu.VMEM((8, ch), F32),
        "ACT": pltpu.VMEM((4, width, ch), BF),
        "POOL": pltpu.VMEM((2, half, ch), BF),
        "GI": pltpu.VMEM((4, c_in, width), BF),
        "GC": pltpu.VMEM((2, half, c_coarse), BF),
        "local_sem": pltpu.SemaphoreType.DMA((24,)),
        "halo_send": pltpu.SemaphoreType.DMA((4, 2)),
        "halo_recv": pltpu.SemaphoreType.DMA((4, 2)),
        "red_send": pltpu.SemaphoreType.DMA((6, z_n + canvas_n)),
        "red_recv": pltpu.SemaphoreType.DMA((6, z_n + canvas_n)),
    }
    for name, (shape, kind) in pieces.items():
        if name == "bias":
            scratch["P_bias"] = pltpu.VMEM((2,) + shape, kind)
            scratch["RA_bias"] = pltpu.VMEM(shape, kind)
        else:
            scratch["P_" + name] = pltpu.VMEM((2, z_n) + shape, kind)
            scratch["RA_" + name] = pltpu.VMEM((z_n,) + shape, kind)
        scratch["Q_" + name] = pltpu.VMEM((z_n,) + shape, kind)
        scratch["RB_" + name] = pltpu.VMEM((z_n,) + shape, kind)
        if fused:
            landing = (canvas_n,) + shape
        else:
            landing = scratch["P_" + name].shape
        outs["RC_" + name] = jax.ShapeDtypeStruct(landing, kind)

    names = list(OPERANDS) + list(outs) + list(scratch)
    sizes = (width, ch, c_in, c_coarse, rows_n, canvas_n, fused)
    results = pl.pallas_call(
        functools.partial(level_kernel, names, sizes),
        out_shape=tuple(outs.values()),
        in_specs=in_specs,
        out_specs=tuple(any_spec for _ in outs),
        scratch_shapes=list(scratch.values()),
        compiler_params=pltpu.CompilerParams(
            collective_id=0, has_side_effects=True, vmem_limit_bytes=VMEM_BYTES
        ),
        name="level",
    )(*(arg[name] for name in OPERANDS))
    held = dict(zip(outs, results))

    if not fused:
        return unfused_tail(held, rows_n, ch, c_in, c_coarse)

    done = {"out_" + name: outs[name] for name in ("activations", "pooled", "grad_inputs", "grad_coarse")}
    for name in ("first", "second", "third", "fourth"):
        shape = pieces[name][0]
        done["out_w_" + name] = jax.ShapeDtypeStruct((3, 3, share, shape[2] // 3), F32)
    done["out_w_up"] = jax.ShapeDtypeStruct((2, 2, share, c_coarse), F32)
    for name in ("first", "second", "up", "third", "fourth"):
        done["out_b_" + name] = jax.ShapeDtypeStruct((1, share), F32)
    big = ("activations", "pooled", "grad_inputs", "grad_coarse")
    finals = pl.pallas_call(
        functools.partial(finish_kernel, list(outs) + list(done) + ["sem"], (ch, share)),
        out_shape=tuple(done.values()),
        in_specs=[any_spec if name in big else vmem_spec for name in outs],
        out_specs=tuple(any_spec if name[4:] in big else vmem_spec for name in done),
        scratch_shapes=[pltpu.SemaphoreType.DMA((4,))],
        name="finish",
    )(*results)
    final = dict(zip(done, finals))
    return ordered(
        {name: final["out_" + name] for name in big},
        {name: final["out_w_" + name] for name in LAYERS},
        {name: final["out_b_" + name].reshape(share) for name in LAYERS},
    )


def ordered(big, weights, biases):
    turned = {name: jnp.swapaxes(value, 2, 3) for name, value in weights.items()}
    pairs = []
    for name in ("first", "second", "up", "third", "fourth"):
        pairs += [turned[name], biases[name]]
    return (
        big["activations"],
        big["pooled"],
        jnp.swapaxes(big["grad_inputs"], 2, 3),
        big["grad_coarse"],
        *pairs,
    )


def unfused_tail(held, rows_n, ch, c_in, c_coarse):
    share = ch // rows_n
    offset = lax.axis_index("rows") * share

    def whole(name):
        parts = held["RC_" + name].astype(F32)
        blocks, piece, lanes = parts.shape[2:]
        parts = jnp.transpose(parts, (2, 1, 0, 3, 4)).reshape(blocks, ch, lanes)
        if name == "up":
            return parts.reshape(2, 2, ch, lanes)
        return jnp.transpose(parts.reshape(3, ch, 3, lanes // 3), (2, 0, 1, 3))

    weights = {name: whole(name) for name in LAYERS}
    weights, biases = lax.psum((weights, held["RC_bias"][0]), ("canvas", "rows"))
    weights = {name: lax.dynamic_slice_in_dim(value, offset, share, 2) for name, value in weights.items()}
    biases = lax.dynamic_slice_in_dim(biases, offset, share, 1)
    places = {"first": 0, "second": 1, "up": 2, "third": 3, "fourth": 4}
    return ordered(held, weights, {name: biases[place] for name, place in places.items()})


def solution(mesh):
    rows_n, canvas_n = mesh.shape["rows"], mesh.shape["canvas"]
    fused = rows_n == 8 and canvas_n == 4
    split = P("canvas", "rows", None, None)
    pairs = (P(None, None, None, "rows"), P("rows"))
    return jax.shard_map(
        functools.partial(on_device, fused, rows_n, canvas_n),
        mesh=mesh,
        in_specs=(split, split, P("canvas", None), P("canvas", None)) + (P(),) * 10 + (split, split),
        out_specs=(split,) * 4 + pairs * 5,
        check_vma=False,
    )
```

```python
import functools
import types

import jax
import jax.numpy as jnp
from jax import lax
from jax.experimental import pallas as pl
from jax.experimental.pallas import tpu as pltpu
from jax.sharding import PartitionSpec as P

MESH = pl.DeviceIdType.MESH
BF = jnp.bfloat16
F32 = jnp.float32
VMEM_BYTES = 58 * 2**20

FIRST, SECOND, UP, THIRD, FOURTH, BIAS = "first", "second", "up", "third", "fourth", "bias"
LAYERS = (FOURTH, THIRD, UP, SECOND, FIRST)
ORDER = (FIRST, SECOND, UP, THIRD, FOURTH)
BIG = ("activations", "pooled", "grad_inputs", "grad_coarse")


def dot_nn(a, b):
    return lax.dot_general(a, b, (((1,), (0,)), ((), ())), preferred_element_type=F32)


def dot_tn(a, b):
    return lax.dot_general(a, b, (((0,), (0,)), ((), ())), preferred_element_type=F32)


def dot_nt(a, b):
    return lax.dot_general(a, b, (((1,), (1,)), ((), ())), preferred_element_type=F32)


def silu_and_slope(values):
    sigma = 0.5 * jnp.tanh(0.5 * values) + 0.5
    act = values * sigma
    return act, sigma + act * (1.0 - sigma)


def level_kernel(names, sizes, *refs):
    ref = types.SimpleNamespace(**dict(zip(names, refs)))
    width, ch, c_in, c_coarse, rows_n, canvas_n, fused = sizes
    half = width // 2
    c = lax.axis_index("canvas")
    r = lax.axis_index("rows")
    z, k = r // 2, lax.rem(r, 2)
    up_id, down_id = (c, r - 1), (c, r + 1)
    has_up, has_down = r > 0, r < rows_n - 1
    z_n = rows_n // 2

    barrier = pltpu.get_barrier_semaphore()

    def greet(device):
        pl.semaphore_signal(barrier, inc=1, device_id=device, device_id_type=MESH)

    pl.when(has_up)(lambda: greet(up_id))
    pl.when(has_down)(lambda: greet(down_id))
    if fused:
        for step in range(1, z_n):
            greet((c, lax.rem(z + step, z_n) * 2 + k))
        for step in range(1, canvas_n):
            greet((lax.rem(c + step, canvas_n), r))

    local_sem = ref.local_sem
    used = [0]

    def fetch(src, dst):
        copy = pltpu.make_async_copy(src, dst, local_sem.at[used[0]])
        used[0] += 1
        copy.start()
        return copy

    X, CO = ref.X, ref.CO
    in_x = fetch(ref.inputs.at[0], X.at[pl.ds(4, 4)])
    in_w1 = fetch(ref.w_first, ref.KB1.at[pl.ds(1, 3)])
    in_co = fetch(ref.coarse.at[0], CO.at[pl.ds(1, 2)])
    in_up = [
        fetch(ref.w_up.at[a, b], ref.WU.at[:, pl.ds((2 * a + b) * ch, ch)])
        for a in (0, 1)
        for b in (0, 1)
    ]
    in_w2 = fetch(ref.w_second, ref.KB2.at[pl.ds(1, 3)])
    in_w3 = fetch(ref.w_third, ref.KB3.at[pl.ds(1, 3)])
    in_w4 = fetch(ref.w_fourth, ref.KB4.at[pl.ds(1, 3)])
    in_cot = fetch(ref.cot_out.at[0], ref.COT)
    in_cp = fetch(ref.cot_pool.at[0], ref.CP)

    first, total_rows = r * 4, rows_n * 4

    def link(h):
        row = first + h
        inside = jnp.logical_and(row > 0, row < total_rows)
        cut = ref.row_cuts[0, jnp.clip(row, 0, total_rows - 1)]
        return jnp.where(inside, 1 - cut, 0)

    open_row = 1.0 - ref.col_cuts[...].astype(F32)
    open_row = jnp.where(lax.broadcasted_iota(jnp.int32, (1, width), 1) > 0, open_row, 0.0)
    left_gate = jnp.broadcast_to(open_row, (128, width))
    right_gate = pltpu.roll(left_gate, width - 1, 1)
    GL, GR = ref.GL, ref.GR
    GL[...] = left_gate.T
    GR[...] = right_gate.T
    left_row, right_row = left_gate[:c_in], right_gate[:c_in]

    for bank in (ref.KB1, ref.KB2, ref.KB3, ref.KB4, ref.KT1, ref.KT2, ref.KT3, ref.KT4, ref.VA, ref.VJ, ref.VC):
        bank[0] = jnp.zeros(bank.shape[1:], BF)
    X[12] = jnp.zeros(X.shape[1:], BF)

    halo_send, halo_recv = ref.halo_send, ref.halo_recv

    def remote(src, dst, send, recv, device):
        return pltpu.make_async_remote_copy(
            src_ref=src, dst_ref=dst, send_sem=send, recv_sem=recv, device_id=device, device_id_type=MESH
        )

    def pair_exchange(index, src_up, dst_up, src_down, dst_down):
        to_up = remote(src_up, dst_up, halo_send.at[index, 0], halo_recv.at[index, 0], up_id)
        to_down = remote(src_down, dst_down, halo_send.at[index, 1], halo_recv.at[index, 1], down_id)
        return to_up, to_down

    def start_exchange(pair):
        pl.when(has_up)(lambda: pair[0].start())
        pl.when(has_down)(lambda: pair[1].start())

    def receive(pair):
        pl.when(has_down)(lambda: pair[0].wait_recv())
        pl.when(has_up)(lambda: pair[1].wait_recv())

    def sent(pair):
        pl.when(has_up)(lambda: pair[0].wait_send())
        pl.when(has_down)(lambda: pair[1].wait_send())

    G4, G2 = ref.G4, ref.G2
    x_halo = pair_exchange(0, ref.inputs.at[0], X.at[pl.ds(8, 4)], ref.inputs.at[0], X.at[pl.ds(0, 4)])
    co_halo = pair_exchange(1, ref.coarse.at[0, 0], CO.at[3], ref.coarse.at[0, 1], CO.at[0])
    g4_halo = pair_exchange(2, G4.at[pl.ds(2, 2)], G4.at[pl.ds(6, 2)], G4.at[pl.ds(4, 2)], G4.at[pl.ds(0, 2)])
    g2_halo = pair_exchange(3, G2.at[pl.ds(2, 2)], G2.at[pl.ds(6, 2)], G2.at[pl.ds(4, 2)], G2.at[pl.ds(0, 2)])

    @pl.when(jnp.logical_not(has_up))
    def _():
        X[0:4] = jnp.zeros((4,) + X.shape[1:], BF)
        CO[0] = jnp.zeros(CO.shape[1:], BF)
        G4[0:2] = jnp.zeros((2,) + G4.shape[1:], BF)
        G2[0:2] = jnp.zeros((2,) + G2.shape[1:], BF)

    @pl.when(jnp.logical_not(has_down))
    def _():
        X[8:12] = jnp.zeros((4,) + X.shape[1:], BF)
        CO[3] = jnp.zeros(CO.shape[1:], BF)
        G4[6:8] = jnp.zeros((2,) + G4.shape[1:], BF)
        G2[6:8] = jnp.zeros((2,) + G2.shape[1:], BF)

    peers = (z_n - 1 + canvas_n - 1) if fused else 0
    pl.semaphore_wait(barrier, peers + has_up.astype(jnp.int32) + has_down.astype(jnp.int32))
    start_exchange(x_halo)
    start_exchange(co_halo)

    def widen(value):
        left = (pltpu.roll(value, 1, 0) * GL[...]).astype(BF)
        right = (pltpu.roll(value, width - 1, 0) * GR[...]).astype(BF)
        return left, value.astype(BF), right

    def put_wide(dst, row, value, base=0, stride=ch):
        for place, piece in enumerate(widen(value)):
            lo = base + place * stride
            dst[row, :, lo : lo + ch] = piece

    def taps(bank, h):
        ga, gb, gc = link(h), link(h + 1), link(h + 2)
        return bank[0], bank[ga], bank[2], bank[gb * 3], bank[gb], bank[gc * 3]

    def conv_pair(src, at, bank, h):
        band = jnp.concatenate([src[at + d] for d in (-1, 0, 1, 2)], axis=1)
        zero, up0, mid, down0, up1, down1 = taps(bank, h)
        weights = jnp.concatenate(
            [
                jnp.concatenate([up0, mid, down0, zero], axis=0),
                jnp.concatenate([zero, up1, mid, down1], axis=0),
            ],
            axis=1,
        )
        return dot_nn(band, weights)

    def back_weights(bank, h):
        zero, up0, mid, down0, up1, down1 = taps(bank, h)
        return jnp.concatenate(
            [
                jnp.concatenate([up0, mid, down0, zero], axis=1),
                jnp.concatenate([zero, up1, mid, down1], axis=1),
            ],
            axis=0,
        )

    def back_pair(src, at, bank, h):
        band = jnp.concatenate([src[at + d] for d in (-1, 0, 1, 2)], axis=1)
        return dot_nt(band, back_weights(bank, h))

    def bias(name):
        return getattr(ref, name)[...].astype(F32).reshape(1, ch)

    V3X, V3A, V3J, V3C = ref.V3X, ref.V3A, ref.V3J, ref.V3C
    VA, VJ, VC = ref.VA, ref.VJ, ref.VC
    S1, S2, S3 = ref.S1, ref.S2, ref.S3
    KB1, KB2, KB3, KB4 = ref.KB1, ref.KB2, ref.KB3, ref.KB4
    KT1, KT2, KT3, KT4 = ref.KT1, ref.KT2, ref.KT3, ref.KT4

    def widen_input(row):
        value = X[row].astype(F32)
        V3X[row, 0:c_in] = (pltpu.roll(value, 1, 1) * left_row).astype(BF)
        V3X[row, c_in : 2 * c_in] = X[row]
        V3X[row, 2 * c_in : 3 * c_in] = (pltpu.roll(value, width - 1, 1) * right_row).astype(BF)

    b_first, b_second, b_up, b_third, b_fourth = (
        bias("b_" + name) for name in ORDER
    )

    def first_pair(h):
        at = h + 4
        band = V3X[pl.ds(at - 1, 4)].reshape(4 * 3 * c_in, width)
        zero, up0, mid, down0, up1, down1 = [t.reshape(3 * c_in, ch) for t in taps(KB1, h)]
        weights = jnp.concatenate(
            [
                jnp.concatenate([up0, mid, down0, zero], axis=0),
                jnp.concatenate([zero, up1, mid, down1], axis=0),
            ],
            axis=1,
        )
        both = dot_tn(band, weights)
        for j in (0, 1):
            act, slope = silu_and_slope(both[:, j * ch : (j + 1) * ch] + b_first)
            S1[h + j + 3] = slope
            put_wide(V3A, h + j + 3, act)
            VA[h + j + 4] = act.astype(BF)

    in_x.wait()
    in_w1.wait()
    for row in (4, 5, 6, 7):
        widen_input(row)
    first_pair(1)

    SA, SB = ref.SA, ref.SB
    WU = ref.WU

    def up_rows(i):
        fine = dot_nn(CO[i], WU[...])
        for a in (0, 1):
            for b in (0, 1):
                lo = (2 * a + b) * ch
                piece = (fine[:, lo : lo + ch] + b_up).astype(BF).astype(F32)
                SA[a, pl.ds(b, half, stride=2), :] = piece
        for a in (0, 1):
            value = SA[a]
            put_wide(V3J, 2 * i + a, value, base=0, stride=2 * ch)
            VJ[2 * i + a + 1, :, :ch] = value.astype(BF)

    in_co.wait()
    for copy in in_up:
        copy.wait()
    up_rows(1)
    up_rows(2)

    in_w2.wait()
    in_w3.wait()
    in_w4.wait()
    for bank, back, part in ((KB1, KT1, c_in), (KB2, KT2, ch), (KB3, KT3, 2 * ch), (KB4, KT4, ch)):
        for row_tap in range(3):
            for col_tap in range(3):
                back[1 + (2 - row_tap), :, (2 - col_tap) * ch : (3 - col_tap) * ch] = bank[
                    1 + row_tap, col_tap * part : (col_tap + 1) * part
                ]

    receive(x_halo)
    for row in (0, 1, 2, 3, 8, 9, 10, 11):
        widen_input(row)
    for h in (-1, 3, -3, 5):
        first_pair(h)

    pooled_buf = ref.POOL

    def second_pair(h):
        both = conv_pair(V3A, h + 3, KB2, h)
        acts = []
        for j in (0, 1):
            act, slope = silu_and_slope(both[:, j * ch : (j + 1) * ch] + b_second)
            if 0 <= h + j < 4:
                S2[h + j] = slope
            put_wide(V3J, h + j + 2, act, base=ch, stride=2 * ch)
            rounded = act.astype(BF)
            VJ[h + j + 3, :, ch:] = rounded
            acts.append(rounded.astype(F32))
        if 0 <= h < 4:
            SB[...] = acts[0] + acts[1]
            pooled_buf[h // 2] = (
                (SB[pl.ds(0, half, stride=2), :] + SB[pl.ds(1, half, stride=2), :]) * 0.25
            ).astype(BF)

    for h in (0, 2, -2, 4):
        second_pair(h)
    out_pool = fetch(pooled_buf, ref.pooled.at[0])

    receive(co_halo)
    up_rows(0)
    up_rows(3)

    def third_pair(h):
        both = conv_pair(V3J, h + 2, KB3, h)
        for j in (0, 1):
            act, slope = silu_and_slope(both[:, j * ch : (j + 1) * ch] + b_third)
            S3[h + j + 1] = slope
            put_wide(V3C, h + j + 1, act)
            VC[h + j + 2] = act.astype(BF)

    for h in (1, -1, 3):
        third_pair(h)

    G34, G33, G32, G31 = ref.G34, ref.G33, ref.G32, ref.G31
    DB = ref.DB
    COT, ACT = ref.COT, ref.ACT
    in_cot.wait()
    in_cp.wait()
    sums = {}

    def add_sum(name, value):
        part = jnp.sum(value.reshape(-1, 8, ch), axis=0)
        sums[name] = part if name not in sums else sums[name] + part

    def fourth_pair(h):
        both = conv_pair(V3C, h + 1, KB4, h)
        for j in (0, 1):
            act, slope = silu_and_slope(both[:, j * ch : (j + 1) * ch] + b_fourth)
            ACT[h + j] = act.astype(BF)
            g = (COT[h + j].astype(F32) * slope).astype(BF)
            G4[h + j + 2] = g
            g = g.astype(F32)
            add_sum(FOURTH, g)
            put_wide(G34, h + j + 2, g)

    fourth_pair(0)
    pl.when(has_up)(lambda: g4_halo[0].start())
    fourth_pair(2)
    pl.when(has_down)(lambda: g4_halo[1].start())
    out_act = fetch(ACT, ref.activations.at[0])

    partner = (c, r + 1 - 2 * k)

    class Reduction:
        def __init__(self, index, name):
            self.index, self.name = index, name
            self.part, self.twin = getattr(ref, "P_" + name), getattr(ref, "RA_" + name)
            self.sums, self.along = getattr(ref, "Q_" + name), getattr(ref, "RB_" + name)
            self.slots = getattr(ref, "RC_" + name)
            self.send, self.recv = ref.red_send, ref.red_recv

        def copies_z(self):
            found = []
            for step in range(1, z_n):
                other = lax.rem(z + step, z_n)
                source = lax.rem(z + z_n - step, z_n)
                found.append(
                    remote(
                        self.sums.at[other], self.along.at[z], self.send.at[self.index, step],
                        self.recv.at[self.index, step], (c, other * 2 + k),
                    )
                )
            return found

        def copies_canvas(self):
            found = []
            for step in range(1, canvas_n):
                other = lax.rem(c + step, canvas_n)
                found.append(
                    remote(
                        self.along.at[z], self.slots.at[c], self.send.at[self.index, z_n + step],
                        self.recv.at[self.index, z_n + step], (other, r),
                    )
                )
            return found

        def start_core(self):
            if not fused:
                return
            self.core = remote(
                self.part.at[1 - k], self.twin, self.send.at[self.index, 0], self.recv.at[self.index, 0], partner
            )
            self.core.start()

        def start_z(self):
            if not fused:
                return
            self.core.wait_recv()
            self.sums[...] = (self.part[k].astype(F32) + self.twin[...].astype(F32)).astype(self.sums.dtype)
            self.along_copies = self.copies_z()
            for copy in self.along_copies:
                copy.start()

        def start_canvas(self):
            if not fused:
                return
            for copy in self.along_copies:
                copy.wait()
            self.along[z] = self.sums[z]
            total = self.along[0].astype(F32)
            for place in range(1, z_n):
                total = total + self.along[place].astype(F32)
            self.along[z] = total.astype(self.along.dtype)
            self.canvas = self.copies_canvas()
            for copy in self.canvas:
                copy.start()
            self.own = fetch(self.along.at[z], self.slots.at[c])

        def finish(self):
            if not fused:
                fetch(self.part, self.slots).wait()
                return
            self.core.wait_send()
            for copy in self.canvas:
                copy.wait()
            self.own.wait()

    red = {name: Reduction(index, name) for index, name in enumerate(LAYERS + (BIAS,))}

    def put_parts(name, value):
        part = getattr(ref, "P_" + name)
        blocks, share = part.shape[2], part.shape[3]
        for block in range(blocks):
            place = block if name == UP else blocks - 1 - block
            for owner in range(8):
                lo = block * ch + owner * share
                part[owner % 2, owner // 2, place] = value[lo : lo + share].astype(BF)

    def row_stack(src, off, h):
        return jnp.concatenate(
            [src[link(h) * (h - 1 + off)], src[h + off], src[link(h + 1) * (h + 1 + off)]], axis=1
        )

    def weight_grad(grad3, at, src, off):
        band = grad3[pl.ds(at, 4)].reshape(4 * width, 3 * ch)
        stacked = jnp.concatenate([row_stack(src, off, h) for h in range(4)], axis=0)
        return dot_tn(band, stacked)

    def load_wide(dst, row, src):
        put_wide(dst, row, src.astype(F32))

    def third_back(h):
        both = back_pair(G34, h + 2, KT4, h)
        for j in (0, 1):
            g = (both[:, j * ch : (j + 1) * ch] * S3[h + j + 1]).astype(BF).astype(F32)
            if 0 <= h + j < 4:
                add_sum(THIRD, g)
            put_wide(G33, h + j + 1, g)

    put_parts(FOURTH, weight_grad(G34, 2, VC, 2))
    red[FOURTH].start_core()
    third_back(1)
    receive(g4_halo)
    for row in (0, 1, 6, 7):
        load_wide(G34, row, G4[row])
    third_back(-1)
    third_back(3)
    red[FOURTH].start_z()

    GB, CP = ref.GB, ref.CP

    def joined_back(h):
        band = jnp.concatenate([G33[h + 1 + d] for d in (-1, 0, 1)], axis=1)
        weights = jnp.concatenate([KT3[link(h)], KT3[2], KT3[link(h + 1) * 3]], axis=1)
        d_joined = dot_nt(band, weights)
        g_up = d_joined[:, :ch].astype(BF).astype(F32)
        add_sum(UP, g_up)
        a = h % 2
        SA[a] = g_up
        for b in (0, 1):
            lo = (2 * a + b) * ch
            GB[h // 2, :, lo : lo + ch] = SA[a, pl.ds(b, half, stride=2), :].astype(BF)
        if a == 0:
            spread = CP[h // 2].astype(F32) * 0.25
            SB[pl.ds(0, half, stride=2), :] = spread
            SB[pl.ds(1, half, stride=2), :] = spread
        g = ((d_joined[:, ch:] + SB[...]) * S2[h]).astype(BF)
        G2[h + 2] = g
        g = g.astype(F32)
        add_sum(SECOND, g)
        put_wide(G32, h + 2, g)

    joined_back(0)
    joined_back(1)
    pl.when(has_up)(lambda: g2_halo[0].start())
    joined_back(2)
    joined_back(3)
    pl.when(has_down)(lambda: g2_halo[1].start())

    put_parts(THIRD, weight_grad(G33, 1, VJ, 3))
    red[THIRD].start_core()
    red[FOURTH].start_canvas()
    bands = GB[...].reshape(2 * half, 4 * ch)
    put_parts(UP, dot_tn(bands, CO[1:3].reshape(2 * half, c_coarse)))
    red[UP].start_core()
    red[THIRD].start_z()
    put_parts(SECOND, weight_grad(G32, 2, VA, 4))
    red[SECOND].start_core()
    red[UP].start_z()

    def first_back(h):
        both = back_pair(G32, h + 2, KT2, h)
        for j in (0, 1):
            g = (both[:, j * ch : (j + 1) * ch] * S1[h + j + 3]).astype(BF).astype(F32)
            if 0 <= h + j < 4:
                add_sum(FIRST, g)
            put_wide(G31, h + j + 1, g)

    first_back(1)
    receive(g2_halo)
    for row in (0, 1, 6, 7):
        load_wide(G32, row, G2[row])
    first_back(-1)
    first_back(3)

    def pick(h, joined):
        return X[12 + joined * (h - 8)]

    stacked = jnp.concatenate(
        [
            jnp.concatenate([pick(h - 1, link(h)), X[h + 4], pick(h + 1, link(h + 1))], axis=0)
            for h in range(4)
        ],
        axis=1,
    )
    put_parts(FIRST, dot_nn(stacked, G31[1:5].reshape(4 * width, 3 * ch)).T)
    red[FIRST].start_core()
    for place, name in enumerate(ORDER):
        DB[place : place + 1] = jnp.sum(sums[name], axis=0, keepdims=True)
    if fused:
        ref.P_bias[0] = DB[...]
        ref.P_bias[1] = DB[...]
    else:
        ref.P_bias[0] = DB[...]
    red[BIAS].start_core()
    red[SECOND].start_z()

    GI = ref.GI

    def input_back(h):
        weights = back_weights(KT1, h)
        band = jnp.concatenate([G31[h + 1 + d] for d in (-1, 0, 1, 2)], axis=1)
        both = dot_nt(weights, band).astype(BF)
        GI[h] = both[:c_in]
        GI[h + 1] = both[c_in:]

    red[FIRST].start_z()
    input_back(0)
    input_back(2)
    out_gi = fetch(GI, ref.grad_inputs.at[0])
    GC = ref.GC
    for i in (0, 1):
        GC[i] = dot_nt(GB[i], WU[...]).astype(BF)
    out_gc = fetch(GC, ref.grad_coarse.at[0])
    red[THIRD].start_canvas()
    red[UP].start_canvas()
    red[SECOND].start_canvas()

    if fused:
        bias_red = red[BIAS]
        bias_red.core.wait_recv()
        bias_red.sums[z] = bias_red.part[k] + bias_red.twin[...]
        bias_red.along_copies = []
        for step in range(1, z_n):
            other = lax.rem(z + step, z_n)
            bias_red.along_copies.append(
                remote(
                    bias_red.sums.at[z], bias_red.along.at[z], bias_red.send.at[bias_red.index, step],
                    bias_red.recv.at[bias_red.index, step], (c, other * 2 + k),
                )
            )
        for copy in bias_red.along_copies:
            copy.start()
    red[FIRST].start_canvas()
    red[BIAS].start_canvas()

    for name in LAYERS + (BIAS,):
        red[name].finish()
    for pair in (x_halo, co_halo, g4_halo, g2_halo):
        sent(pair)
    for copy in (out_pool, out_act, out_gi, out_gc):
        copy.wait()


def finish_kernel(names, sizes, *refs):
    ref = types.SimpleNamespace(**dict(zip(names, refs)))
    ref.held, ref.sem = refs[-5:-1], refs[-1]
    ch, share = sizes
    r = lax.axis_index("rows")
    copies = []
    for place, name in enumerate(BIG):
        held = ref.held[place]
        enter = pltpu.make_async_copy(getattr(ref, name), held, ref.sem.at[0, place])
        leave = pltpu.make_async_copy(held, getattr(ref, "out_" + name), ref.sem.at[1, place])
        enter.start()
        copies.append((enter, leave))

    def total(slots):
        value = slots[0].astype(F32)
        for place in range(1, slots.shape[0]):
            value = value + slots[place].astype(F32)
        return value

    for name in (FIRST, SECOND, THIRD, FOURTH):
        value = total(getattr(ref, "RC_" + name))
        out = getattr(ref, "out_w_" + name)
        part = out.shape[3]
        for row_tap in range(3):
            out[row_tap] = value[:, :, row_tap * part : (row_tap + 1) * part]
    value = total(ref.RC_up)
    for a in (0, 1):
        for b in (0, 1):
            ref.out_w_up[a, b] = value[2 * a + b]
    sums = pltpu.roll(total(ref.RC_bias), lax.rem(ch - r * share, ch), 1)
    for place, name in enumerate(ORDER):
        getattr(ref, "out_b_" + name)[...] = sums[place : place + 1, :share]
    for enter, leave in copies:
        enter.wait()
        leave.start()
    for enter, leave in copies:
        leave.wait()


def on_device(
    fused,
    rows_n,
    canvas_n,
    inputs,
    coarse,
    row_cuts,
    col_cuts,
    w_first,
    b_first,
    w_second,
    b_second,
    w_up,
    b_up,
    w_third,
    b_third,
    w_fourth,
    b_fourth,
    cot_out,
    cot_pool,
):
    arg = dict(
        inputs=inputs,
        coarse=coarse,
        row_cuts=row_cuts,
        col_cuts=col_cuts,
        w_first=w_first,
        b_first=b_first,
        w_second=w_second,
        b_second=b_second,
        w_up=w_up,
        b_up=b_up,
        w_third=w_third,
        b_third=b_third,
        w_fourth=w_fourth,
        b_fourth=b_fourth,
        cot_out=cot_out,
        cot_pool=cot_pool,
    )
    _, length, width, c_in = arg["inputs"].shape
    ch = arg["w_first"].shape[3]
    c_coarse = arg["coarse"].shape[3]
    half = width // 2
    assert length == 4
    arg["inputs"] = jnp.swapaxes(arg["inputs"], 2, 3)
    arg["w_first"] = arg["w_first"].reshape(3, 3 * c_in, ch)
    arg["w_second"] = arg["w_second"].reshape(3, 3 * ch, ch)
    arg["w_third"] = arg["w_third"].reshape(3, 6 * ch, ch)
    arg["w_fourth"] = arg["w_fourth"].reshape(3, 3 * ch, ch)
    for name in ORDER:
        name = "b_" + name
        arg[name] = arg[name].reshape(1, ch)

    any_spec = pl.BlockSpec(memory_space=pl.ANY)
    vmem_spec = pl.BlockSpec(memory_space=pltpu.VMEM)
    in_specs = []
    for name in arg:
        if name == "row_cuts":
            in_specs.append(pl.BlockSpec(memory_space=pltpu.SMEM))
        elif name == "col_cuts" or name.startswith("b_"):
            in_specs.append(vmem_spec)
        else:
            in_specs.append(any_spec)

    owners, z_n = 8, 4
    share = ch // owners
    pieces = dict(
        fourth=((3, share, 3 * ch), BF),
        third=((3, share, 6 * ch), BF),
        up=((4, share, c_coarse), BF),
        second=((3, share, 3 * ch), BF),
        first=((3, share, 3 * c_in), BF),
        bias=((8, ch), F32),
    )
    outs = dict(
        activations=jax.ShapeDtypeStruct((1, 4, width, ch), BF),
        pooled=jax.ShapeDtypeStruct((1, 2, half, ch), BF),
        grad_inputs=jax.ShapeDtypeStruct((1, 4, c_in, width), BF),
        grad_coarse=jax.ShapeDtypeStruct((1, 2, half, c_coarse), BF),
    )
    scratch = dict(
        X=pltpu.VMEM((13, c_in, width), BF),
        CO=pltpu.VMEM((4, half, c_coarse), BF),
        COT=pltpu.VMEM((4, width, ch), BF),
        CP=pltpu.VMEM((2, half, ch), BF),
        WU=pltpu.VMEM((c_coarse, 4 * ch), BF),
        GL=pltpu.VMEM((width, ch), F32),
        GR=pltpu.VMEM((width, ch), F32),
        KB1=pltpu.VMEM((4, 3 * c_in, ch), BF),
        KB2=pltpu.VMEM((4, 3 * ch, ch), BF),
        KB3=pltpu.VMEM((4, 6 * ch, ch), BF),
        KB4=pltpu.VMEM((4, 3 * ch, ch), BF),
        KT1=pltpu.VMEM((4, c_in, 3 * ch), BF),
        KT2=pltpu.VMEM((4, ch, 3 * ch), BF),
        KT3=pltpu.VMEM((4, 2 * ch, 3 * ch), BF),
        KT4=pltpu.VMEM((4, ch, 3 * ch), BF),
        V3X=pltpu.VMEM((12, 3 * c_in, width), BF),
        V3A=pltpu.VMEM((10, width, 3 * ch), BF),
        V3J=pltpu.VMEM((8, width, 6 * ch), BF),
        V3C=pltpu.VMEM((6, width, 3 * ch), BF),
        VA=pltpu.VMEM((11, width, ch), BF),
        VJ=pltpu.VMEM((9, width, 2 * ch), BF),
        VC=pltpu.VMEM((7, width, ch), BF),
        S1=pltpu.VMEM((10, width, ch), F32),
        S2=pltpu.VMEM((4, width, ch), F32),
        S3=pltpu.VMEM((6, width, ch), F32),
        G4=pltpu.VMEM((8, width, ch), BF),
        G2=pltpu.VMEM((8, width, ch), BF),
        G34=pltpu.VMEM((8, width, 3 * ch), BF),
        G33=pltpu.VMEM((6, width, 3 * ch), BF),
        G32=pltpu.VMEM((8, width, 3 * ch), BF),
        G31=pltpu.VMEM((6, width, 3 * ch), BF),
        GB=pltpu.VMEM((2, half, 4 * ch), BF),
        SA=pltpu.VMEM((2, width, ch), F32),
        SB=pltpu.VMEM((width, ch), F32),
        DB=pltpu.VMEM((8, ch), F32),
        ACT=pltpu.VMEM((4, width, ch), BF),
        POOL=pltpu.VMEM((2, half, ch), BF),
        GI=pltpu.VMEM((4, c_in, width), BF),
        GC=pltpu.VMEM((2, half, c_coarse), BF),
        local_sem=pltpu.SemaphoreType.DMA((24,)),
        halo_send=pltpu.SemaphoreType.DMA((4, 2)),
        halo_recv=pltpu.SemaphoreType.DMA((4, 2)),
        red_send=pltpu.SemaphoreType.DMA((6, z_n + canvas_n)),
        red_recv=pltpu.SemaphoreType.DMA((6, z_n + canvas_n)),
    )
    for name, (shape, kind) in pieces.items():
        if name == BIAS:
            scratch["P_bias"] = pltpu.VMEM((2,) + shape, kind)
            scratch["RA_bias"] = pltpu.VMEM(shape, kind)
        else:
            scratch["P_" + name] = pltpu.VMEM((2, z_n) + shape, kind)
            scratch["RA_" + name] = pltpu.VMEM((z_n,) + shape, kind)
        scratch["Q_" + name] = pltpu.VMEM((z_n,) + shape, kind)
        scratch["RB_" + name] = pltpu.VMEM((z_n,) + shape, kind)
        if fused:
            landing = (canvas_n,) + shape
        else:
            landing = scratch["P_" + name].shape
        outs["RC_" + name] = jax.ShapeDtypeStruct(landing, kind)

    names = list(arg) + list(outs) + list(scratch)
    sizes = (width, ch, c_in, c_coarse, rows_n, canvas_n, fused)
    results = pl.pallas_call(
        functools.partial(level_kernel, names, sizes),
        out_shape=tuple(outs.values()),
        in_specs=in_specs,
        out_specs=tuple(any_spec for _ in outs),
        scratch_shapes=list(scratch.values()),
        compiler_params=pltpu.CompilerParams(
            collective_id=0, has_side_effects=True, vmem_limit_bytes=VMEM_BYTES
        ),
        name="level",
    )(*(arg[name] for name in arg))
    held = dict(zip(outs, results))

    if not fused:
        return unfused_tail(held, rows_n, ch, c_in, c_coarse)

    done = {"out_" + name: outs[name] for name in BIG}
    for name in (FIRST, SECOND, THIRD, FOURTH):
        shape = pieces[name][0]
        done["out_w_" + name] = jax.ShapeDtypeStruct((3, 3, share, shape[2] // 3), F32)
    done["out_w_up"] = jax.ShapeDtypeStruct((2, 2, share, c_coarse), F32)
    for name in ORDER:
        done["out_b_" + name] = jax.ShapeDtypeStruct((1, share), F32)
    finals = pl.pallas_call(
        functools.partial(finish_kernel, list(outs) + list(done), (ch, share)),
        out_shape=tuple(done.values()),
        in_specs=[any_spec if name in BIG else vmem_spec for name in outs],
        out_specs=tuple(any_spec if name[4:] in BIG else vmem_spec for name in done),
        scratch_shapes=[pltpu.VMEM(outs[name].shape, BF) for name in BIG] + [pltpu.SemaphoreType.DMA((2, 4))],
        name="finish",
    )(*results)
    final = dict(zip(done, finals))
    return ordered(
        {name: final["out_" + name] for name in BIG},
        {name: final["out_w_" + name] for name in LAYERS},
        {name: final["out_b_" + name].reshape(share) for name in LAYERS},
    )


def ordered(big, weights, biases):
    turned = {name: jnp.swapaxes(value, 2, 3) for name, value in weights.items()}
    pairs = []
    for name in ORDER:
        pairs += [turned[name], biases[name]]
    return (
        big["activations"],
        big["pooled"],
        jnp.swapaxes(big["grad_inputs"], 2, 3),
        big["grad_coarse"],
        *pairs,
    )


def unfused_tail(held, rows_n, ch, c_in, c_coarse):
    share = ch // rows_n
    offset = lax.axis_index("rows") * share

    def whole(name):
        parts = held["RC_" + name].astype(F32)
        blocks, piece, lanes = parts.shape[2:]
        parts = jnp.transpose(parts, (2, 1, 0, 3, 4)).reshape(blocks, ch, lanes)
        if name == UP:
            return parts.reshape(2, 2, ch, lanes)
        return jnp.transpose(parts.reshape(3, ch, 3, lanes // 3), (2, 0, 1, 3))

    weights = {name: whole(name) for name in LAYERS}
    weights, biases = lax.psum((weights, held["RC_bias"][0]), ("canvas", "rows"))
    weights = {name: lax.dynamic_slice_in_dim(value, offset, share, 2) for name, value in weights.items()}
    biases = lax.dynamic_slice_in_dim(biases, offset, share, 1)
    places = {FIRST: 0, SECOND: 1, UP: 2, THIRD: 3, FOURTH: 4}
    return ordered(held, weights, {name: biases[place] for name, place in places.items()})


def solution(mesh):
    rows_n, canvas_n = mesh.shape["rows"], mesh.shape["canvas"]
    fused = rows_n == 8 and canvas_n == 4
    split = P("canvas", "rows", None, None)
    pairs = (P(None, None, None, "rows"), P("rows"))
    return jax.shard_map(
        functools.partial(on_device, fused, rows_n, canvas_n),
        mesh=mesh,
        in_specs=(split, split, P("canvas", None), P("canvas", None)) + (P(),) * 10 + (split, split),
        out_specs=(split,) * 4 + pairs * 5,
        check_vma=False,
    )
```

```python
import functools
import types

import jax
import jax.numpy as jnp
from jax import lax
from jax.experimental import pallas as pl
from jax.experimental.pallas import tpu as pltpu
from jax.sharding import PartitionSpec as P

MESH = pl.DeviceIdType.MESH
BF = jnp.bfloat16
F32 = jnp.float32
VMEM_BYTES = 58 * 2**20

FIRST, SECOND, UP, THIRD, FOURTH = "first", "second", "up", "third", "fourth"
LAYERS = (FOURTH, THIRD, UP, SECOND, FIRST)
WIDE = (FOURTH, THIRD)
ORDER = (FIRST, SECOND, UP, THIRD, FOURTH)
BIG = ("activations", "pooled", "grad_inputs", "grad_coarse")


def dot_nn(a, b):
    return lax.dot_general(a, b, (((1,), (0,)), ((), ())), preferred_element_type=F32)


def dot_tn(a, b):
    return lax.dot_general(a, b, (((0,), (0,)), ((), ())), preferred_element_type=F32)


def dot_nt(a, b):
    return lax.dot_general(a, b, (((1,), (1,)), ((), ())), preferred_element_type=F32)


def silu_and_slope(values):
    sigma = 0.5 * jnp.tanh(0.5 * values) + 0.5
    act = values * sigma
    return act, sigma + act * (1.0 - sigma)


def level_kernel(names, sizes, *refs):
    ref = types.SimpleNamespace(**dict(zip(names, refs)))
    width, ch, c_in, c_coarse, rows_n, canvas_n, fused = sizes
    half = width // 2
    c = lax.axis_index("canvas")
    r = lax.axis_index("rows")
    z, k = r // 2, lax.rem(r, 2)
    up_id, down_id = (c, r - 1), (c, r + 1)
    has_up, has_down = r > 0, r < rows_n - 1
    z_n = rows_n // 2

    barrier = pltpu.get_barrier_semaphore()

    def greet(device):
        pl.semaphore_signal(barrier, inc=1, device_id=device, device_id_type=MESH)

    pl.when(has_up)(lambda: greet(up_id))
    pl.when(has_down)(lambda: greet(down_id))
    if fused:
        for step in range(1, z_n):
            greet((c, lax.rem(z + step, z_n) * 2 + k))
        for step in range(1, canvas_n):
            greet((lax.rem(c + step, canvas_n), r))

    local_sem = ref.local_sem
    used = [0]

    def fetch(src, dst):
        copy = pltpu.make_async_copy(src, dst, local_sem.at[used[0]])
        used[0] += 1
        copy.start()
        return copy

    X, CO = ref.X, ref.CO
    in_x = fetch(ref.inputs.at[0], X.at[pl.ds(4, 4)])
    in_w1 = fetch(ref.w_first, ref.KB1.at[pl.ds(1, 3)])
    in_co = fetch(ref.coarse.at[0], CO.at[pl.ds(1, 2)])
    in_up = [
        fetch(ref.w_up.at[a, b], ref.WU.at[:, pl.ds((2 * a + b) * ch, ch)])
        for a in (0, 1)
        for b in (0, 1)
    ]
    in_w2 = fetch(ref.w_second, ref.KB2.at[pl.ds(1, 3)])
    in_w3 = fetch(ref.w_third, ref.KB3.at[pl.ds(1, 3)])
    in_w4 = fetch(ref.w_fourth, ref.KB4.at[pl.ds(1, 3)])
    in_cot = fetch(ref.cot_out.at[0], ref.COT)
    in_cp = fetch(ref.cot_pool.at[0], ref.CP)

    first, total_rows = r * 4, rows_n * 4

    def link(h):
        row = first + h
        inside = jnp.logical_and(row > 0, row < total_rows)
        cut = ref.row_cuts[0, jnp.clip(row, 0, total_rows - 1)]
        return jnp.where(inside, 1 - cut, 0)

    open_row = 1.0 - ref.col_cuts[...].astype(F32)
    open_row = jnp.where(lax.broadcasted_iota(jnp.int32, (1, width), 1) > 0, open_row, 0.0)
    left_gate = jnp.broadcast_to(open_row, (128, width))
    right_gate = pltpu.roll(left_gate, width - 1, 1)
    GL, GR = ref.GL, ref.GR
    GL[...] = left_gate.T
    GR[...] = right_gate.T
    left_row, right_row = left_gate[:c_in], right_gate[:c_in]

    for bank in (ref.KB1, ref.KB2, ref.KB3, ref.KB4, ref.KT1, ref.KT2, ref.KT3, ref.KT4, ref.VA, ref.VJ, ref.VC):
        bank[0] = jnp.zeros(bank.shape[1:], BF)
    X[12] = jnp.zeros(X.shape[1:], BF)
    for part, lo in ((ref.P_fourth, 9), (ref.P_third, 18)):
        part[:, :, lo:] = jnp.zeros(part.shape[:2] + (part.shape[2] - lo,) + part.shape[3:], BF)

    halo_send, halo_recv = ref.halo_send, ref.halo_recv

    def remote(src, dst, send, recv, device):
        return pltpu.make_async_remote_copy(
            src_ref=src, dst_ref=dst, send_sem=send, recv_sem=recv, device_id=device, device_id_type=MESH
        )

    def pair_exchange(index, src_up, dst_up, src_down, dst_down):
        to_up = remote(src_up, dst_up, halo_send.at[index, 0], halo_recv.at[index, 0], up_id)
        to_down = remote(src_down, dst_down, halo_send.at[index, 1], halo_recv.at[index, 1], down_id)
        return to_up, to_down

    near_up = jnp.logical_and(k == 0, has_up)
    near_down = jnp.logical_and(k == 1, has_down)

    def pair_at(h):
        return h + k * (2 - 2 * h)

    def start_near(pair):
        pl.when(near_up)(lambda: pair[0].start())
        pl.when(near_down)(lambda: pair[1].start())

    def start_far(pair):
        pl.when(k == 0)(lambda: pair[1].start())
        pl.when(k == 1)(lambda: pair[0].start())

    def receive_near(pair):
        pl.when(near_up)(lambda: pair[1].wait_recv())
        pl.when(near_down)(lambda: pair[0].wait_recv())

    def receive_far(pair):
        pl.when(k == 0)(lambda: pair[0].wait_recv())
        pl.when(k == 1)(lambda: pair[1].wait_recv())

    def sent(pair):
        pl.when(has_up)(lambda: pair[0].wait_send())
        pl.when(has_down)(lambda: pair[1].wait_send())

    G4, G2 = ref.G4, ref.G2
    x_halo = pair_exchange(0, ref.inputs.at[0], X.at[pl.ds(8, 4)], ref.inputs.at[0], X.at[pl.ds(0, 4)])
    co_halo = pair_exchange(1, ref.coarse.at[0, 0], CO.at[3], ref.coarse.at[0, 1], CO.at[0])
    g4_halo = pair_exchange(2, G4.at[pl.ds(2, 2)], G4.at[pl.ds(6, 2)], G4.at[pl.ds(4, 2)], G4.at[pl.ds(0, 2)])
    g2_halo = pair_exchange(3, G2.at[pl.ds(2, 2)], G2.at[pl.ds(6, 2)], G2.at[pl.ds(4, 2)], G2.at[pl.ds(0, 2)])

    @pl.when(jnp.logical_not(has_up))
    def _():
        X[0:4] = jnp.zeros((4,) + X.shape[1:], BF)
        CO[0] = jnp.zeros(CO.shape[1:], BF)
        G4[0:2] = jnp.zeros((2,) + G4.shape[1:], BF)
        G2[0:2] = jnp.zeros((2,) + G2.shape[1:], BF)

    @pl.when(jnp.logical_not(has_down))
    def _():
        X[8:12] = jnp.zeros((4,) + X.shape[1:], BF)
        CO[3] = jnp.zeros(CO.shape[1:], BF)
        G4[6:8] = jnp.zeros((2,) + G4.shape[1:], BF)
        G2[6:8] = jnp.zeros((2,) + G2.shape[1:], BF)

    peers = (z_n - 1 + canvas_n - 1) if fused else 0
    pl.semaphore_wait(barrier, peers + has_up.astype(jnp.int32) + has_down.astype(jnp.int32))
    start_near(x_halo)
    start_far(x_halo)
    start_far(co_halo)
    start_near(co_halo)

    def widen(value):
        left = (pltpu.roll(value, 1, 0) * GL[...]).astype(BF)
        right = (pltpu.roll(value, width - 1, 0) * GR[...]).astype(BF)
        return left, value.astype(BF), right

    def put_wide(dst, row, value, base=0, stride=ch):
        for place, piece in enumerate(widen(value)):
            lo = base + place * stride
            dst[row, :, lo : lo + ch] = piece

    def taps(bank, h):
        ga, gb, gc = link(h), link(h + 1), link(h + 2)
        return bank[0], bank[ga], bank[2], bank[gb * 3], bank[gb], bank[gc * 3]

    def conv_pair(src, at, bank, h):
        band = jnp.concatenate([src[at + d] for d in (-1, 0, 1, 2)], axis=1)
        zero, up0, mid, down0, up1, down1 = taps(bank, h)
        weights = jnp.concatenate(
            [
                jnp.concatenate([up0, mid, down0, zero], axis=0),
                jnp.concatenate([zero, up1, mid, down1], axis=0),
            ],
            axis=1,
        )
        return dot_nn(band, weights)

    def back_weights(bank, h):
        zero, up0, mid, down0, up1, down1 = taps(bank, h)
        return jnp.concatenate(
            [
                jnp.concatenate([up0, mid, down0, zero], axis=1),
                jnp.concatenate([zero, up1, mid, down1], axis=1),
            ],
            axis=0,
        )

    def back_pair(src, at, bank, h):
        band = jnp.concatenate([src[at + d] for d in (-1, 0, 1, 2)], axis=1)
        return dot_nt(band, back_weights(bank, h))

    def bias(name):
        return getattr(ref, name)[...].astype(F32).reshape(1, ch)

    V3X, V3A, V3J, V3C = ref.V3X, ref.V3A, ref.V3J, ref.V3C
    VA, VJ, VC = ref.VA, ref.VJ, ref.VC
    S1, S2, S3 = ref.S1, ref.S2, ref.S3
    KB1, KB2, KB3, KB4 = ref.KB1, ref.KB2, ref.KB3, ref.KB4
    KT1, KT2, KT3, KT4 = ref.KT1, ref.KT2, ref.KT3, ref.KT4

    def widen_input(row):
        value = X[row].astype(F32)
        V3X[row, 0:c_in] = (pltpu.roll(value, 1, 1) * left_row).astype(BF)
        V3X[row, c_in : 2 * c_in] = X[row]
        V3X[row, 2 * c_in : 3 * c_in] = (pltpu.roll(value, width - 1, 1) * right_row).astype(BF)

    b_first, b_second, b_up, b_third, b_fourth = (
        bias("b_" + name) for name in ORDER
    )

    def first_pair(h):
        at = h + 4
        band = V3X[pl.ds(at - 1, 4)].reshape(4 * 3 * c_in, width)
        zero, up0, mid, down0, up1, down1 = [t.reshape(3 * c_in, ch) for t in taps(KB1, h)]
        weights = jnp.concatenate(
            [
                jnp.concatenate([up0, mid, down0, zero], axis=0),
                jnp.concatenate([zero, up1, mid, down1], axis=0),
            ],
            axis=1,
        )
        both = dot_tn(band, weights)
        for j in (0, 1):
            act, slope = silu_and_slope(both[:, j * ch : (j + 1) * ch] + b_first)
            S1[h + j + 3] = slope
            put_wide(V3A, h + j + 3, act)
            VA[h + j + 4] = act.astype(BF)

    in_x.wait()
    in_w1.wait()
    for row in (4, 5, 6, 7):
        widen_input(row)
    first_pair(1)

    SA, SB = ref.SA, ref.SB
    WU = ref.WU

    def up_rows(i):
        fine = dot_nn(CO[i], WU[...])
        for a in (0, 1):
            for b in (0, 1):
                lo = (2 * a + b) * ch
                piece = (fine[:, lo : lo + ch] + b_up).astype(BF).astype(F32)
                SA[a, pl.ds(b, half, stride=2), :] = piece
        for a in (0, 1):
            value = SA[a]
            put_wide(V3J, 2 * i + a, value, base=0, stride=2 * ch)
            VJ[2 * i + a + 1, :, :ch] = value.astype(BF)

    in_co.wait()
    for copy in in_up:
        copy.wait()
    up_rows(1)
    up_rows(2)

    in_w2.wait()
    in_w3.wait()
    in_w4.wait()
    for bank, back, part in ((KB1, KT1, c_in), (KB2, KT2, ch), (KB3, KT3, 2 * ch), (KB4, KT4, ch)):
        for row_tap in range(3):
            for col_tap in range(3):
                back[1 + (2 - row_tap), :, (2 - col_tap) * ch : (3 - col_tap) * ch] = bank[
                    1 + row_tap, col_tap * part : (col_tap + 1) * part
                ]

    pooled_buf = ref.POOL

    def second_pair(h):
        both = conv_pair(V3A, h + 3, KB2, h)
        acts = []
        for j in (0, 1):
            act, slope = silu_and_slope(both[:, j * ch : (j + 1) * ch] + b_second)
            S2[h + j + 2] = slope
            put_wide(V3J, h + j + 2, act, base=ch, stride=2 * ch)
            rounded = act.astype(BF)
            VJ[h + j + 3, :, ch:] = rounded
            acts.append(rounded.astype(F32))
        return acts

    def pool(acts, place):
        SB[...] = acts[0] + acts[1]
        pooled_buf[place] = (
            (SB[pl.ds(0, half, stride=2), :] + SB[pl.ds(1, half, stride=2), :]) * 0.25
        ).astype(BF)

    def third_pair(h):
        both = conv_pair(V3J, h + 2, KB3, h)
        for j in (0, 1):
            act, slope = silu_and_slope(both[:, j * ch : (j + 1) * ch] + b_third)
            S3[h + j + 1] = slope
            put_wide(V3C, h + j + 1, act)
            VC[h + j + 2] = act.astype(BF)

    receive_far(x_halo)
    for row in range(4):
        widen_input(8 - 8 * k + row)
    first_pair(pair_at(3))
    first_pair(pair_at(5))
    pool(second_pair(pair_at(2)), 1 - k)
    second_pair(pair_at(4))
    receive_far(co_halo)
    up_rows(3 - 3 * k)
    third_pair(pair_at(3))

    receive_near(x_halo)
    for row in range(4):
        widen_input(8 * k + row)
    first_pair(pair_at(-1))
    first_pair(pair_at(-3))
    pool(second_pair(pair_at(0)), k)
    out_pool = fetch(pooled_buf, ref.pooled.at[0])
    third_pair(1)
    second_pair(pair_at(-2))
    receive_near(co_halo)
    up_rows(3 * k)
    third_pair(pair_at(-1))

    G34, G33, G32, G31 = ref.G34, ref.G33, ref.G32, ref.G31
    COT, ACT = ref.COT, ref.ACT
    in_cot.wait()
    in_cp.wait()
    sums = {}

    def add_sum(name, value, own=None):
        part = jnp.sum(value.reshape(-1, 8, ch), axis=0)
        part = part if own is None else part * own
        sums[name] = part if name not in sums else sums[name] + part

    def fourth_pair(h):
        both = conv_pair(V3C, h + 1, KB4, h)
        for j in (0, 1):
            act, slope = silu_and_slope(both[:, j * ch : (j + 1) * ch] + b_fourth)
            ACT[h + j] = act.astype(BF)
            g = (COT[h + j].astype(F32) * slope).astype(BF)
            G4[h + j + 2] = g
            g = g.astype(F32)
            add_sum(FOURTH, g)
            put_wide(G34, h + j + 2, g)

    fourth_pair(pair_at(0))
    start_near(g4_halo)
    fourth_pair(pair_at(2))
    start_far(g4_halo)
    out_act = fetch(ACT, ref.activations.at[0])

    partner = (c, r + 1 - 2 * k)

    class Reduction:
        def __init__(self, index, name):
            self.part, self.twin = getattr(ref, "P_" + name), getattr(ref, "RA_" + name)
            self.sums, self.along = getattr(ref, "Q_" + name), getattr(ref, "RB_" + name)
            self.total, self.slots = getattr(ref, "T_" + name), getattr(ref, "RC_" + name)
            self.index, self.name = index, name

        def copy(self, phase, step, src, dst, device):
            place = self.index, 4 * phase + step
            return remote(src, dst, ref.red_send.at[place], ref.red_recv.at[place], device)

        def to_core(self):
            if fused:
                self.core = self.copy(0, 0, self.part.at[1 - k], self.twin, partner)
                self.core.start()

        def join_core(self):
            self.core.wait_recv()
            return self.part[k].astype(F32) + self.twin[...].astype(F32)

        def scatter(self, phase, own, n, src, dst, device):
            found = []
            for step in range(1, n):
                other = lax.rem(own + step, n)
                found.append(self.copy(phase, step, src.at[other], dst.at[own], device(other)))
                found[-1].start()
            return found

        def gather(self, phase, src):
            found = []
            for step in range(1, canvas_n):
                other = lax.rem(c + step, canvas_n)
                found.append(self.copy(phase, step, src, self.slots.at[c], (other, r)))
                found[-1].start()
            self.own = fetch(src, self.slots.at[c])
            return found

        def collect(self, copies, own, n, src, dst):
            for copy in copies:
                copy.wait_recv()
            total = src[own].astype(F32)
            for step in range(1, n):
                total = total + dst[lax.rem(own + step, n)].astype(F32)
            return total

        def to_z(self):
            if fused:
                self.sums[...] = self.join_core().astype(BF)
                self.z_copies = self.scatter(1, z, z_n, self.sums, self.along, lambda other: (c, other * 2 + k))

        def to_canvas(self):
            if fused:
                total = self.collect(self.z_copies, z, z_n, self.sums, self.along)
                self.total[...] = total.astype(BF)
                self.last = self.gather(2, self.total)

        def finish(self):
            if not fused:
                fetch(self.part, self.slots).wait()
                return
            self.core.wait_send()
            for copy in self.z_copies:
                copy.wait_send()
            for copy in self.last:
                copy.wait()
            self.own.wait()

    class WideReduction(Reduction):
        def to_quarters(self):
            if fused:
                total = self.join_core()
                quarter = total.shape[1] // canvas_n
                for place in range(canvas_n):
                    self.sums[place] = total[:, place * quarter : (place + 1) * quarter].astype(BF)
                self.c_copies = self.scatter(1, c, canvas_n, self.sums, self.along, lambda other: (other, r))

        def to_z(self):
            if fused:
                total = self.collect(self.c_copies, c, canvas_n, self.sums, self.along)
                self.zs, self.zl = getattr(ref, "ZS_" + self.name), getattr(ref, "ZL_" + self.name)
                self.zs[...] = total.astype(BF)
                self.z_copies = self.scatter(2, z, z_n, self.zs, self.zl, lambda other: (c, other * 2 + k))

        def to_canvas(self):
            if fused:
                total = self.collect(self.z_copies, z, z_n, self.zs, self.zl)
                self.total[...] = total.astype(BF)
                self.last = self.gather(3, self.total)

        def finish(self):
            if fused:
                for copy in self.c_copies:
                    copy.wait_send()
            super().finish()

    red = {
        name: (WideReduction if name in WIDE else Reduction)(index, name) for index, name in enumerate(LAYERS)
    }

    def put_parts(name, value):
        part = getattr(ref, "P_" + name)
        blocks, lanes = value.shape[0] // ch, value.shape[1] // 128
        for block in range(blocks):
            first = (block if name == UP else blocks - 1 - block) * lanes
            for owner in range(8):
                lo = block * ch + owner * 16
                for lane in range(lanes):
                    part[owner % 2, owner // 2, first + lane] = value[
                        lo : lo + 16, lane * 128 : (lane + 1) * 128
                    ].astype(BF)

    def row_stack(src, off, h):
        return jnp.concatenate(
            [src[link(h) * (h - 1 + off)], src[h + off], src[link(h + 1) * (h + 1 + off)]], axis=1
        )

    def weight_grad(grad3, at, src, off):
        band = grad3[pl.ds(at, 4)].reshape(4 * width, 3 * ch)
        stacked = jnp.concatenate([row_stack(src, off, h) for h in range(4)], axis=0)
        return dot_tn(band, stacked)

    def load_wide(dst, row, src):
        put_wide(dst, row, src[row].astype(F32))

    def is_own(row):
        return jnp.logical_and(row >= 0, row < 4).astype(F32)

    def third_back(h):
        both = back_pair(G34, h + 2, KT4, h)
        for j in (0, 1):
            g = (both[:, j * ch : (j + 1) * ch] * S3[h + j + 1]).astype(BF).astype(F32)
            add_sum(THIRD, g, is_own(h + j))
            put_wide(G33, h + j + 1, g)

    put_parts(FOURTH, weight_grad(G34, 2, VC, 2))
    red[FOURTH].to_core()
    third_back(1)
    receive_far(g4_halo)
    for row in (0, 1):
        load_wide(G34, 6 - 6 * k + row, G4)
    third_back(pair_at(3))
    if fused:
        red[FOURTH].to_quarters()
    receive_near(g4_halo)
    for row in (0, 1):
        load_wide(G34, 6 * k + row, G4)
    third_back(pair_at(-1))

    GB, CP = ref.GB, ref.CP

    def joined_back(h):
        i = h // 2
        spread = CP[i].astype(F32) * 0.25
        SB[pl.ds(0, half, stride=2), :] = spread
        SB[pl.ds(1, half, stride=2), :] = spread
        for a in (0, 1):
            row = h + a
            band = jnp.concatenate([G33[row + 1 + d] for d in (-1, 0, 1)], axis=1)
            weights = jnp.concatenate([KT3[link(row)], KT3[2], KT3[link(row + 1) * 3]], axis=1)
            d_joined = dot_nt(band, weights)
            g_up = d_joined[:, :ch].astype(BF).astype(F32)
            add_sum(UP, g_up)
            SA[a] = g_up
            for b in (0, 1):
                lo = (2 * a + b) * ch
                GB[i, :, lo : lo + ch] = SA[a, pl.ds(b, half, stride=2), :].astype(BF)
            g = ((d_joined[:, ch:] + SB[...]) * S2[row + 2]).astype(BF)
            G2[row + 2] = g
            g = g.astype(F32)
            add_sum(SECOND, g)
            put_wide(G32, row + 2, g)

    joined_back(pair_at(0))
    start_near(g2_halo)
    put_parts(THIRD, weight_grad(G33, 1, VJ, 3))
    red[THIRD].to_core()
    red[FOURTH].to_z()
    joined_back(pair_at(2))
    start_far(g2_halo)
    if fused:
        red[THIRD].to_quarters()
    put_parts(SECOND, weight_grad(G32, 2, VA, 4))
    red[SECOND].to_core()
    bands = GB[...].reshape(2 * half, 4 * ch)
    put_parts(UP, dot_tn(bands, CO[1:3].reshape(2 * half, c_coarse)))
    red[UP].to_core()

    def first_back(h):
        both = back_pair(G32, h + 2, KT2, h)
        for j in (0, 1):
            g = (both[:, j * ch : (j + 1) * ch] * S1[h + j + 3]).astype(BF).astype(F32)
            add_sum(FIRST, g, is_own(h + j))
            put_wide(G31, h + j + 1, g)

    first_back(1)
    receive_far(g2_halo)
    for row in (0, 1):
        load_wide(G32, 6 - 6 * k + row, G2)
    first_back(pair_at(3))
    red[FOURTH].to_canvas()
    red[SECOND].to_z()
    receive_near(g2_halo)
    for row in (0, 1):
        load_wide(G32, 6 * k + row, G2)
    first_back(pair_at(-1))

    def pick(h, joined):
        return X[12 + joined * (h - 8)]

    stacked = jnp.concatenate(
        [
            jnp.concatenate([pick(h - 1, link(h)), X[h + 4], pick(h + 1, link(h + 1))], axis=0)
            for h in range(4)
        ],
        axis=1,
    )
    grad = dot_nn(stacked, G31[1:5].reshape(4 * width, 3 * ch)).T
    put_parts(FIRST, jnp.concatenate([grad, jnp.zeros((3 * ch, 256 - 3 * c_in), F32)], axis=1))
    DB = ref.DB
    DB[...] = jnp.zeros(DB.shape, F32)
    for place, name in enumerate(ORDER):
        DB[place : place + 1] = jnp.sum(sums[name], axis=0, keepdims=True)
    for owner in range(8):
        ref.P_first[owner % 2, owner // 2, 6] = DB[...].astype(BF)
    red[FIRST].to_core()
    red[UP].to_z()
    red[THIRD].to_z()

    GI = ref.GI

    def input_back(h):
        weights = back_weights(KT1, h)
        band = jnp.concatenate([G31[h + 1 + d] for d in (-1, 0, 1, 2)], axis=1)
        both = dot_nt(weights, band).astype(BF)
        GI[h] = both[:c_in]
        GI[h + 1] = both[c_in:]

    red[FIRST].to_z()
    input_back(0)
    input_back(2)
    out_gi = fetch(GI, ref.grad_inputs.at[0])
    GC = ref.GC
    for i in (0, 1):
        GC[i] = dot_nt(GB[i], WU[...]).astype(BF)
    out_gc = fetch(GC, ref.grad_coarse.at[0])
    red[SECOND].to_canvas()
    red[UP].to_canvas()
    red[THIRD].to_canvas()
    red[FIRST].to_canvas()

    for name in LAYERS:
        red[name].finish()
    for pair in (x_halo, co_halo, g4_halo, g2_halo):
        sent(pair)
    for copy in (out_pool, out_act, out_gi, out_gc):
        copy.wait()


def finish_kernel(names, staged, sizes, *refs):
    ref = types.SimpleNamespace(**dict(zip(names, refs)))
    held = types.SimpleNamespace(**dict(zip(staged, refs[len(names) : -1])))
    sem = refs[-1]
    ch, share = sizes
    r = lax.axis_index("rows")
    enter, leave = {}, {}
    for place, name in enumerate(staged):
        stage = getattr(held, name)
        if name in BIG or name.startswith("RC"):
            enter[name] = pltpu.make_async_copy(getattr(ref, name), stage, sem.at[0, place])
            enter[name].start()
        if name in BIG or name.startswith("w"):
            leave[name] = pltpu.make_async_copy(stage, getattr(ref, "out_" + name), sem.at[1, place])

    def tiles(name):
        slots = getattr(held, "RC_" + name)
        if name in WIDE:
            quarter = slots.shape[1]
            return lambda t: slots[t // quarter, t % quarter].astype(F32)

        def total(t):
            value = slots[0, t].astype(F32)
            for place in range(1, slots.shape[0]):
                value = value + slots[place, t].astype(F32)
            return value

        return total

    for name in BIG + LAYERS:
        if name in BIG:
            enter[name].wait()
            leave[name].start()
            continue
        enter["RC_" + name].wait()
        tile = tiles(name)
        out = getattr(held, "w_" + name)
        if name == FIRST:
            part = out.shape[3]
            for col_tap in range(3):
                for row_tap in range(3):
                    value = tile(2 * col_tap + row_tap // 2)
                    lo = part * (row_tap % 2)
                    out[row_tap, col_tap] = value[:, lo : lo + part]
            sums = pltpu.roll(tile(6), lax.rem(ch - r * share, ch), 1)
            for place, layer in enumerate(ORDER):
                getattr(ref, "out_b_" + layer)[...] = sums[place : place + 1, :share]
        elif name == UP:
            for a in (0, 1):
                for b in (0, 1):
                    for lane in (0, 1):
                        out[a, b, :, lane * 128 : (lane + 1) * 128] = tile(4 * a + 2 * b + lane)
        else:
            lanes = out.shape[3] // 128
            for col_tap in range(3):
                for row_tap in range(3):
                    for lane in range(lanes):
                        out[row_tap, col_tap, :, lane * 128 : (lane + 1) * 128] = tile(
                            (3 * col_tap + row_tap) * lanes + lane
                        )
        leave["w_" + name].start()
    for copy in leave.values():
        copy.wait()


def on_device(
    fused,
    rows_n,
    canvas_n,
    inputs,
    coarse,
    row_cuts,
    col_cuts,
    w_first,
    b_first,
    w_second,
    b_second,
    w_up,
    b_up,
    w_third,
    b_third,
    w_fourth,
    b_fourth,
    cot_out,
    cot_pool,
):
    arg = dict(
        inputs=inputs,
        coarse=coarse,
        row_cuts=row_cuts,
        col_cuts=col_cuts,
        w_first=w_first,
        b_first=b_first,
        w_second=w_second,
        b_second=b_second,
        w_up=w_up,
        b_up=b_up,
        w_third=w_third,
        b_third=b_third,
        w_fourth=w_fourth,
        b_fourth=b_fourth,
        cot_out=cot_out,
        cot_pool=cot_pool,
    )
    _, length, width, c_in = arg["inputs"].shape
    ch = arg["w_first"].shape[3]
    c_coarse = arg["coarse"].shape[3]
    half = width // 2
    assert length == 4
    arg["inputs"] = jnp.swapaxes(arg["inputs"], 2, 3)
    arg["w_first"] = arg["w_first"].reshape(3, 3 * c_in, ch)
    arg["w_second"] = arg["w_second"].reshape(3, 3 * ch, ch)
    arg["w_third"] = arg["w_third"].reshape(3, 6 * ch, ch)
    arg["w_fourth"] = arg["w_fourth"].reshape(3, 3 * ch, ch)
    for name in ORDER:
        name = "b_" + name
        arg[name] = arg[name].reshape(1, ch)

    any_spec = pl.BlockSpec(memory_space=pl.ANY)
    vmem_spec = pl.BlockSpec(memory_space=pltpu.VMEM)
    in_specs = []
    for name in arg:
        if name == "row_cuts":
            in_specs.append(pl.BlockSpec(memory_space=pltpu.SMEM))
        elif name == "col_cuts" or name.startswith("b_"):
            in_specs.append(vmem_spec)
        else:
            in_specs.append(any_spec)

    owners, z_n = 8, 4
    share = ch // owners
    tiles = dict(fourth=12, third=20, up=8, second=9, first=7)
    outs = dict(
        activations=jax.ShapeDtypeStruct((1, 4, width, ch), BF),
        pooled=jax.ShapeDtypeStruct((1, 2, half, ch), BF),
        grad_inputs=jax.ShapeDtypeStruct((1, 4, c_in, width), BF),
        grad_coarse=jax.ShapeDtypeStruct((1, 2, half, c_coarse), BF),
    )
    scratch = dict(
        X=pltpu.VMEM((13, c_in, width), BF),
        CO=pltpu.VMEM((4, half, c_coarse), BF),
        COT=pltpu.VMEM((4, width, ch), BF),
        CP=pltpu.VMEM((2, half, ch), BF),
        WU=pltpu.VMEM((c_coarse, 4 * ch), BF),
        GL=pltpu.VMEM((width, ch), F32),
        GR=pltpu.VMEM((width, ch), F32),
        KB1=pltpu.VMEM((4, 3 * c_in, ch), BF),
        KB2=pltpu.VMEM((4, 3 * ch, ch), BF),
        KB3=pltpu.VMEM((4, 6 * ch, ch), BF),
        KB4=pltpu.VMEM((4, 3 * ch, ch), BF),
        KT1=pltpu.VMEM((4, c_in, 3 * ch), BF),
        KT2=pltpu.VMEM((4, ch, 3 * ch), BF),
        KT3=pltpu.VMEM((4, 2 * ch, 3 * ch), BF),
        KT4=pltpu.VMEM((4, ch, 3 * ch), BF),
        V3X=pltpu.VMEM((12, 3 * c_in, width), BF),
        V3A=pltpu.VMEM((10, width, 3 * ch), BF),
        V3J=pltpu.VMEM((8, width, 6 * ch), BF),
        V3C=pltpu.VMEM((6, width, 3 * ch), BF),
        VA=pltpu.VMEM((11, width, ch), BF),
        VJ=pltpu.VMEM((9, width, 2 * ch), BF),
        VC=pltpu.VMEM((7, width, ch), BF),
        S1=pltpu.VMEM((10, width, ch), F32),
        S2=pltpu.VMEM((8, width, ch), F32),
        S3=pltpu.VMEM((6, width, ch), F32),
        G4=pltpu.VMEM((8, width, ch), BF),
        G2=pltpu.VMEM((8, width, ch), BF),
        G34=pltpu.VMEM((8, width, 3 * ch), BF),
        G33=pltpu.VMEM((6, width, 3 * ch), BF),
        G32=pltpu.VMEM((8, width, 3 * ch), BF),
        G31=pltpu.VMEM((6, width, 3 * ch), BF),
        GB=pltpu.VMEM((2, half, 4 * ch), BF),
        SA=pltpu.VMEM((2, width, ch), F32),
        SB=pltpu.VMEM((width, ch), F32),
        DB=pltpu.VMEM((16, ch), F32),
        ACT=pltpu.VMEM((4, width, ch), BF),
        POOL=pltpu.VMEM((2, half, ch), BF),
        GI=pltpu.VMEM((4, c_in, width), BF),
        GC=pltpu.VMEM((2, half, c_coarse), BF),
        local_sem=pltpu.SemaphoreType.DMA((24,)),
        halo_send=pltpu.SemaphoreType.DMA((4, 2)),
        halo_recv=pltpu.SemaphoreType.DMA((4, 2)),
        red_send=pltpu.SemaphoreType.DMA((5, 16)),
        red_recv=pltpu.SemaphoreType.DMA((5, 16)),
    )
    for name, count in tiles.items():

        def buffer(*lead):
            return pltpu.VMEM(lead + (16, 128), BF)

        landing = (canvas_n, count, 16, 128)
        scratch["P_" + name] = buffer(2, z_n, count)
        scratch["RA_" + name] = buffer(z_n, count)
        if name in WIDE:
            quarter = count // 4
            scratch["Q_" + name] = buffer(4, z_n, quarter)
            scratch["RB_" + name] = buffer(4, z_n, quarter)
            scratch["ZS_" + name] = buffer(z_n, quarter)
            scratch["ZL_" + name] = buffer(z_n, quarter)
            scratch["T_" + name] = buffer(quarter)
            landing = (4, quarter, 16, 128)
        else:
            scratch["Q_" + name] = buffer(z_n, count)
            scratch["RB_" + name] = buffer(z_n, count)
            scratch["T_" + name] = buffer(count)
        if not fused:
            landing = (2, z_n, count, 16, 128)
        outs["RC_" + name] = jax.ShapeDtypeStruct(landing, BF)

    names = list(arg) + list(outs) + list(scratch)
    sizes = (width, ch, c_in, c_coarse, rows_n, canvas_n, fused)
    results = pl.pallas_call(
        functools.partial(level_kernel, names, sizes),
        out_shape=tuple(outs.values()),
        in_specs=in_specs,
        out_specs=tuple(any_spec for _ in outs),
        scratch_shapes=list(scratch.values()),
        compiler_params=pltpu.CompilerParams(
            collective_id=0, has_side_effects=True, vmem_limit_bytes=VMEM_BYTES
        ),
        name="level",
    )(*(arg[name] for name in arg))
    held = dict(zip(outs, results))

    if not fused:
        return unfused_tail(held, rows_n, ch, c_in, c_coarse)

    done = {"out_" + name: outs[name] for name in BIG}
    parts = dict(first=c_in, second=ch, third=2 * ch, fourth=ch)
    for name in LAYERS:
        if name == UP:
            shape = (2, 2, share, c_coarse)
        else:
            shape = (3, 3, share, parts[name])
        done["out_w_" + name] = jax.ShapeDtypeStruct(shape, F32)
    for name in LAYERS:
        done["out_b_" + name] = jax.ShapeDtypeStruct((1, share), F32)
    staged = {name: outs[name] for name in outs}
    staged.update({"w_" + name: done["out_w_" + name] for name in LAYERS})
    finals = pl.pallas_call(
        functools.partial(finish_kernel, list(outs) + list(done), list(staged), (ch, share)),
        out_shape=tuple(done.values()),
        in_specs=[any_spec] * len(outs),
        out_specs=tuple(vmem_spec if name.startswith("out_b") else any_spec for name in done),
        scratch_shapes=[pltpu.VMEM(like.shape, like.dtype) for like in staged.values()]
        + [pltpu.SemaphoreType.DMA((2, len(staged)))],
        name="finish",
    )(*results)
    final = dict(zip(done, finals))
    return ordered(
        {name: final["out_" + name] for name in BIG},
        {name: final["out_w_" + name] for name in LAYERS},
        {name: final["out_b_" + name].reshape(share) for name in LAYERS},
    )


def ordered(big, weights, biases):
    turned = {name: jnp.swapaxes(value, 2, 3) for name, value in weights.items()}
    pairs = []
    for name in ORDER:
        pairs += [turned[name], biases[name]]
    return (
        big["activations"],
        big["pooled"],
        jnp.swapaxes(big["grad_inputs"], 2, 3),
        big["grad_coarse"],
        *pairs,
    )


def unfused_tail(held, rows_n, ch, c_in, c_coarse):
    share = ch // rows_n
    offset = lax.axis_index("rows") * share

    def whole(name):
        parts = held["RC_" + name].astype(F32)
        return jnp.transpose(parts, (2, 1, 0, 3, 4)).reshape(-1, ch, 128)

    tiles = lax.psum({name: whole(name) for name in LAYERS}, ("canvas", "rows"))
    weights = {}
    for name in LAYERS:
        if name == UP:
            value = tiles[name].reshape(4, 1, 2, ch, 128)
        elif name == FIRST:
            value = jnp.swapaxes(tiles[name][:6].reshape(3, 2, ch, 128), 1, 2).reshape(3, ch, 256)
            value = jnp.transpose(value[..., : 3 * c_in].reshape(3, ch, 3, c_in), (0, 2, 1, 3))[:, :, None]
        else:
            lanes = 2 if name == THIRD else 1
            value = tiles[name][: 9 * lanes].reshape(3, 3, lanes, ch, 128)
        value = jnp.transpose(value, (1, 0, 3, 2, 4)).reshape(value.shape[1], value.shape[0], ch, -1)
        if name == UP:
            value = value.reshape(2, 2, ch, c_coarse)
        weights[name] = lax.dynamic_slice_in_dim(value, offset, share, 2)
    biases = lax.dynamic_slice_in_dim(tiles[FIRST][6], offset, share, 1)
    return ordered(held, weights, {name: biases[place] for place, name in enumerate(ORDER)})


def solution(mesh):
    rows_n, canvas_n = mesh.shape["rows"], mesh.shape["canvas"]
    fused = rows_n == 8 and canvas_n == 4
    split = P("canvas", "rows", None, None)
    pairs = (P(None, None, None, "rows"), P("rows"))
    return jax.shard_map(
        functools.partial(on_device, fused, rows_n, canvas_n),
        mesh=mesh,
        in_specs=(split, split, P("canvas", None), P("canvas", None)) + (P(),) * 10 + (split, split),
        out_specs=(split,) * 4 + pairs * 5,
        check_vma=False,
    )
```

```python
import functools
import types

import jax
import jax.numpy as jnp
from jax import lax
from jax.experimental import pallas as pl
from jax.experimental.pallas import tpu as pltpu
from jax.sharding import PartitionSpec as P

MESH = pl.DeviceIdType.MESH
BF = jnp.bfloat16
F32 = jnp.float32
VMEM_BYTES = 58 * 2**20

FIRST, SECOND, UP, THIRD, FOURTH = "first", "second", "up", "third", "fourth"
THIRD_A, THIRD_B = "third_a", "third_b"
GROUPS = (FOURTH, THIRD_A, THIRD_B, SECOND, UP, FIRST)
WIDE = (FOURTH, THIRD_A, SECOND, UP)
ORDER = (FIRST, SECOND, UP, THIRD, FOURTH)
BIG = ("activations", "pooled", "grad_inputs", "grad_coarse")


def dot_nn(a, b):
    return lax.dot_general(a, b, (((1,), (0,)), ((), ())), preferred_element_type=F32)


def dot_tn(a, b):
    return lax.dot_general(a, b, (((0,), (0,)), ((), ())), preferred_element_type=F32)


def dot_nt(a, b):
    return lax.dot_general(a, b, (((1,), (1,)), ((), ())), preferred_element_type=F32)


def silu_and_slope(values):
    sigma = 0.5 * jnp.tanh(0.5 * values) + 0.5
    act = values * sigma
    return act, sigma + act * (1.0 - sigma)


def level_kernel(names, sizes, *refs):
    ref = types.SimpleNamespace(**dict(zip(names, refs)))
    width, ch, c_in, c_coarse, rows_n, canvas_n, fused = sizes
    half = width // 2
    c = lax.axis_index("canvas")
    r = lax.axis_index("rows")
    z, k = r // 2, lax.rem(r, 2)
    z_n = rows_n // 2

    near_id, far_id = (c, r - 1 + 2 * k), (c, r + 1 - 2 * k)
    has_near = jnp.logical_and(near_id[1] >= 0, near_id[1] < rows_n)

    def flip(index, last):
        return index + k * (last - 2 * index)

    barrier = pltpu.get_barrier_semaphore()

    def greet(device):
        pl.semaphore_signal(barrier, inc=1, device_id=device, device_id_type=MESH)

    pl.when(has_near)(lambda: greet(near_id))
    greet(far_id)
    if fused:
        for step in range(1, z_n):
            greet((c, lax.rem(z + step, z_n) * 2 + k))
        for step in range(1, canvas_n):
            greet((lax.rem(c + step, canvas_n), r))

    used = [0]

    def fetch(src, dst):
        copy = pltpu.make_async_copy(src, dst, ref.local_sem.at[used[0]])
        used[0] += 1
        assert used[0] <= ref.local_sem.shape[0]
        copy.start()
        return copy

    def fetch_taps(weights, bank):
        return [fetch(weights.at[flip(tap, 2)], bank.at[1 + tap]) for tap in range(3)]

    def wait(copies):
        for copy in copies:
            copy.wait()

    X, CO, WU = ref.X, ref.CO, ref.WU
    KB1, KB2, KU3, KB3, KB4 = ref.KB1, ref.KB2, ref.KU3, ref.KB3, ref.KB4
    KT1, KT2, KT3, KT4 = ref.KT1, ref.KT2, ref.KT3, ref.KT4
    in_x = [fetch(ref.inputs.at[0, flip(row, 3)], X.at[4 + row]) for row in range(4)]
    in_w1 = fetch_taps(ref.w_first, KB1)

    def remote(src, dst, send, recv, device):
        return pltpu.make_async_remote_copy(
            src_ref=src, dst_ref=dst, send_sem=send, recv_sem=recv, device_id=device, device_id_type=MESH
        )

    halo_count = [0]

    def exchange(src_near, dst_near, src_far, dst_far):
        place = halo_count[0]
        halo_count[0] += 1
        near = remote(src_near, dst_near, ref.halo_send.at[place, 0], ref.halo_recv.at[place, 0], near_id)
        far = remote(src_far, dst_far, ref.halo_send.at[place, 1], ref.halo_recv.at[place, 1], far_id)
        return near, far

    def start_near(pairs):
        def start():
            for pair in pairs:
                pair[0].start()

        pl.when(has_near)(start)

    def start_far(pairs):
        for pair in pairs:
            pair[1].start()

    def receive_near(pairs):
        def receive():
            for pair in pairs:
                pair[0].wait_recv()

        pl.when(has_near)(receive)

    def receive_far(pairs):
        for pair in pairs:
            pair[1].wait_recv()

    def sent(pairs):
        def near():
            for pair in pairs:
                pair[0].wait_send()

        pl.when(has_near)(near)
        for pair in pairs:
            pair[1].wait_send()

    G4, G2 = ref.G4, ref.G2

    def row_exchange(buffer, row):
        return exchange(
            buffer.at[2 + row], buffer.at[1 - row], buffer.at[5 - row], buffer.at[6 + row]
        )

    x_halo = []
    for row in range(4):
        mine, last = ref.inputs.at[0, flip(row, 3)], ref.inputs.at[0, flip(3 - row, 3)]
        x_halo.append(exchange(mine, X.at[3 - row], last, X.at[8 + row]))
    co_halo = [exchange(ref.coarse.at[0, flip(0, 1)], CO.at[0], ref.coarse.at[0, flip(1, 1)], CO.at[3])]
    g4_halo = [row_exchange(G4, 0), row_exchange(G4, 1)]
    g2_halo, g2_second = [row_exchange(G2, 0)], [row_exchange(G2, 1)]

    in_co = [fetch(ref.coarse.at[0, flip(i, 1)], CO.at[1 + i]) for i in (0, 1)]
    in_up = [
        fetch(ref.w_up.at[flip(a, 1), b], WU.at[:, pl.ds((2 * a + b) * ch, ch)]) for a in (0, 1) for b in (0, 1)
    ]
    in_w2 = fetch_taps(ref.w_second, KB2)
    in_w3 = [
        fetch(ref.w_third.at[flip(tap, 2), :, pl.ds(lo, ch)], bank.at[1 + tap])
        for bank, lo in ((KU3, 0), (KB3, ch))
        for tap in range(3)
    ]
    in_w4 = fetch_taps(ref.w_fourth, KB4)
    in_cot = [fetch(ref.cot_out.at[0, flip(row, 3)], ref.COT.at[row]) for row in range(4)]
    in_cp = [fetch(ref.cot_pool.at[0, flip(i, 1)], ref.CP.at[i]) for i in (0, 1)]

    @pl.when(jnp.logical_not(has_near))
    def _():
        X[0:4] = jnp.zeros((4,) + X.shape[1:], BF)
        CO[0] = jnp.zeros(CO.shape[1:], BF)
        G4[0:2] = jnp.zeros((2,) + G4.shape[1:], BF)
        G2[0:2] = jnp.zeros((2,) + G2.shape[1:], BF)

    first, total_rows = r * 4, rows_n * 4

    def link(h):
        row = first + flip(h, 4)
        inside = jnp.logical_and(row > 0, row < total_rows)
        cut = ref.row_cuts[0, jnp.clip(row, 0, total_rows - 1)]
        return jnp.where(inside, 1 - cut, 0)

    open_row = 1.0 - ref.col_cuts[...].astype(F32)
    open_row = jnp.where(lax.broadcasted_iota(jnp.int32, (1, width), 1) > 0, open_row, 0.0)
    left_gate = jnp.broadcast_to(open_row, (128, width))
    right_gate = pltpu.roll(left_gate, width - 1, 1)
    GL, GR = ref.GL, ref.GR
    GL[...] = left_gate.T
    GR[...] = right_gate.T
    left_row, right_row = left_gate[:c_in], right_gate[:c_in]

    for bank in (KB1, KB2, KU3, KB3, KB4, KT1, KT2, KT3, KT4, ref.VA, ref.VJ, ref.VC):
        bank[0] = jnp.zeros(bank.shape[1:], BF)
    X[12] = jnp.zeros(X.shape[1:], BF)
    for part in (ref.P_fourth, ref.P_third_a, ref.P_third_b, ref.P_second):
        if part.shape[2] > 9:
            part[:, :, 9:] = jnp.zeros(part.shape[:2] + (part.shape[2] - 9,) + part.shape[3:], BF)

    peers = (z_n - 1 + canvas_n - 1) if fused else 0
    pl.semaphore_wait(barrier, peers + 1 + has_near.astype(jnp.int32))
    start_near(x_halo)
    start_far(x_halo)
    start_far(co_halo)

    def put_wide(dst, row, value, base=0, stride=ch):
        left = (pltpu.roll(value, 1, 0) * GL[...]).astype(BF)
        right = (pltpu.roll(value, width - 1, 0) * GR[...]).astype(BF)
        for place, piece in enumerate((left, value.astype(BF), right)):
            lo = base + place * stride
            dst[row, :, lo : lo + ch] = piece

    def taps(bank, h):
        ga, gb, gc = link(h), link(h + 1), link(h + 2)
        found = bank[0], bank[ga], bank[2], bank[gb * 3], bank[gb], bank[gc * 3]
        return [tap.reshape(-1, tap.shape[-1]) for tap in found]

    def forward_weights(bank, h):
        zero, up0, mid, down0, up1, down1 = taps(bank, h)
        return jnp.concatenate(
            [
                jnp.concatenate([up0, mid, down0, zero], axis=0),
                jnp.concatenate([zero, up1, mid, down1], axis=0),
            ],
            axis=1,
        )

    def back_weights(bank, h):
        zero, up0, mid, down0, up1, down1 = taps(bank, h)
        return jnp.concatenate(
            [
                jnp.concatenate([up0, mid, down0, zero], axis=1),
                jnp.concatenate([zero, up1, mid, down1], axis=1),
            ],
            axis=0,
        )

    def band(src, at, reach=(-1, 0, 1, 2)):
        return jnp.concatenate([src[at + d] for d in reach], axis=1)

    def conv_pair(src, at, bank, h):
        return dot_nn(band(src, at), forward_weights(bank, h))

    def back_pair(src, at, bank, h):
        return dot_nt(band(src, at), back_weights(bank, h))

    def back_row(src, at, bank, h):
        weights = jnp.concatenate([bank[link(h)], bank[2], bank[link(h + 1) * 3]], axis=1)
        return dot_nt(band(src, at, (-1, 0, 1)), weights)

    def bias(layer):
        return getattr(ref, "b_" + layer)[...].astype(F32).reshape(1, ch)

    b_first, b_second, b_up, b_third, b_fourth = (bias(layer) for layer in ORDER)
    V3X, V3A, V3U, V3B, V3C = ref.V3X, ref.V3A, ref.V3U, ref.V3B, ref.V3C
    VA, VJ, VC = ref.VA, ref.VJ, ref.VC
    S1, S2, S3 = ref.S1, ref.S2, ref.S3
    SA, SB = ref.SA, ref.SB

    def widen_input(row):
        value = X[row].astype(F32)
        V3X[row, 0:c_in] = (pltpu.roll(value, 1, 1) * left_row).astype(BF)
        V3X[row, c_in : 2 * c_in] = X[row]
        V3X[row, 2 * c_in : 3 * c_in] = (pltpu.roll(value, width - 1, 1) * right_row).astype(BF)

    def first_pair(h):
        rows = V3X[h + 3 : h + 7].reshape(4 * 3 * c_in, width)
        both = dot_tn(rows, forward_weights(KB1, h))
        for j in (0, 1):
            act, slope = silu_and_slope(both[:, j * ch : (j + 1) * ch] + b_first)
            if -1 <= h + j < 5:
                S1[h + j + 1] = slope
                VA[h + j + 2] = act.astype(BF)
            put_wide(V3A, h + j + 3, act)

    def up_rows(i):
        fine = dot_nn(CO[i], WU[...])
        for a in (0, 1):
            for b in (0, 1):
                lo = (2 * a + b) * ch
                SA[a, pl.ds(b, half, stride=2), :] = (fine[:, lo : lo + ch] + b_up).astype(BF).astype(F32)
        for a in (0, 1):
            value = SA[a]
            row = 2 * i + a - 2
            put_wide(V3U, row + 2, value)
            if -1 <= row < 5:
                VJ[row + 2, :, :ch] = value.astype(BF)

    def second_pair(h):
        both = conv_pair(V3A, h + 3, KB2, h)
        for j in (0, 1):
            act, slope = silu_and_slope(both[:, j * ch : (j + 1) * ch] + b_second)
            if 0 <= h + j < 4:
                S2[h + j] = slope
            put_wide(V3B, h + j + 2, act)
            if -1 <= h + j < 5:
                VJ[h + j + 2, :, ch:] = act.astype(BF)

    def pool(i):
        SB[...] = VJ[2 * i + 2, :, ch:].astype(F32) + VJ[2 * i + 3, :, ch:].astype(F32)
        ref.POOL[i] = (
            (SB[pl.ds(0, half, stride=2), :] + SB[pl.ds(1, half, stride=2), :]) * 0.25
        ).astype(BF)

    def third_pair(h):
        both = conv_pair(V3U, h + 2, KU3, h) + conv_pair(V3B, h + 2, KB3, h)
        for j in (0, 1):
            act, slope = silu_and_slope(both[:, j * ch : (j + 1) * ch] + b_third)
            S3[h + j + 1] = slope
            put_wide(V3C, h + j + 1, act)
            VC[h + j + 2] = act.astype(BF)

    def turn(bank, back, part, lo=0):
        for row_tap in range(3):
            taps_of = bank[1 + row_tap].reshape(3, part, ch)
            for col_tap in range(3):
                back[3 - row_tap, lo : lo + part, (2 - col_tap) * ch : (3 - col_tap) * ch] = taps_of[col_tap]

    wait(in_x)
    wait(in_w1)
    wait(in_co)
    wait(in_up)
    for row in (4, 5, 6, 7):
        widen_input(row)
    first_pair(1)
    up_rows(1)
    up_rows(2)
    start_near(co_halo)
    wait(in_w2)
    wait(in_w3)
    wait(in_w4)
    turn(KB4, KT4, ch)
    turn(KU3, KT3, ch)
    turn(KB3, KT3, ch, ch)
    turn(KB2, KT2, ch)
    turn(KB1, KT1, c_in)
    wait(in_cot)
    wait(in_cp)

    receive_far(x_halo)
    receive_far(co_halo)
    for row in (8, 9, 10, 11):
        widen_input(row)
    first_pair(3)
    first_pair(5)
    up_rows(3)
    second_pair(2)
    second_pair(4)
    third_pair(3)

    receive_near(x_halo)
    receive_near(co_halo)
    for row in (0, 1, 2, 3):
        widen_input(row)
    first_pair(-1)
    first_pair(-3)
    up_rows(0)
    second_pair(0)
    second_pair(-2)
    third_pair(1)
    third_pair(-1)

    G34, G33, G32, G31 = ref.G34, ref.G33, ref.G32, ref.G31
    COT, ACT = ref.COT, ref.ACT
    sums = {}

    def add_sum(layer, value):
        part = jnp.sum(value.reshape(-1, 8, ch), axis=0)
        sums[layer] = part if layer not in sums else sums[layer] + part

    def fourth_pair(h, send):
        both = conv_pair(V3C, h + 1, KB4, h)
        pending = []
        for j in (0, 1):
            act, slope = silu_and_slope(both[:, j * ch : (j + 1) * ch] + b_fourth)
            g = (COT[h + j].astype(F32) * slope).astype(BF)
            G4[h + j + 2] = g
            ACT[h + j] = act.astype(BF)
            pending.append(g)
        send(g4_halo)
        for j in (0, 1):
            g = pending[j].astype(F32)
            add_sum(FOURTH, g)
            put_wide(G34, h + j + 2, g)

    fourth_pair(0, start_near)
    fourth_pair(2, start_far)
    out_act = [fetch(ACT.at[row], ref.activations.at[0, flip(row, 3)]) for row in range(4)]

    class Reduction:
        def __init__(self, index, name):
            self.part, self.twin = getattr(ref, "P_" + name), getattr(ref, "RA_" + name)
            self.sums, self.along = getattr(ref, "Q_" + name), getattr(ref, "RB_" + name)
            self.total, self.slots = getattr(ref, "T_" + name), getattr(ref, "RC_" + name)
            self.index, self.name = index, name

        def copy(self, phase, step, src, dst, device):
            place = self.index, 4 * phase + step
            return remote(src, dst, ref.red_send.at[place], ref.red_recv.at[place], device)

        def to_core(self):
            if fused:
                self.core = self.copy(0, 0, self.part.at[1 - k], self.twin, far_id)
                self.core.start()

        def join_core(self):
            self.core.wait_recv()
            return self.part[k].astype(F32) + self.twin[...].astype(F32)

        def scatter(self, phase, own, n, src, dst, device):
            found = []
            for step in range(1, n):
                other = lax.rem(own + step, n)
                found.append(self.copy(phase, step, src.at[other], dst.at[own], device(other)))
                found[-1].start()
            return found

        def gather(self, phase, src):
            found = []
            for step in range(1, canvas_n):
                other = lax.rem(c + step, canvas_n)
                found.append(self.copy(phase, step, src, self.slots.at[c], (other, r)))
                found[-1].start()
            self.own = fetch(src, self.slots.at[c])
            return found

        def collect(self, copies, own, n, src, dst):
            for copy in copies:
                copy.wait_recv()
            total = src[own].astype(F32)
            for step in range(1, n):
                total = total + dst[lax.rem(own + step, n)].astype(F32)
            return total

        def second(self):
            if fused:
                self.sums[...] = self.join_core().astype(BF)
                self.z_copies = self.scatter(1, z, z_n, self.sums, self.along, lambda other: (c, other * 2 + k))

        def third(self):
            if fused:
                total = self.collect(self.z_copies, z, z_n, self.sums, self.along)
                self.total[...] = total.astype(BF)
                self.last = self.gather(2, self.total)

        def fourth(self):
            pass

        def finish(self):
            if not fused:
                fetch(self.part, self.slots).wait()
                return
            self.core.wait_send()
            for copy in self.z_copies:
                copy.wait_send()
            for copy in self.last:
                copy.wait()
            self.own.wait()

    class WideReduction(Reduction):
        def second(self):
            if fused:
                total = self.join_core()
                quarter = total.shape[1] // canvas_n
                for place in range(canvas_n):
                    self.sums[place] = total[:, place * quarter : (place + 1) * quarter].astype(BF)
                self.c_copies = self.scatter(1, c, canvas_n, self.sums, self.along, lambda other: (other, r))

        def third(self):
            if fused:
                total = self.collect(self.c_copies, c, canvas_n, self.sums, self.along)
                self.zs, self.zl = getattr(ref, "ZS_" + self.name), getattr(ref, "ZL_" + self.name)
                self.zs[...] = total.astype(BF)
                self.z_copies = self.scatter(2, z, z_n, self.zs, self.zl, lambda other: (c, other * 2 + k))

        def fourth(self):
            if fused:
                total = self.collect(self.z_copies, z, z_n, self.zs, self.zl)
                self.total[...] = total.astype(BF)
                self.last = self.gather(3, self.total)

        def finish(self):
            if fused:
                for copy in self.c_copies:
                    copy.wait_send()
            super().finish()

    red = {
        name: (WideReduction if name in WIDE else Reduction)(index, name) for index, name in enumerate(GROUPS)
    }

    def put_parts(name, value, lanes):
        part = getattr(ref, "P_" + name)
        blocks = value.shape[0] // ch
        for block in range(blocks):
            first = (block if name == UP else blocks - 1 - block) * len(lanes)
            for owner in range(8):
                lo = block * ch + owner * 16
                for place, lane in enumerate(lanes):
                    part[owner % 2, owner // 2, first + place] = value[
                        lo : lo + 16, lane * 128 : (lane + 1) * 128
                    ].astype(BF)

    def above_below(h, off, closed):
        above = closed + link(h) * (h - 1 + off - closed)
        below = closed + link(h + 1) * (h + 1 + off - closed)
        return jnp.where(k == 0, above, below), jnp.where(k == 0, below, above)

    def row_stack(src, h):
        above, below = above_below(h, 2, 0)
        return jnp.concatenate([src[above], src[h + 2], src[below]], axis=1)

    def weight_grad(grad3, at, src, lo=0, n=4):
        rows = grad3[at + lo : at + lo + n].reshape(n * width, 3 * ch)
        stacked = jnp.concatenate([row_stack(src, lo + h) for h in range(n)], axis=0)
        return dot_tn(rows, stacked)

    def load_wide(dst, row, src):
        put_wide(dst, row + 2, src[row + 2].astype(F32))

    def third_back(h):
        both = back_pair(G34, h + 2, KT4, h)
        for j in (0, 1):
            g = (both[:, j * ch : (j + 1) * ch] * S3[h + j + 1]).astype(BF).astype(F32)
            if 0 <= h + j < 4:
                add_sum(THIRD, g)
            put_wide(G33, h + j + 1, g)

    put_parts(FOURTH, weight_grad(G34, 2, VC), (0, 1, 2))
    red[FOURTH].to_core()
    third_back(1)
    pool(0)
    pool(1)
    out_pool = [fetch(ref.POOL.at[i], ref.pooled.at[0, flip(i, 1)]) for i in (0, 1)]
    receive_far(g4_halo)
    load_wide(G34, 4, G4)
    load_wide(G34, 5, G4)
    third_back(3)
    ref.far_third[...] = weight_grad(G33, 1, VJ, 1, 3)
    red[FOURTH].second()
    receive_near(g4_halo)
    load_wide(G34, -1, G4)
    load_wide(G34, -2, G4)
    third_back(-1)

    GB, CP = ref.GB, ref.CP

    def joined_back(i, sends):
        spread = CP[i].astype(F32) * 0.25
        SB[pl.ds(0, half, stride=2), :] = spread
        SB[pl.ds(1, half, stride=2), :] = spread
        pending = []
        for a, send in enumerate(sends):
            row = 2 * i + a
            d_joined = back_row(G33, row + 1, KT3, row)
            g = ((d_joined[:, ch:] + SB[...]) * S2[row]).astype(BF)
            G2[row + 2] = g
            send()
            pending.append((a, row, d_joined[:, :ch], g))
        for a, row, d_up, g in pending:
            g_up = d_up.astype(BF).astype(F32)
            add_sum(UP, g_up)
            SA[a] = g_up
            for b in (0, 1):
                GB[i, a, :, b * ch : (b + 1) * ch] = SA[a, pl.ds(b, half, stride=2), :].astype(BF)
            g = g.astype(F32)
            add_sum(SECOND, g)
            put_wide(G32, row + 2, g)

    joined_back(0, (lambda: start_near(g2_halo), lambda: start_near(g2_second)))
    grad = ref.far_third[...] + weight_grad(G33, 1, VJ, 0, 1)
    put_parts(THIRD_B, grad, (1, 3, 5))
    red[THIRD_B].to_core()
    put_parts(THIRD_A, grad, (0, 2, 4))
    red[THIRD_A].to_core()
    joined_back(1, (lambda: start_far(g2_second), lambda: start_far(g2_halo)))

    def bands(i, first, second):
        return jnp.concatenate([GB[i, first], GB[i, second]], axis=1)

    red[THIRD_B].second()
    red[THIRD_A].second()
    put_parts(SECOND, weight_grad(G32, 2, VA), (0, 1, 2))
    red[SECOND].to_core()
    grad = dot_tn(
        jnp.concatenate([bands(0, k, 1 - k), bands(1, k, 1 - k)], axis=0), CO[1:3].reshape(2 * half, c_coarse)
    )
    put_parts(UP, grad, (0, 1))
    red[UP].to_core()

    def first_back(h):
        both = back_pair(G32, h + 2, KT2, h)
        for j in (0, 1):
            g = (both[:, j * ch : (j + 1) * ch] * S1[h + j + 1]).astype(BF).astype(F32)
            add_sum(FIRST, g)
            put_wide(G31, h + j + 1, g)

    def first_back_row(row):
        put_wide(G31, row + 1, (back_row(G32, row + 2, KT2, row) * S1[row + 1]).astype(BF).astype(F32))

    def first_grad(lo):
        stacks = []
        for h in (lo, lo + 1):
            above, below = above_below(h, 4, 12)
            stacks.append(jnp.concatenate([X[above], X[h + 4], X[below]], axis=0))
        rows = G31[lo + 1 : lo + 3].reshape(2 * width, 3 * ch)
        return dot_nn(jnp.concatenate(stacks, axis=1), rows)

    receive_far(g2_halo)
    receive_far(g2_second)
    load_wide(G32, 4, G2)
    load_wide(G32, 5, G2)
    first_back(2)
    ref.far_first[...] = first_grad(2)
    red[SECOND].second()
    red[FOURTH].third()
    red[UP].second()
    receive_near(g2_halo)
    load_wide(G32, -1, G2)
    first_back(0)

    grad = (ref.far_first[...] + first_grad(0)).T
    put_parts(FIRST, jnp.concatenate([grad, jnp.zeros((3 * ch, 256 - 3 * c_in), F32)], axis=1), (0, 1))
    DB = ref.DB
    DB[...] = jnp.zeros(DB.shape, F32)
    for place, layer in enumerate(ORDER):
        DB[place : place + 1] = jnp.sum(sums[layer], axis=0, keepdims=True)
    for owner in range(8):
        ref.P_first[owner % 2, owner // 2, 6] = DB[...].astype(BF)
    red[FIRST].to_core()

    GI, GC = ref.GI, ref.GC

    def input_back(h):
        both = dot_nt(back_weights(KT1, h), band(G31, h + 1)).astype(BF)
        GI[h] = both[:c_in]
        GI[h + 1] = both[c_in:]

    receive_near(g2_second)
    load_wide(G32, -2, G2)
    first_back_row(-1)
    first_back_row(4)
    red[FIRST].second()
    red[THIRD_A].third()
    input_back(0)
    input_back(2)
    out_gi = [fetch(GI.at[row], ref.grad_inputs.at[0, flip(row, 3)]) for row in range(4)]
    red[THIRD_B].third()
    red[FOURTH].fourth()
    for i in (0, 1):
        GC[i] = dot_nt(bands(i, 0, 1), WU[...]).astype(BF)
    out_gc = [fetch(GC.at[i], ref.grad_coarse.at[0, flip(i, 1)]) for i in (0, 1)]
    red[SECOND].third()
    red[UP].third()
    red[THIRD_A].fourth()
    red[THIRD_B].fourth()
    red[FIRST].third()
    red[SECOND].fourth()
    red[UP].fourth()

    for name in GROUPS:
        red[name].finish()
    for pairs in (x_halo, co_halo, g4_halo, g2_halo, g2_second):
        sent(pairs)
    for copies in (out_pool, out_act, out_gi, out_gc):
        wait(copies)


def finish_kernel(names, staged, sizes, *refs):
    ref = types.SimpleNamespace(**dict(zip(names, refs)))
    held = types.SimpleNamespace(**dict(zip(staged, refs[len(names) : -1])))
    sem = refs[-1]
    ch, share = sizes
    r = lax.axis_index("rows")
    enter, leave = {}, {}
    for place, name in enumerate(staged):
        stage = getattr(held, name)
        if name in BIG or name.startswith("RC"):
            enter[name] = pltpu.make_async_copy(getattr(ref, name), stage, sem.at[0, place])
            enter[name].start()
        if name in BIG or name.startswith("w"):
            leave[name] = pltpu.make_async_copy(stage, getattr(ref, "out_" + name), sem.at[1, place])

    def tiles(name):
        slots = getattr(held, "RC_" + name)
        if name in WIDE:
            quarter = slots.shape[1]
            return lambda t: slots[t // quarter, t % quarter].astype(F32)

        def total(t):
            value = slots[0, t].astype(F32)
            for place in range(1, slots.shape[0]):
                value = value + slots[place, t].astype(F32)
            return value

        return total

    for name in BIG:
        enter[name].wait()
        leave[name].start()
    for name in GROUPS:
        enter["RC_" + name].wait()
        tile = tiles(name)
        if name == FIRST:
            out = held.w_first
            part = out.shape[3]
            for col_tap in range(3):
                for row_tap in range(3):
                    value = tile(2 * col_tap + row_tap // 2)
                    lo = part * (row_tap % 2)
                    out[row_tap, col_tap] = value[:, lo : lo + part]
            sums = pltpu.roll(tile(6), lax.rem(ch - r * share, ch), 1)
            for place, layer in enumerate(ORDER):
                getattr(ref, "out_b_" + layer)[...] = sums[place : place + 1, :share]
        layer = name.split("_")[0]
        out = getattr(held, "w_" + layer)
        if name == UP:
            for place in range(4):
                for lane in (0, 1):
                    out[place // 2, place % 2, :, lane * 128 : (lane + 1) * 128] = tile(2 * place + lane)
        elif name != FIRST:
            lo = 128 * (name == THIRD_B)
            for col_tap in range(3):
                for row_tap in range(3):
                    out[row_tap, col_tap, :, lo : lo + 128] = tile(3 * col_tap + row_tap)
        if name != THIRD_A:
            leave["w_" + layer].start()
    for copy in leave.values():
        copy.wait()


def on_device(
    fused,
    rows_n,
    canvas_n,
    inputs,
    coarse,
    row_cuts,
    col_cuts,
    w_first,
    b_first,
    w_second,
    b_second,
    w_up,
    b_up,
    w_third,
    b_third,
    w_fourth,
    b_fourth,
    cot_out,
    cot_pool,
):
    arg = dict(
        inputs=inputs,
        coarse=coarse,
        row_cuts=row_cuts,
        col_cuts=col_cuts,
        w_first=w_first,
        b_first=b_first,
        w_second=w_second,
        b_second=b_second,
        w_up=w_up,
        b_up=b_up,
        w_third=w_third,
        b_third=b_third,
        w_fourth=w_fourth,
        b_fourth=b_fourth,
        cot_out=cot_out,
        cot_pool=cot_pool,
    )
    _, length, width, c_in = arg["inputs"].shape
    ch = arg["w_first"].shape[3]
    c_coarse = arg["coarse"].shape[3]
    half = width // 2
    assert length == 4
    arg["inputs"] = jnp.swapaxes(arg["inputs"], 2, 3)
    arg["w_first"] = arg["w_first"].reshape(3, 3 * c_in, ch)
    arg["w_second"] = arg["w_second"].reshape(3, 3 * ch, ch)
    arg["w_fourth"] = arg["w_fourth"].reshape(3, 3 * ch, ch)
    for name in ORDER:
        name = "b_" + name
        arg[name] = arg[name].reshape(1, ch)

    any_spec = pl.BlockSpec(memory_space=pl.ANY)
    vmem_spec = pl.BlockSpec(memory_space=pltpu.VMEM)
    in_specs = []
    for name in arg:
        if name == "row_cuts":
            in_specs.append(pl.BlockSpec(memory_space=pltpu.SMEM))
        elif name == "col_cuts" or name.startswith("b_"):
            in_specs.append(vmem_spec)
        else:
            in_specs.append(any_spec)

    owners, z_n = 8, 4
    share = ch // owners
    tiles = dict(fourth=9, third_a=9, third_b=9, second=9, up=8, first=7)
    tiles = {name: -(-count // 4) * 4 if name in WIDE else count for name, count in tiles.items()}
    outs = dict(
        activations=jax.ShapeDtypeStruct((1, 4, width, ch), BF),
        pooled=jax.ShapeDtypeStruct((1, 2, half, ch), BF),
        grad_inputs=jax.ShapeDtypeStruct((1, 4, c_in, width), BF),
        grad_coarse=jax.ShapeDtypeStruct((1, 2, half, c_coarse), BF),
    )
    scratch = dict(
        X=pltpu.VMEM((13, c_in, width), BF),
        CO=pltpu.VMEM((4, half, c_coarse), BF),
        COT=pltpu.VMEM((4, width, ch), BF),
        CP=pltpu.VMEM((2, half, ch), BF),
        WU=pltpu.VMEM((c_coarse, 4 * ch), BF),
        GL=pltpu.VMEM((width, ch), F32),
        GR=pltpu.VMEM((width, ch), F32),
        KB1=pltpu.VMEM((4, 3 * c_in, ch), BF),
        KB2=pltpu.VMEM((4, 3 * ch, ch), BF),
        KU3=pltpu.VMEM((4, 3, ch, ch), BF),
        KB3=pltpu.VMEM((4, 3, ch, ch), BF),
        KB4=pltpu.VMEM((4, 3 * ch, ch), BF),
        KT1=pltpu.VMEM((4, c_in, 3 * ch), BF),
        KT2=pltpu.VMEM((4, ch, 3 * ch), BF),
        KT3=pltpu.VMEM((4, 2 * ch, 3 * ch), BF),
        KT4=pltpu.VMEM((4, ch, 3 * ch), BF),
        V3X=pltpu.VMEM((12, 3 * c_in, width), BF),
        V3A=pltpu.VMEM((10, width, 3 * ch), BF),
        V3U=pltpu.VMEM((8, width, 3 * ch), BF),
        V3B=pltpu.VMEM((8, width, 3 * ch), BF),
        V3C=pltpu.VMEM((6, width, 3 * ch), BF),
        VA=pltpu.VMEM((7, width, ch), BF),
        VJ=pltpu.VMEM((7, width, 2 * ch), BF),
        VC=pltpu.VMEM((7, width, ch), BF),
        S1=pltpu.VMEM((6, width, ch), F32),
        S2=pltpu.VMEM((4, width, ch), F32),
        S3=pltpu.VMEM((6, width, ch), F32),
        G4=pltpu.VMEM((8, width, ch), BF),
        G2=pltpu.VMEM((8, width, ch), BF),
        G34=pltpu.VMEM((8, width, 3 * ch), BF),
        G33=pltpu.VMEM((6, width, 3 * ch), BF),
        G32=pltpu.VMEM((8, width, 3 * ch), BF),
        G31=pltpu.VMEM((6, width, 3 * ch), BF),
        far_third=pltpu.VMEM((3 * ch, 6 * ch), F32),
        far_first=pltpu.VMEM((3 * c_in, 3 * ch), F32),
        GB=pltpu.VMEM((2, 2, half, 2 * ch), BF),
        SA=pltpu.VMEM((2, width, ch), F32),
        SB=pltpu.VMEM((width, ch), F32),
        DB=pltpu.VMEM((16, ch), F32),
        ACT=pltpu.VMEM((4, width, ch), BF),
        POOL=pltpu.VMEM((2, half, ch), BF),
        GI=pltpu.VMEM((4, c_in, width), BF),
        GC=pltpu.VMEM((2, half, c_coarse), BF),
        local_sem=pltpu.SemaphoreType.DMA((64,)),
        halo_send=pltpu.SemaphoreType.DMA((9, 2)),
        halo_recv=pltpu.SemaphoreType.DMA((9, 2)),
        red_send=pltpu.SemaphoreType.DMA((6, 16)),
        red_recv=pltpu.SemaphoreType.DMA((6, 16)),
    )
    for name, count in tiles.items():

        def buffer(*lead):
            return pltpu.VMEM(lead + (16, 128), BF)

        landing = (canvas_n, count, 16, 128)
        scratch["P_" + name] = buffer(2, z_n, count)
        scratch["RA_" + name] = buffer(z_n, count)
        if name in WIDE:
            quarter = count // 4
            scratch["Q_" + name] = buffer(4, z_n, quarter)
            scratch["RB_" + name] = buffer(4, z_n, quarter)
            scratch["ZS_" + name] = buffer(z_n, quarter)
            scratch["ZL_" + name] = buffer(z_n, quarter)
            scratch["T_" + name] = buffer(quarter)
            landing = (4, quarter, 16, 128)
        else:
            scratch["Q_" + name] = buffer(z_n, count)
            scratch["RB_" + name] = buffer(z_n, count)
            scratch["T_" + name] = buffer(count)
        if not fused:
            landing = (2, z_n, count, 16, 128)
        outs["RC_" + name] = jax.ShapeDtypeStruct(landing, BF)

    names = list(arg) + list(outs) + list(scratch)
    sizes = (width, ch, c_in, c_coarse, rows_n, canvas_n, fused)
    results = pl.pallas_call(
        functools.partial(level_kernel, names, sizes),
        out_shape=tuple(outs.values()),
        in_specs=in_specs,
        out_specs=tuple(any_spec for _ in outs),
        scratch_shapes=list(scratch.values()),
        compiler_params=pltpu.CompilerParams(
            collective_id=0, has_side_effects=True, vmem_limit_bytes=VMEM_BYTES
        ),
        name="level",
    )(*(arg[name] for name in arg))
    held = dict(zip(outs, results))

    if not fused:
        return unfused_tail(held, rows_n, ch, c_in, c_coarse)

    done = {"out_" + name: outs[name] for name in BIG}
    parts = dict(first=c_in, second=ch, third=2 * ch, fourth=ch)
    for name in ORDER:
        shape = (2, 2, share, c_coarse) if name == UP else (3, 3, share, parts[name])
        done["out_w_" + name] = jax.ShapeDtypeStruct(shape, F32)
    for name in ORDER:
        done["out_b_" + name] = jax.ShapeDtypeStruct((1, share), F32)
    staged = {name: outs[name] for name in outs}
    staged.update({"w_" + name: done["out_w_" + name] for name in ORDER})
    finals = pl.pallas_call(
        functools.partial(finish_kernel, list(outs) + list(done), list(staged), (ch, share)),
        out_shape=tuple(done.values()),
        in_specs=[any_spec] * len(outs),
        out_specs=tuple(vmem_spec if name.startswith("out_b") else any_spec for name in done),
        scratch_shapes=[pltpu.VMEM(like.shape, like.dtype) for like in staged.values()]
        + [pltpu.SemaphoreType.DMA((2, len(staged)))],
        name="finish",
    )(*results)
    final = dict(zip(done, finals))
    return ordered(
        {name: final["out_" + name] for name in BIG},
        {name: final["out_w_" + name] for name in ORDER},
        {name: final["out_b_" + name].reshape(share) for name in ORDER},
    )


def ordered(big, weights, biases):
    turned = {name: jnp.swapaxes(value, 2, 3) for name, value in weights.items()}
    pairs = []
    for name in ORDER:
        pairs += [turned[name], biases[name]]
    return (
        big["activations"],
        big["pooled"],
        jnp.swapaxes(big["grad_inputs"], 2, 3),
        big["grad_coarse"],
        *pairs,
    )


def unfused_tail(held, rows_n, ch, c_in, c_coarse):
    share = ch // rows_n
    offset = lax.axis_index("rows") * share

    def whole(name):
        parts = held["RC_" + name].astype(F32)
        return jnp.transpose(parts, (2, 1, 0, 3, 4)).reshape(-1, ch, 128)

    tiles = lax.psum({name: whole(name) for name in GROUPS}, ("canvas", "rows"))
    weights = {}
    for name in ORDER:
        if name == UP:
            value = tiles[UP].reshape(4, 1, 2, ch, 128)
        elif name == FIRST:
            value = jnp.swapaxes(tiles[name][:6].reshape(3, 2, ch, 128), 1, 2).reshape(3, ch, 256)
            value = jnp.transpose(value[..., : 3 * c_in].reshape(3, ch, 3, c_in), (0, 2, 1, 3))[:, :, None]
        else:
            sides = (THIRD_A, THIRD_B) if name == THIRD else (name,)
            value = jnp.stack([tiles[side][:9].reshape(3, 3, ch, 128) for side in sides], axis=2)
        value = jnp.transpose(value, (1, 0, 3, 2, 4)).reshape(value.shape[1], value.shape[0], ch, -1)
        if name == UP:
            value = value.reshape(2, 2, ch, c_coarse)
        weights[name] = lax.dynamic_slice_in_dim(value, offset, share, 2)
    biases = lax.dynamic_slice_in_dim(tiles[FIRST][6], offset, share, 1)
    return ordered(held, weights, {name: biases[place] for place, name in enumerate(ORDER)})


def solution(mesh):
    rows_n, canvas_n = mesh.shape["rows"], mesh.shape["canvas"]
    fused = rows_n == 8 and canvas_n == 4
    split = P("canvas", "rows", None, None)
    pairs = (P(None, None, None, "rows"), P("rows"))
    return jax.shard_map(
        functools.partial(on_device, fused, rows_n, canvas_n),
        mesh=mesh,
        in_specs=(split, split, P("canvas", None), P("canvas", None)) + (P(),) * 10 + (split, split),
        out_specs=(split,) * 4 + pairs * 5,
        check_vma=False,
    )
```

```python
import functools
import types

import jax
import jax.numpy as jnp
from jax import lax
from jax.experimental import pallas as pl
from jax.experimental.pallas import tpu as pltpu
from jax.sharding import PartitionSpec as P

MESH = pl.DeviceIdType.MESH
BF = jnp.bfloat16
F32 = jnp.float32
VMEM_BYTES = 58 * 2**20

FIRST, SECOND, UP, THIRD, FOURTH = "first", "second", "up", "third", "fourth"
THIRD_A, THIRD_B = "third_a", "third_b"
GROUPS = (FOURTH, THIRD_A, THIRD_B, SECOND, UP, FIRST)
WIDE = (FOURTH, THIRD_A, SECOND, UP)
ORDER = (FIRST, SECOND, UP, THIRD, FOURTH)
BIG = ("activations", "pooled", "grad_inputs", "grad_coarse")


def place_of(layer, tile):
    if layer == THIRD:
        return (THIRD_A, tile) if tile < 8 else (THIRD_B, tile - 8)
    if layer == SECOND and tile == 8:
        return FIRST, 6
    return layer, tile


def dot_nn(a, b):
    return lax.dot_general(a, b, (((1,), (0,)), ((), ())), preferred_element_type=F32)


def dot_tn(a, b):
    return lax.dot_general(a, b, (((0,), (0,)), ((), ())), preferred_element_type=F32)


def dot_nt(a, b):
    return lax.dot_general(a, b, (((1,), (1,)), ((), ())), preferred_element_type=F32)


def silu_and_slope(values):
    sigma = 0.5 * jnp.tanh(0.5 * values) + 0.5
    act = values * sigma
    return act, sigma + act * (1.0 - sigma)


def level_kernel(names, sizes, *refs):
    ref = types.SimpleNamespace(**dict(zip(names, refs)))
    width, ch, c_in, c_coarse, rows_n, canvas_n, fused = sizes
    half = width // 2
    c = lax.axis_index("canvas")
    r = lax.axis_index("rows")
    z, k = r // 2, lax.rem(r, 2)
    z_n = rows_n // 2

    near_id, far_id = (c, r - 1 + 2 * k), (c, r + 1 - 2 * k)
    has_near = jnp.logical_and(near_id[1] >= 0, near_id[1] < rows_n)

    def flip(index, last):
        return index + k * (last - 2 * index)

    barrier = pltpu.get_barrier_semaphore()

    def greet(device):
        pl.semaphore_signal(barrier, inc=1, device_id=device, device_id_type=MESH)

    pl.when(has_near)(lambda: greet(near_id))
    greet(far_id)
    if fused:
        for step in range(1, z_n):
            greet((c, lax.rem(z + step, z_n) * 2 + k))
        for step in range(1, canvas_n):
            greet((lax.rem(c + step, canvas_n), r))

    used = [0]

    def fetch(src, dst):
        copy = pltpu.make_async_copy(src, dst, ref.local_sem.at[used[0]])
        used[0] += 1
        assert used[0] <= ref.local_sem.shape[0]
        copy.start()
        return copy

    def fetch_taps(weights, bank):
        return [fetch(weights.at[flip(tap, 2)], bank.at[1 + tap]) for tap in range(3)]

    def wait(copies):
        for copy in copies:
            copy.wait()

    X, CO, WU = ref.X, ref.CO, ref.WU
    KB1, KB2, KU3, KB3, KB4 = ref.KB1, ref.KB2, ref.KU3, ref.KB3, ref.KB4
    KT1, KT2, KT3, KT4 = ref.KT1, ref.KT2, ref.KT3, ref.KT4
    in_x = [fetch(ref.inputs.at[0, flip(row, 3)], X.at[4 + row]) for row in range(4)]
    in_w1 = fetch_taps(ref.w_first, KB1)

    def remote(src, dst, send, recv, device):
        return pltpu.make_async_remote_copy(
            src_ref=src, dst_ref=dst, send_sem=send, recv_sem=recv, device_id=device, device_id_type=MESH
        )

    halo_count = [0]

    def exchange(src_near, dst_near, src_far, dst_far):
        place = halo_count[0]
        halo_count[0] += 1
        near = remote(src_near, dst_near, ref.halo_send.at[place, 0], ref.halo_recv.at[place, 0], near_id)
        far = remote(src_far, dst_far, ref.halo_send.at[place, 1], ref.halo_recv.at[place, 1], far_id)
        return near, far

    def start_near(pairs):
        def start():
            for pair in pairs:
                pair[0].start()

        pl.when(has_near)(start)

    def start_far(pairs):
        for pair in pairs:
            pair[1].start()

    def receive_near(pairs):
        def receive():
            for pair in pairs:
                pair[0].wait_recv()

        pl.when(has_near)(receive)

    def receive_far(pairs):
        for pair in pairs:
            pair[1].wait_recv()

    def sent(pairs):
        def near():
            for pair in pairs:
                pair[0].wait_send()

        pl.when(has_near)(near)
        for pair in pairs:
            pair[1].wait_send()

    G4, G2 = ref.G4, ref.G2

    def row_exchange(buffer, row):
        return exchange(
            buffer.at[2 + row], buffer.at[1 - row], buffer.at[5 - row], buffer.at[6 + row]
        )

    x_halo = []
    for row in range(4):
        mine, last = ref.inputs.at[0, flip(row, 3)], ref.inputs.at[0, flip(3 - row, 3)]
        x_halo.append(exchange(mine, X.at[3 - row], last, X.at[8 + row]))
    co_halo = [exchange(ref.coarse.at[0, flip(0, 1)], CO.at[0], ref.coarse.at[0, flip(1, 1)], CO.at[3])]
    g4_halo = [row_exchange(G4, 0), row_exchange(G4, 1)]
    g2_halo, g2_second = [row_exchange(G2, 0)], [row_exchange(G2, 1)]

    in_co = [fetch(ref.coarse.at[0, flip(i, 1)], CO.at[1 + i]) for i in (0, 1)]
    in_up = [
        fetch(ref.w_up.at[flip(a, 1), b], WU.at[:, pl.ds((2 * a + b) * ch, ch)]) for a in (0, 1) for b in (0, 1)
    ]
    in_w2 = fetch_taps(ref.w_second, KB2)
    in_w3 = [
        fetch(ref.w_third.at[flip(tap, 2), :, pl.ds(lo, ch)], bank.at[1 + tap])
        for bank, lo in ((KU3, 0), (KB3, ch))
        for tap in range(3)
    ]
    in_w4 = fetch_taps(ref.w_fourth, KB4)
    in_cot = [fetch(ref.cot_out.at[0, flip(row, 3)], ref.COT.at[row]) for row in range(4)]
    in_cp = [fetch(ref.cot_pool.at[0, flip(i, 1)], ref.CP.at[i]) for i in (0, 1)]

    @pl.when(jnp.logical_not(has_near))
    def _():
        X[0:4] = jnp.zeros((4,) + X.shape[1:], BF)
        CO[0] = jnp.zeros(CO.shape[1:], BF)
        G4[0:2] = jnp.zeros((2,) + G4.shape[1:], BF)
        G2[0:2] = jnp.zeros((2,) + G2.shape[1:], BF)

    first, total_rows = r * 4, rows_n * 4

    def link(h):
        row = first + flip(h, 4)
        inside = jnp.logical_and(row > 0, row < total_rows)
        cut = ref.row_cuts[0, jnp.clip(row, 0, total_rows - 1)]
        return jnp.where(inside, 1 - cut, 0)

    open_row = 1.0 - ref.col_cuts[...].astype(F32)
    open_row = jnp.where(lax.broadcasted_iota(jnp.int32, (1, width), 1) > 0, open_row, 0.0)
    left_gate = jnp.broadcast_to(open_row, (128, width))
    right_gate = pltpu.roll(left_gate, width - 1, 1)
    GL, GR = ref.GL, ref.GR
    GL[...] = left_gate.T
    GR[...] = right_gate.T
    left_row, right_row = left_gate[:c_in], right_gate[:c_in]

    for bank in (KB1, KB2, KU3, KB3, KB4, KT1, KT2, KT3, KT4, ref.VA, ref.VJ, ref.VC):
        bank[0] = jnp.zeros(bank.shape[1:], BF)
    X[12] = jnp.zeros(X.shape[1:], BF)
    ref.P_fourth[:, :, 9:] = jnp.zeros((2, ref.P_fourth.shape[1], 3, 16, 128), BF)
    peers = (z_n - 1 + canvas_n - 1) if fused else 0
    pl.semaphore_wait(barrier, peers + 1 + has_near.astype(jnp.int32))
    start_near(x_halo)
    start_far(x_halo)
    start_far(co_halo)

    def put_wide(dst, row, value, base=0, stride=ch):
        left = (pltpu.roll(value, 1, 0) * GL[...]).astype(BF)
        right = (pltpu.roll(value, width - 1, 0) * GR[...]).astype(BF)
        for place, piece in enumerate((left, value.astype(BF), right)):
            lo = base + place * stride
            dst[row, :, lo : lo + ch] = piece

    def taps(bank, h):
        ga, gb, gc = link(h), link(h + 1), link(h + 2)
        found = bank[0], bank[ga], bank[2], bank[gb * 3], bank[gb], bank[gc * 3]
        return [tap.reshape(-1, tap.shape[-1]) for tap in found]

    def forward_weights(bank, h):
        zero, up0, mid, down0, up1, down1 = taps(bank, h)
        return jnp.concatenate(
            [
                jnp.concatenate([up0, mid, down0, zero], axis=0),
                jnp.concatenate([zero, up1, mid, down1], axis=0),
            ],
            axis=1,
        )

    def back_weights(bank, h):
        zero, up0, mid, down0, up1, down1 = taps(bank, h)
        return jnp.concatenate(
            [
                jnp.concatenate([up0, mid, down0, zero], axis=1),
                jnp.concatenate([zero, up1, mid, down1], axis=1),
            ],
            axis=0,
        )

    def band(src, at, reach=(-1, 0, 1, 2)):
        return jnp.concatenate([src[at + d] for d in reach], axis=1)

    def conv_pair(src, at, bank, h):
        return dot_nn(band(src, at), forward_weights(bank, h))

    def back_pair(src, at, bank, h):
        return dot_nt(band(src, at), back_weights(bank, h))

    def back_row(src, at, bank, h):
        weights = jnp.concatenate([bank[link(h)], bank[2], bank[link(h + 1) * 3]], axis=1)
        return dot_nt(band(src, at, (-1, 0, 1)), weights)

    def bias(layer):
        return getattr(ref, "b_" + layer)[...].astype(F32).reshape(1, ch)

    b_first, b_second, b_up, b_third, b_fourth = (bias(layer) for layer in ORDER)
    V3X, V3A, V3U, V3B, V3C = ref.V3X, ref.V3A, ref.V3U, ref.V3B, ref.V3C
    VA, VJ, VC = ref.VA, ref.VJ, ref.VC
    S1, S2, S3 = ref.S1, ref.S2, ref.S3
    SA, SB = ref.SA, ref.SB

    def widen_input(row):
        value = X[row].astype(F32)
        V3X[row, 0:c_in] = (pltpu.roll(value, 1, 1) * left_row).astype(BF)
        V3X[row, c_in : 2 * c_in] = X[row]
        V3X[row, 2 * c_in : 3 * c_in] = (pltpu.roll(value, width - 1, 1) * right_row).astype(BF)

    def first_pair(h):
        rows = V3X[h + 3 : h + 7].reshape(4 * 3 * c_in, width)
        both = dot_tn(rows, forward_weights(KB1, h))
        for j in (0, 1):
            act, slope = silu_and_slope(both[:, j * ch : (j + 1) * ch] + b_first)
            if -1 <= h + j < 5:
                S1[h + j + 1] = slope
                VA[h + j + 2] = act.astype(BF)
            put_wide(V3A, h + j + 3, act)

    def up_rows(i):
        fine = dot_nn(CO[i], WU[...])
        for a in (0, 1):
            for b in (0, 1):
                lo = (2 * a + b) * ch
                SA[a, pl.ds(b, half, stride=2), :] = (fine[:, lo : lo + ch] + b_up).astype(BF).astype(F32)
        for a in (0, 1):
            value = SA[a]
            row = 2 * i + a - 2
            put_wide(V3U, row + 2, value)
            if -1 <= row < 5:
                VJ[row + 2, :, :ch] = value.astype(BF)

    def second_pair(h):
        both = conv_pair(V3A, h + 3, KB2, h)
        for j in (0, 1):
            act, slope = silu_and_slope(both[:, j * ch : (j + 1) * ch] + b_second)
            if 0 <= h + j < 4:
                S2[h + j] = slope
            put_wide(V3B, h + j + 2, act)
            if -1 <= h + j < 5:
                VJ[h + j + 2, :, ch:] = act.astype(BF)

    def pool(i):
        SB[...] = VJ[2 * i + 2, :, ch:].astype(F32) + VJ[2 * i + 3, :, ch:].astype(F32)
        ref.POOL[i] = (
            (SB[pl.ds(0, half, stride=2), :] + SB[pl.ds(1, half, stride=2), :]) * 0.25
        ).astype(BF)

    def third_pair(h):
        both = conv_pair(V3U, h + 2, KU3, h) + conv_pair(V3B, h + 2, KB3, h)
        for j in (0, 1):
            act, slope = silu_and_slope(both[:, j * ch : (j + 1) * ch] + b_third)
            S3[h + j + 1] = slope
            put_wide(V3C, h + j + 1, act)
            VC[h + j + 2] = act.astype(BF)

    def turn(bank, back, part, lo=0):
        for row_tap in range(3):
            taps_of = bank[1 + row_tap].reshape(3, part, ch)
            for col_tap in range(3):
                back[3 - row_tap, lo : lo + part, (2 - col_tap) * ch : (3 - col_tap) * ch] = taps_of[col_tap]

    wait(in_x)
    wait(in_w1)
    wait(in_co)
    wait(in_up)
    for row in (4, 5, 6, 7):
        widen_input(row)
    first_pair(1)
    up_rows(1)
    up_rows(2)
    start_near(co_halo)
    wait(in_w2)
    wait(in_w3)
    wait(in_w4)
    turn(KB4, KT4, ch)
    turn(KU3, KT3, ch)
    turn(KB3, KT3, ch, ch)
    turn(KB2, KT2, ch)
    turn(KB1, KT1, c_in)
    wait(in_cot)
    wait(in_cp)

    receive_far(x_halo)
    receive_far(co_halo)
    for row in (8, 9, 10, 11):
        widen_input(row)
    first_pair(3)
    first_pair(5)
    up_rows(3)
    second_pair(2)
    second_pair(4)
    third_pair(3)

    receive_near(x_halo)
    receive_near(co_halo)
    for row in (0, 1, 2, 3):
        widen_input(row)
    first_pair(-1)
    first_pair(-3)
    up_rows(0)
    second_pair(0)
    second_pair(-2)
    third_pair(1)
    third_pair(-1)

    G34, G33, G32, G31 = ref.G34, ref.G33, ref.G32, ref.G31
    COT, ACT = ref.COT, ref.ACT
    sums = {}

    def add_sum(layer, value):
        part = jnp.sum(value.reshape(-1, 8, ch), axis=0)
        sums[layer] = part if layer not in sums else sums[layer] + part

    def fourth_pair(h, send):
        both = conv_pair(V3C, h + 1, KB4, h)
        pending = []
        for j in (0, 1):
            act, slope = silu_and_slope(both[:, j * ch : (j + 1) * ch] + b_fourth)
            g = (COT[h + j].astype(F32) * slope).astype(BF)
            G4[h + j + 2] = g
            ACT[h + j] = act.astype(BF)
            pending.append(g)
        send(g4_halo)
        for j in (0, 1):
            g = pending[j].astype(F32)
            add_sum(FOURTH, g)
            put_wide(G34, h + j + 2, g)

    fourth_pair(0, start_near)
    fourth_pair(2, start_far)
    out_act = [fetch(ACT.at[row], ref.activations.at[0, flip(row, 3)]) for row in range(4)]

    class Reduction:
        def __init__(self, index, name):
            self.part, self.twin = getattr(ref, "P_" + name), getattr(ref, "RA_" + name)
            self.sums, self.along = getattr(ref, "Q_" + name), getattr(ref, "RB_" + name)
            self.total, self.slots = getattr(ref, "T_" + name), getattr(ref, "RC_" + name)
            self.index, self.name = index, name

        def copy(self, phase, step, src, dst, device):
            place = self.index, 4 * phase + step
            return remote(src, dst, ref.red_send.at[place], ref.red_recv.at[place], device)

        def to_core(self):
            if fused:
                self.core = self.copy(0, 0, self.part.at[1 - k], self.twin, far_id)
                self.core.start()

        def join_core(self):
            self.core.wait_recv()
            return self.part[k].astype(F32) + self.twin[...].astype(F32)

        def scatter(self, phase, own, n, src, dst, device):
            found = []
            for step in range(1, n):
                other = lax.rem(own + step, n)
                found.append(self.copy(phase, step, src.at[other], dst.at[own], device(other)))
                found[-1].start()
            return found

        def gather(self, phase, src):
            found = []
            for step in range(1, canvas_n):
                other = lax.rem(c + step, canvas_n)
                found.append(self.copy(phase, step, src, self.slots.at[c], (other, r)))
                found[-1].start()
            self.own = fetch(src, self.slots.at[c])
            return found

        def collect(self, copies, own, n, src, dst):
            for copy in copies:
                copy.wait_recv()
            total = src[own].astype(F32)
            for step in range(1, n):
                total = total + dst[lax.rem(own + step, n)].astype(F32)
            return total

        def second(self):
            if fused:
                self.sums[...] = self.join_core().astype(BF)
                self.z_copies = self.scatter(1, z, z_n, self.sums, self.along, lambda other: (c, other * 2 + k))

        def third(self):
            if fused:
                total = self.collect(self.z_copies, z, z_n, self.sums, self.along)
                self.total[...] = total.astype(BF)
                self.last = self.gather(2, self.total)

        def fourth(self):
            pass

        def settle_first(self):
            if fused:
                self.core.wait_send()

        def settle_z(self):
            if fused:
                for copy in self.z_copies:
                    copy.wait_send()

        def finish(self):
            if not fused:
                fetch(self.part, self.slots).wait()
                return
            self.own.wait()
            for copy in self.last:
                copy.wait()

    class WideReduction(Reduction):
        def second(self):
            if fused:
                total = self.join_core()
                quarter = total.shape[1] // canvas_n
                for place in range(canvas_n):
                    self.sums[place] = total[:, place * quarter : (place + 1) * quarter].astype(BF)
                self.c_copies = self.scatter(1, c, canvas_n, self.sums, self.along, lambda other: (other, r))

        def third(self):
            if fused:
                total = self.collect(self.c_copies, c, canvas_n, self.sums, self.along)
                self.zs, self.zl = getattr(ref, "ZS_" + self.name), getattr(ref, "ZL_" + self.name)
                self.zs[...] = total.astype(BF)
                self.z_copies = self.scatter(2, z, z_n, self.zs, self.zl, lambda other: (c, other * 2 + k))

        def fourth(self):
            if fused:
                total = self.collect(self.z_copies, z, z_n, self.zs, self.zl)
                self.total[...] = total.astype(BF)
                self.last = self.gather(3, self.total)

        def settle_first(self):
            if fused:
                self.core.wait_send()
                for copy in self.c_copies:
                    copy.wait_send()

    red = {
        name: (WideReduction if name in WIDE else Reduction)(index, name) for index, name in enumerate(GROUPS)
    }

    def put_tile(group, index, value):
        part = getattr(ref, "P_" + group)
        for owner in range(8):
            part[owner % 2, owner // 2, index] = value[16 * owner : 16 * owner + 16].astype(BF)

    def put_grad(layer, value):
        blocks, lanes = value.shape[0] // ch, value.shape[1] // 128
        for block in range(blocks):
            first = (block if layer == UP else blocks - 1 - block) * lanes
            for lane in range(lanes):
                put_tile(
                    *place_of(layer, first + lane),
                    value[block * ch : (block + 1) * ch, lane * 128 : (lane + 1) * 128],
                )

    def above_below(h, off, closed):
        above = closed + link(h) * (h - 1 + off - closed)
        below = closed + link(h + 1) * (h + 1 + off - closed)
        return jnp.where(k == 0, above, below), jnp.where(k == 0, below, above)

    def row_stack(src, h):
        above, below = above_below(h, 2, 0)
        return jnp.concatenate([src[above], src[h + 2], src[below]], axis=1)

    def weight_grad(grad3, at, src, lo=0, n=4):
        rows = grad3[at + lo : at + lo + n].reshape(n * width, 3 * ch)
        stacked = jnp.concatenate([row_stack(src, lo + h) for h in range(n)], axis=0)
        return dot_tn(rows, stacked)

    def load_wide(dst, row, src):
        put_wide(dst, row + 2, src[row + 2].astype(F32))

    def third_back(h):
        both = back_pair(G34, h + 2, KT4, h)
        for j in (0, 1):
            g = (both[:, j * ch : (j + 1) * ch] * S3[h + j + 1]).astype(BF).astype(F32)
            if 0 <= h + j < 4:
                add_sum(THIRD, g)
            put_wide(G33, h + j + 1, g)

    put_grad(FOURTH, weight_grad(G34, 2, VC))
    red[FOURTH].to_core()
    third_back(1)
    pool(0)
    pool(1)
    out_pool = [fetch(ref.POOL.at[i], ref.pooled.at[0, flip(i, 1)]) for i in (0, 1)]
    receive_far(g4_halo)
    load_wide(G34, 4, G4)
    load_wide(G34, 5, G4)
    third_back(3)
    ref.far_third[...] = weight_grad(G33, 1, VJ, 1, 3)
    red[FOURTH].second()
    receive_near(g4_halo)
    load_wide(G34, -1, G4)
    load_wide(G34, -2, G4)
    third_back(-1)

    GB, CP = ref.GB, ref.CP

    def joined_back(i, sends):
        spread = CP[i].astype(F32) * 0.25
        SB[pl.ds(0, half, stride=2), :] = spread
        SB[pl.ds(1, half, stride=2), :] = spread
        pending = []
        for a, send in enumerate(sends):
            row = 2 * i + a
            d_joined = back_row(G33, row + 1, KT3, row)
            g = ((d_joined[:, ch:] + SB[...]) * S2[row]).astype(BF)
            G2[row + 2] = g
            send()
            pending.append((a, row, d_joined[:, :ch], g))
        for a, row, d_up, g in pending:
            g_up = d_up.astype(BF).astype(F32)
            add_sum(UP, g_up)
            SA[a] = g_up
            for b in (0, 1):
                GB[i, a, :, b * ch : (b + 1) * ch] = SA[a, pl.ds(b, half, stride=2), :].astype(BF)
            g = g.astype(F32)
            add_sum(SECOND, g)
            put_wide(G32, row + 2, g)

    joined_back(0, (lambda: start_near(g2_halo), lambda: start_near(g2_second)))
    put_grad(THIRD, ref.far_third[...] + weight_grad(G33, 1, VJ, 0, 1))
    red[THIRD_B].to_core()
    red[THIRD_A].to_core()
    joined_back(1, (lambda: start_far(g2_second), lambda: start_far(g2_halo)))

    def bands(i, first, second):
        return jnp.concatenate([GB[i, first], GB[i, second]], axis=1)

    red[THIRD_B].second()
    red[THIRD_A].second()
    put_grad(SECOND, weight_grad(G32, 2, VA))
    red[SECOND].to_core()
    grad = dot_tn(
        jnp.concatenate([bands(0, k, 1 - k), bands(1, k, 1 - k)], axis=0), CO[1:3].reshape(2 * half, c_coarse)
    )
    put_grad(UP, grad)
    red[UP].to_core()

    def first_back(h):
        both = back_pair(G32, h + 2, KT2, h)
        for j in (0, 1):
            g = (both[:, j * ch : (j + 1) * ch] * S1[h + j + 1]).astype(BF).astype(F32)
            add_sum(FIRST, g)
            put_wide(G31, h + j + 1, g)

    def first_back_row(row):
        put_wide(G31, row + 1, (back_row(G32, row + 2, KT2, row) * S1[row + 1]).astype(BF).astype(F32))

    def first_grad(lo):
        stacks = []
        for h in (lo, lo + 1):
            above, below = above_below(h, 4, 12)
            stacks.append(jnp.concatenate([X[above], X[h + 4], X[below]], axis=0))
        rows = G31[lo + 1 : lo + 3].reshape(2 * width, 3 * ch)
        return dot_nn(jnp.concatenate(stacks, axis=1), rows)

    receive_far(g2_halo)
    receive_far(g2_second)
    load_wide(G32, 4, G2)
    load_wide(G32, 5, G2)
    first_back(2)
    red[SECOND].second()
    ref.far_first[...] = first_grad(2)
    red[FOURTH].third()
    red[UP].second()
    receive_near(g2_halo)
    load_wide(G32, -1, G2)
    first_back(0)

    grad = (ref.far_first[...] + first_grad(0)).T
    rest = [grad[lo : lo + ch, 128:] for lo in (2 * ch, ch, 0)]
    for tap in range(3):
        put_tile(FIRST, tap, grad[(2 - tap) * ch : (3 - tap) * ch, :128])
    put_tile(FIRST, 3, jnp.concatenate(rest[:2], axis=1))
    put_tile(FIRST, 4, jnp.concatenate([rest[2], jnp.zeros(rest[2].shape, F32)], axis=1))
    DB = ref.DB
    DB[...] = jnp.zeros(DB.shape, F32)
    for place, layer in enumerate(ORDER):
        DB[place : place + 1] = jnp.sum(sums[layer], axis=0, keepdims=True)
    for owner in range(8):
        ref.P_first[owner % 2, owner // 2, 5] = DB[...].astype(BF)
    red[FIRST].to_core()

    GI, GC = ref.GI, ref.GC

    def input_back(h):
        both = dot_nt(back_weights(KT1, h), band(G31, h + 1)).astype(BF)
        GI[h] = both[:c_in]
        GI[h + 1] = both[c_in:]

    red[THIRD_A].third()
    receive_near(g2_second)
    load_wide(G32, -2, G2)
    first_back_row(-1)
    red[FIRST].second()
    first_back_row(4)
    input_back(0)
    input_back(2)
    out_gi = [fetch(GI.at[row], ref.grad_inputs.at[0, flip(row, 3)]) for row in range(4)]
    red[THIRD_B].third()
    red[FOURTH].fourth()
    red[SECOND].third()
    red[UP].third()
    for i in (0, 1):
        GC[i] = dot_nt(bands(i, 0, 1), WU[...]).astype(BF)
    out_gc = [fetch(GC.at[i], ref.grad_coarse.at[0, flip(i, 1)]) for i in (0, 1)]
    for pairs in (x_halo, co_halo, g4_halo, g2_halo, g2_second):
        sent(pairs)
    wait(out_act)
    wait(out_pool)
    for name in GROUPS:
        red[name].settle_first()
    red[THIRD_A].fourth()
    red[FOURTH].settle_z()
    red[THIRD_B].settle_z()
    red[FOURTH].finish()
    red[THIRD_B].finish()
    red[FIRST].third()
    red[SECOND].fourth()
    red[UP].fourth()
    wait(out_gi)
    wait(out_gc)
    for name in (THIRD_A, FIRST, SECOND, UP):
        red[name].settle_z()
    for name in (THIRD_A, FIRST, SECOND, UP):
        red[name].finish()


def finish_kernel(names, staged, sizes, *refs):
    ref = types.SimpleNamespace(**dict(zip(names, refs)))
    held = types.SimpleNamespace(**dict(zip(staged, refs[len(names) : -1])))
    sem = refs[-1]
    ch, share = sizes
    r = lax.axis_index("rows")
    enter, leave = {}, {}
    for place, name in enumerate(staged):
        stage = getattr(held, name)
        if name in BIG or name.startswith("RC"):
            enter[name] = pltpu.make_async_copy(getattr(ref, name), stage, sem.at[0, place])
            enter[name].start()
        if name in BIG or name.startswith("w"):
            leave[name] = pltpu.make_async_copy(stage, getattr(ref, "out_" + name), sem.at[1, place])

    def tile(group, index):
        slots = getattr(held, "RC_" + group)
        if group in WIDE:
            quarter = slots.shape[1]
            return slots[index // quarter, index % quarter].astype(F32)
        value = slots[0, index].astype(F32)
        for place in range(1, slots.shape[0]):
            value = value + slots[place, index].astype(F32)
        return value

    for name in BIG:
        enter[name].wait()
        leave[name].start()
    for name in GROUPS:
        enter["RC_" + name].wait()
    for layer in ORDER:
        out = getattr(held, "w_" + layer)
        lanes = out.shape[3] // 128
        if layer == FIRST:
            part = out.shape[3]
            for col_tap in range(3):
                whole, rest = tile(FIRST, col_tap), tile(FIRST, 3 + col_tap // 2)
                lo = part * (col_tap % 2)
                out[0, col_tap] = whole[:, :part]
                out[1, col_tap] = whole[:, part:]
                out[2, col_tap] = rest[:, lo : lo + part]
        else:
            for place in range(out.shape[0] * out.shape[1]):
                col_tap, row_tap = place // out.shape[0], place % out.shape[0]
                first, second = (col_tap, row_tap) if layer == UP else (row_tap, col_tap)
                for lane in range(lanes):
                    value = tile(*place_of(layer, place * lanes + lane))
                    out[first, second, :, lane * 128 : (lane + 1) * 128] = value
        leave["w_" + layer].start()
    sums = pltpu.roll(tile(FIRST, 5), lax.rem(ch - r * share, ch), 1)
    for place, layer in enumerate(ORDER):
        getattr(ref, "out_b_" + layer)[...] = sums[place : place + 1, :share]
    for copy in leave.values():
        copy.wait()


def on_device(
    fused,
    rows_n,
    canvas_n,
    inputs,
    coarse,
    row_cuts,
    col_cuts,
    w_first,
    b_first,
    w_second,
    b_second,
    w_up,
    b_up,
    w_third,
    b_third,
    w_fourth,
    b_fourth,
    cot_out,
    cot_pool,
):
    arg = dict(
        inputs=inputs,
        coarse=coarse,
        row_cuts=row_cuts,
        col_cuts=col_cuts,
        w_first=w_first,
        b_first=b_first,
        w_second=w_second,
        b_second=b_second,
        w_up=w_up,
        b_up=b_up,
        w_third=w_third,
        b_third=b_third,
        w_fourth=w_fourth,
        b_fourth=b_fourth,
        cot_out=cot_out,
        cot_pool=cot_pool,
    )
    _, length, width, c_in = arg["inputs"].shape
    ch = arg["w_first"].shape[3]
    c_coarse = arg["coarse"].shape[3]
    half = width // 2
    assert length == 4
    arg["inputs"] = jnp.swapaxes(arg["inputs"], 2, 3)
    arg["w_first"] = arg["w_first"].reshape(3, 3 * c_in, ch)
    arg["w_second"] = arg["w_second"].reshape(3, 3 * ch, ch)
    arg["w_fourth"] = arg["w_fourth"].reshape(3, 3 * ch, ch)
    for name in ORDER:
        name = "b_" + name
        arg[name] = arg[name].reshape(1, ch)

    any_spec = pl.BlockSpec(memory_space=pl.ANY)
    vmem_spec = pl.BlockSpec(memory_space=pltpu.VMEM)
    in_specs = []
    for name in arg:
        if name == "row_cuts":
            in_specs.append(pl.BlockSpec(memory_space=pltpu.SMEM))
        elif name == "col_cuts" or name.startswith("b_"):
            in_specs.append(vmem_spec)
        else:
            in_specs.append(any_spec)

    owners, z_n = 8, 4
    share = ch // owners
    tiles = dict(fourth=12, third_a=8, third_b=10, second=8, up=8, first=7)
    outs = dict(
        activations=jax.ShapeDtypeStruct((1, 4, width, ch), BF),
        pooled=jax.ShapeDtypeStruct((1, 2, half, ch), BF),
        grad_inputs=jax.ShapeDtypeStruct((1, 4, c_in, width), BF),
        grad_coarse=jax.ShapeDtypeStruct((1, 2, half, c_coarse), BF),
    )
    scratch = dict(
        X=pltpu.VMEM((13, c_in, width), BF),
        CO=pltpu.VMEM((4, half, c_coarse), BF),
        COT=pltpu.VMEM((4, width, ch), BF),
        CP=pltpu.VMEM((2, half, ch), BF),
        WU=pltpu.VMEM((c_coarse, 4 * ch), BF),
        GL=pltpu.VMEM((width, ch), F32),
        GR=pltpu.VMEM((width, ch), F32),
        KB1=pltpu.VMEM((4, 3 * c_in, ch), BF),
        KB2=pltpu.VMEM((4, 3 * ch, ch), BF),
        KU3=pltpu.VMEM((4, 3, ch, ch), BF),
        KB3=pltpu.VMEM((4, 3, ch, ch), BF),
        KB4=pltpu.VMEM((4, 3 * ch, ch), BF),
        KT1=pltpu.VMEM((4, c_in, 3 * ch), BF),
        KT2=pltpu.VMEM((4, ch, 3 * ch), BF),
        KT3=pltpu.VMEM((4, 2 * ch, 3 * ch), BF),
        KT4=pltpu.VMEM((4, ch, 3 * ch), BF),
        V3X=pltpu.VMEM((12, 3 * c_in, width), BF),
        V3A=pltpu.VMEM((10, width, 3 * ch), BF),
        V3U=pltpu.VMEM((8, width, 3 * ch), BF),
        V3B=pltpu.VMEM((8, width, 3 * ch), BF),
        V3C=pltpu.VMEM((6, width, 3 * ch), BF),
        VA=pltpu.VMEM((7, width, ch), BF),
        VJ=pltpu.VMEM((7, width, 2 * ch), BF),
        VC=pltpu.VMEM((7, width, ch), BF),
        S1=pltpu.VMEM((6, width, ch), F32),
        S2=pltpu.VMEM((4, width, ch), F32),
        S3=pltpu.VMEM((6, width, ch), F32),
        G4=pltpu.VMEM((8, width, ch), BF),
        G2=pltpu.VMEM((8, width, ch), BF),
        G34=pltpu.VMEM((8, width, 3 * ch), BF),
        G33=pltpu.VMEM((6, width, 3 * ch), BF),
        G32=pltpu.VMEM((8, width, 3 * ch), BF),
        G31=pltpu.VMEM((6, width, 3 * ch), BF),
        far_third=pltpu.VMEM((3 * ch, 6 * ch), F32),
        far_first=pltpu.VMEM((3 * c_in, 3 * ch), F32),
        GB=pltpu.VMEM((2, 2, half, 2 * ch), BF),
        SA=pltpu.VMEM((2, width, ch), F32),
        SB=pltpu.VMEM((width, ch), F32),
        DB=pltpu.VMEM((16, ch), F32),
        ACT=pltpu.VMEM((4, width, ch), BF),
        POOL=pltpu.VMEM((2, half, ch), BF),
        GI=pltpu.VMEM((4, c_in, width), BF),
        GC=pltpu.VMEM((2, half, c_coarse), BF),
        local_sem=pltpu.SemaphoreType.DMA((64,)),
        halo_send=pltpu.SemaphoreType.DMA((9, 2)),
        halo_recv=pltpu.SemaphoreType.DMA((9, 2)),
        red_send=pltpu.SemaphoreType.DMA((6, 16)),
        red_recv=pltpu.SemaphoreType.DMA((6, 16)),
    )
    for name, count in tiles.items():

        def buffer(*lead):
            return pltpu.VMEM(lead + (16, 128), BF)

        landing = (canvas_n, count, 16, 128)
        scratch["P_" + name] = buffer(2, z_n, count)
        scratch["RA_" + name] = buffer(z_n, count)
        if name in WIDE:
            quarter = count // 4
            scratch["Q_" + name] = buffer(4, z_n, quarter)
            scratch["RB_" + name] = buffer(4, z_n, quarter)
            scratch["ZS_" + name] = buffer(z_n, quarter)
            scratch["ZL_" + name] = buffer(z_n, quarter)
            scratch["T_" + name] = buffer(quarter)
            landing = (4, quarter, 16, 128)
        else:
            scratch["Q_" + name] = buffer(z_n, count)
            scratch["RB_" + name] = buffer(z_n, count)
            scratch["T_" + name] = buffer(count)
        if not fused:
            landing = (2, z_n, count, 16, 128)
        outs["RC_" + name] = jax.ShapeDtypeStruct(landing, BF)

    names = list(arg) + list(outs) + list(scratch)
    sizes = (width, ch, c_in, c_coarse, rows_n, canvas_n, fused)
    results = pl.pallas_call(
        functools.partial(level_kernel, names, sizes),
        out_shape=tuple(outs.values()),
        in_specs=in_specs,
        out_specs=tuple(any_spec for _ in outs),
        scratch_shapes=list(scratch.values()),
        compiler_params=pltpu.CompilerParams(
            collective_id=0, has_side_effects=True, vmem_limit_bytes=VMEM_BYTES
        ),
        name="level",
    )(*(arg[name] for name in arg))
    held = dict(zip(outs, results))

    if not fused:
        return unfused_tail(held, rows_n, ch, c_in, c_coarse)

    done = {"out_" + name: outs[name] for name in BIG}
    parts = dict(first=c_in, second=ch, third=2 * ch, fourth=ch)
    for name in ORDER:
        shape = (2, 2, share, c_coarse) if name == UP else (3, 3, share, parts[name])
        done["out_w_" + name] = jax.ShapeDtypeStruct(shape, F32)
    for name in ORDER:
        done["out_b_" + name] = jax.ShapeDtypeStruct((1, share), F32)
    staged = {name: outs[name] for name in outs}
    staged.update({"w_" + name: done["out_w_" + name] for name in ORDER})
    finals = pl.pallas_call(
        functools.partial(finish_kernel, list(outs) + list(done), list(staged), (ch, share)),
        out_shape=tuple(done.values()),
        in_specs=[any_spec] * len(outs),
        out_specs=tuple(vmem_spec if name.startswith("out_b") else any_spec for name in done),
        scratch_shapes=[pltpu.VMEM(like.shape, like.dtype) for like in staged.values()]
        + [pltpu.SemaphoreType.DMA((2, len(staged)))],
        name="finish",
    )(*results)
    final = dict(zip(done, finals))
    return ordered(
        {name: final["out_" + name] for name in BIG},
        {name: final["out_w_" + name] for name in ORDER},
        {name: final["out_b_" + name].reshape(share) for name in ORDER},
    )


def ordered(big, weights, biases):
    turned = {name: jnp.swapaxes(value, 2, 3) for name, value in weights.items()}
    pairs = []
    for name in ORDER:
        pairs += [turned[name], biases[name]]
    return (
        big["activations"],
        big["pooled"],
        jnp.swapaxes(big["grad_inputs"], 2, 3),
        big["grad_coarse"],
        *pairs,
    )


def unfused_tail(held, rows_n, ch, c_in, c_coarse):
    share = ch // rows_n
    offset = lax.axis_index("rows") * share

    def whole(name):
        parts = held["RC_" + name].astype(F32)
        return jnp.transpose(parts, (2, 1, 0, 3, 4)).reshape(-1, ch, 128)

    tiles = lax.psum({name: whole(name) for name in GROUPS}, ("canvas", "rows"))
    weights = {}
    for name in ORDER:
        if name == FIRST:
            whole_taps = tiles[FIRST][:3]
            rest = jnp.stack([tiles[FIRST][3][:, :c_in], tiles[FIRST][3][:, c_in:], tiles[FIRST][4][:, :c_in]])
            value = jnp.stack([whole_taps[..., :c_in], whole_taps[..., c_in:], rest], axis=1)[:, :, None]
        else:
            lanes, shape = (2, (4, 1)) if name == UP else (2 if name == THIRD else 1, (3, 3))
            count = lanes * shape[0] * shape[1]
            found = [place_of(name, place) for place in range(count)]
            value = jnp.stack([tiles[group][index] for group, index in found]).reshape(*shape, lanes, ch, 128)
        value = jnp.transpose(value, (1, 0, 3, 2, 4)).reshape(value.shape[1], value.shape[0], ch, -1)
        if name == UP:
            value = value.reshape(2, 2, ch, c_coarse)
        weights[name] = lax.dynamic_slice_in_dim(value, offset, share, 2)
    biases = lax.dynamic_slice_in_dim(tiles[FIRST][5], offset, share, 1)
    return ordered(held, weights, {name: biases[place] for place, name in enumerate(ORDER)})


def solution(mesh):
    rows_n, canvas_n = mesh.shape["rows"], mesh.shape["canvas"]
    fused = rows_n == 8 and canvas_n == 4
    split = P("canvas", "rows", None, None)
    pairs = (P(None, None, None, "rows"), P("rows"))
    return jax.shard_map(
        functools.partial(on_device, fused, rows_n, canvas_n),
        mesh=mesh,
        in_specs=(split, split, P("canvas", None), P("canvas", None)) + (P(),) * 10 + (split, split),
        out_specs=(split,) * 4 + pairs * 5,
        check_vma=False,
    )
```

```python
import functools
import types

import jax
import jax.numpy as jnp
from jax import lax
from jax.experimental import pallas as pl
from jax.experimental.pallas import tpu as pltpu
from jax.sharding import PartitionSpec as P

MESH = pl.DeviceIdType.MESH
BF = jnp.bfloat16
F32 = jnp.float32
VMEM_BYTES = 58 * 2**20

FIRST, SECOND, UP, THIRD, FOURTH = "first", "second", "up", "third", "fourth"
THIRD_A, THIRD_B = "third_a", "third_b"
GROUPS = (FOURTH, THIRD_A, THIRD_B, SECOND, UP, FIRST)
WIDE = (FOURTH, THIRD_A, SECOND, UP)
ORDER = (FIRST, SECOND, UP, THIRD, FOURTH)
BIG = ("activations", "pooled", "grad_inputs", "grad_coarse")


def place_of(layer, tile):
    if layer == THIRD:
        return (THIRD_A, tile) if tile < 8 else (THIRD_B, tile - 8)
    if layer == SECOND and tile == 8:
        return FIRST, 5
    return layer, tile


def dot_nn(a, b):
    return lax.dot_general(a, b, (((1,), (0,)), ((), ())), preferred_element_type=F32)


def dot_tn(a, b):
    return lax.dot_general(a, b, (((0,), (0,)), ((), ())), preferred_element_type=F32)


def dot_nt(a, b):
    return lax.dot_general(a, b, (((1,), (1,)), ((), ())), preferred_element_type=F32)


def silu_and_slope(values):
    sigma = 0.5 * jnp.tanh(0.5 * values) + 0.5
    act = values * sigma
    return act, sigma + act * (1.0 - sigma)


def level_kernel(names, sizes, *refs):
    ref = types.SimpleNamespace(**dict(zip(names, refs)))
    width, ch, c_in, c_coarse, rows_n, canvas_n, fused = sizes
    half = width // 2
    c = lax.axis_index("canvas")
    r = lax.axis_index("rows")
    z, k = r // 2, lax.rem(r, 2)
    z_n = rows_n // 2

    near_id, far_id = (c, r - 1 + 2 * k), (c, r + 1 - 2 * k)
    has_near = jnp.logical_and(near_id[1] >= 0, near_id[1] < rows_n)

    def flip(index, last):
        return index + k * (last - 2 * index)

    barrier = pltpu.get_barrier_semaphore()

    def greet(device):
        pl.semaphore_signal(barrier, inc=1, device_id=device, device_id_type=MESH)

    pl.when(has_near)(lambda: greet(near_id))
    greet(far_id)
    if fused:
        for step in range(1, z_n):
            greet((c, lax.rem(z + step, z_n) * 2 + k))
        for step in range(1, canvas_n):
            greet((lax.rem(c + step, canvas_n), r))

    used = [0]

    def fetch(src, dst):
        copy = pltpu.make_async_copy(src, dst, ref.local_sem.at[used[0]])
        used[0] += 1
        assert used[0] <= ref.local_sem.shape[0]
        copy.start()
        return copy

    def fetch_taps(weights, bank):
        return [fetch(weights.at[flip(tap, 2)], bank.at[1 + tap]) for tap in range(3)]

    def wait(copies):
        for copy in copies:
            copy.wait()

    X, CO, WU = ref.X, ref.CO, ref.WU
    KB1, KB2, KU3, KB3, KB4 = ref.KB1, ref.KB2, ref.KU3, ref.KB3, ref.KB4
    KT1, KT2, KT3, KT4 = ref.KT1, ref.KT2, ref.KT3, ref.KT4
    in_x = [fetch(ref.inputs.at[0, flip(row, 3)], X.at[4 + row]) for row in range(4)]
    in_w1 = fetch_taps(ref.w_first, KB1)

    def remote(src, dst, send, recv, device):
        return pltpu.make_async_remote_copy(
            src_ref=src, dst_ref=dst, send_sem=send, recv_sem=recv, device_id=device, device_id_type=MESH
        )

    halo_count = [0]

    def exchange(src_near, dst_near, src_far, dst_far):
        place = halo_count[0]
        halo_count[0] += 1
        near = remote(src_near, dst_near, ref.halo_send.at[place, 0], ref.halo_recv.at[place, 0], near_id)
        far = remote(src_far, dst_far, ref.halo_send.at[place, 1], ref.halo_recv.at[place, 1], far_id)
        return near, far

    def start_near(pairs):
        def start():
            for pair in pairs:
                pair[0].start()

        pl.when(has_near)(start)

    def start_far(pairs):
        for pair in pairs:
            pair[1].start()

    def receive_near(pairs):
        def receive():
            for pair in pairs:
                pair[0].wait_recv()

        pl.when(has_near)(receive)

    def receive_far(pairs):
        for pair in pairs:
            pair[1].wait_recv()

    def sent(pairs):
        def near():
            for pair in pairs:
                pair[0].wait_send()

        pl.when(has_near)(near)
        for pair in pairs:
            pair[1].wait_send()

    G4, G2 = ref.G4, ref.G2

    def row_exchange(buffer, row):
        return exchange(
            buffer.at[2 + row], buffer.at[1 - row], buffer.at[5 - row], buffer.at[6 + row]
        )

    x_halo = []
    for row in range(4):
        mine, last = ref.inputs.at[0, flip(row, 3)], ref.inputs.at[0, flip(3 - row, 3)]
        x_halo.append(exchange(mine, X.at[3 - row], last, X.at[8 + row]))
    co_halo = [exchange(ref.coarse.at[0, flip(0, 1)], CO.at[0], ref.coarse.at[0, flip(1, 1)], CO.at[3])]
    g4_halo = [row_exchange(G4, 0), row_exchange(G4, 1)]
    g2_halo, g2_second = [row_exchange(G2, 0)], [row_exchange(G2, 1)]

    in_co = [fetch(ref.coarse.at[0, flip(i, 1)], CO.at[1 + i]) for i in (0, 1)]
    in_up = [
        fetch(ref.w_up.at[flip(a, 1), b], WU.at[:, pl.ds((2 * a + b) * ch, ch)]) for a in (0, 1) for b in (0, 1)
    ]
    in_w2 = fetch_taps(ref.w_second, KB2)
    in_w3 = [
        fetch(ref.w_third.at[flip(tap, 2), :, pl.ds(lo, ch)], bank.at[1 + tap])
        for bank, lo in ((KU3, 0), (KB3, ch))
        for tap in range(3)
    ]
    in_w4 = fetch_taps(ref.w_fourth, KB4)
    in_cot = [fetch(ref.cot_out.at[0, flip(row, 3)], ref.COT.at[row]) for row in range(4)]
    in_cp = [fetch(ref.cot_pool.at[0, flip(i, 1)], ref.CP.at[i]) for i in (0, 1)]

    @pl.when(jnp.logical_not(has_near))
    def _():
        X[0:4] = jnp.zeros((4,) + X.shape[1:], BF)
        CO[0] = jnp.zeros(CO.shape[1:], BF)
        G4[0:2] = jnp.zeros((2,) + G4.shape[1:], BF)
        G2[0:2] = jnp.zeros((2,) + G2.shape[1:], BF)

    first, total_rows = r * 4, rows_n * 4

    def link(h):
        row = first + flip(h, 4)
        inside = jnp.logical_and(row > 0, row < total_rows)
        cut = ref.row_cuts[0, jnp.clip(row, 0, total_rows - 1)]
        return jnp.where(inside, 1 - cut, 0)

    open_row = 1.0 - ref.col_cuts[...].astype(F32)
    open_row = jnp.where(lax.broadcasted_iota(jnp.int32, (1, width), 1) > 0, open_row, 0.0)
    left_gate = jnp.broadcast_to(open_row, (128, width))
    right_gate = pltpu.roll(left_gate, width - 1, 1)
    GL, GR = ref.GL, ref.GR
    GL[...] = left_gate.T
    GR[...] = right_gate.T
    left_row, right_row = left_gate[:c_in], right_gate[:c_in]

    for bank in (KB1, KB2, KU3, KB3, KB4, KT1, KT2, KT3, KT4, ref.VA, ref.VJ, ref.VC):
        bank[0] = jnp.zeros(bank.shape[1:], BF)
    X[12] = jnp.zeros(X.shape[1:], BF)
    ref.P_fourth[:, :, 9:] = jnp.zeros((2, ref.P_fourth.shape[1], 3, 16, 128), BF)
    peers = (z_n - 1 + canvas_n - 1) if fused else 0
    pl.semaphore_wait(barrier, peers + 1 + has_near.astype(jnp.int32))
    start_near(x_halo)
    start_far(x_halo)
    start_far(co_halo)

    def put_wide(dst, row, value, base=0, stride=ch):
        left = (pltpu.roll(value, 1, 0) * GL[...]).astype(BF)
        right = (pltpu.roll(value, width - 1, 0) * GR[...]).astype(BF)
        for place, piece in enumerate((left, value.astype(BF), right)):
            lo = base + place * stride
            dst[row, :, lo : lo + ch] = piece

    def taps(bank, h):
        ga, gb, gc = link(h), link(h + 1), link(h + 2)
        found = bank[0], bank[ga], bank[2], bank[gb * 3], bank[gb], bank[gc * 3]
        return [tap.reshape(-1, tap.shape[-1]) for tap in found]

    def forward_weights(bank, h):
        zero, up0, mid, down0, up1, down1 = taps(bank, h)
        return jnp.concatenate(
            [
                jnp.concatenate([up0, mid, down0, zero], axis=0),
                jnp.concatenate([zero, up1, mid, down1], axis=0),
            ],
            axis=1,
        )

    def back_weights(bank, h):
        zero, up0, mid, down0, up1, down1 = taps(bank, h)
        return jnp.concatenate(
            [
                jnp.concatenate([up0, mid, down0, zero], axis=1),
                jnp.concatenate([zero, up1, mid, down1], axis=1),
            ],
            axis=0,
        )

    def band(src, at, reach=(-1, 0, 1, 2)):
        return jnp.concatenate([src[at + d] for d in reach], axis=1)

    def conv_pair(src, at, bank, h):
        return dot_nn(band(src, at), forward_weights(bank, h))

    def back_pair(src, at, bank, h):
        return dot_nt(band(src, at), back_weights(bank, h))

    def back_row(src, at, bank, h):
        weights = jnp.concatenate([bank[link(h)], bank[2], bank[link(h + 1) * 3]], axis=1)
        return dot_nt(band(src, at, (-1, 0, 1)), weights)

    def bias(layer):
        return getattr(ref, "b_" + layer)[...].astype(F32).reshape(1, ch)

    b_first, b_second, b_up, b_third, b_fourth = (bias(layer) for layer in ORDER)
    V3X, V3A, V3U, V3B, V3C = ref.V3X, ref.V3A, ref.V3U, ref.V3B, ref.V3C
    VA, VJ, VC = ref.VA, ref.VJ, ref.VC
    S1, S2, S3 = ref.S1, ref.S2, ref.S3
    SA, SB = ref.SA, ref.SB

    def widen_input(row):
        value = X[row].astype(F32)
        V3X[row, 0:c_in] = (pltpu.roll(value, 1, 1) * left_row).astype(BF)
        V3X[row, c_in : 2 * c_in] = X[row]
        V3X[row, 2 * c_in : 3 * c_in] = (pltpu.roll(value, width - 1, 1) * right_row).astype(BF)

    def first_pair(h):
        rows = V3X[h + 3 : h + 7].reshape(4 * 3 * c_in, width)
        both = dot_tn(rows, forward_weights(KB1, h))
        for j in (0, 1):
            act, slope = silu_and_slope(both[:, j * ch : (j + 1) * ch] + b_first)
            if -1 <= h + j < 5:
                S1[h + j + 1] = slope
                VA[h + j + 2] = act.astype(BF)
            put_wide(V3A, h + j + 3, act)

    def up_rows(i):
        fine = dot_nn(CO[i], WU[...])
        for a in (0, 1):
            for b in (0, 1):
                lo = (2 * a + b) * ch
                SA[a, pl.ds(b, half, stride=2), :] = (fine[:, lo : lo + ch] + b_up).astype(BF).astype(F32)
        for a in (0, 1):
            value = SA[a]
            row = 2 * i + a - 2
            put_wide(V3U, row + 2, value)
            if -1 <= row < 5:
                VJ[row + 2, :, :ch] = value.astype(BF)

    def second_pair(h):
        both = conv_pair(V3A, h + 3, KB2, h)
        for j in (0, 1):
            act, slope = silu_and_slope(both[:, j * ch : (j + 1) * ch] + b_second)
            if 0 <= h + j < 4:
                S2[h + j] = slope
            put_wide(V3B, h + j + 2, act)
            if -1 <= h + j < 5:
                VJ[h + j + 2, :, ch:] = act.astype(BF)

    def pool(i):
        SB[...] = VJ[2 * i + 2, :, ch:].astype(F32) + VJ[2 * i + 3, :, ch:].astype(F32)
        ref.POOL[i] = (
            (SB[pl.ds(0, half, stride=2), :] + SB[pl.ds(1, half, stride=2), :]) * 0.25
        ).astype(BF)

    def third_pair(h):
        both = conv_pair(V3U, h + 2, KU3, h) + conv_pair(V3B, h + 2, KB3, h)
        for j in (0, 1):
            act, slope = silu_and_slope(both[:, j * ch : (j + 1) * ch] + b_third)
            S3[h + j + 1] = slope
            put_wide(V3C, h + j + 1, act)
            VC[h + j + 2] = act.astype(BF)

    def turn(bank, back, part, lo=0):
        for row_tap in range(3):
            taps_of = bank[1 + row_tap].reshape(3, part, ch)
            for col_tap in range(3):
                back[3 - row_tap, lo : lo + part, (2 - col_tap) * ch : (3 - col_tap) * ch] = taps_of[col_tap]

    wait(in_x)
    wait(in_w1)
    wait(in_co)
    wait(in_up)
    for row in (4, 5, 6, 7):
        widen_input(row)
    first_pair(1)
    up_rows(1)
    up_rows(2)
    start_near(co_halo)
    wait(in_w2)
    wait(in_w3)
    wait(in_w4)
    turn(KB4, KT4, ch)
    turn(KU3, KT3, ch)
    turn(KB3, KT3, ch, ch)
    turn(KB2, KT2, ch)
    turn(KB1, KT1, c_in)
    wait(in_cot)
    wait(in_cp)

    receive_far(x_halo)
    receive_far(co_halo)
    for row in (8, 9, 10, 11):
        widen_input(row)
    first_pair(3)
    first_pair(5)
    up_rows(3)
    second_pair(2)
    second_pair(4)
    third_pair(3)

    receive_near(x_halo)
    receive_near(co_halo)
    for row in (0, 1, 2, 3):
        widen_input(row)
    first_pair(-1)
    first_pair(-3)
    up_rows(0)
    second_pair(0)
    second_pair(-2)
    third_pair(1)
    third_pair(-1)

    G34, G33, G32, G31 = ref.G34, ref.G33, ref.G32, ref.G31
    COT, ACT = ref.COT, ref.ACT
    sums = {}

    def add_sum(layer, value):
        part = jnp.sum(value.reshape(-1, 8, ch), axis=0)
        sums[layer] = part if layer not in sums else sums[layer] + part

    def fourth_pair(h, send):
        both = conv_pair(V3C, h + 1, KB4, h)
        pending = []
        for j in (0, 1):
            act, slope = silu_and_slope(both[:, j * ch : (j + 1) * ch] + b_fourth)
            g = (COT[h + j].astype(F32) * slope).astype(BF)
            G4[h + j + 2] = g
            ACT[h + j] = act.astype(BF)
            pending.append(g)
        send(g4_halo)
        for j in (0, 1):
            g = pending[j].astype(F32)
            add_sum(FOURTH, g)
            put_wide(G34, h + j + 2, g)

    fourth_pair(0, start_near)
    fourth_pair(2, start_far)
    out_act = [fetch(ACT.at[row], ref.activations.at[0, flip(row, 3)]) for row in range(4)]

    class Reduction:
        def __init__(self, index, name):
            self.part, self.twin = getattr(ref, "P_" + name), getattr(ref, "RA_" + name)
            self.sums, self.along = getattr(ref, "Q_" + name), getattr(ref, "RB_" + name)
            self.total, self.slots = getattr(ref, "T_" + name), getattr(ref, "RC_" + name)
            self.index, self.name = index, name

        def copy(self, phase, step, src, dst, device):
            place = self.index, 4 * phase + step
            return remote(src, dst, ref.red_send.at[place], ref.red_recv.at[place], device)

        def to_core(self):
            if fused:
                self.core = self.copy(0, 0, self.part.at[1 - k], self.twin, far_id)
                self.core.start()

        def join_core(self):
            self.core.wait_recv()
            return self.part[k].astype(F32) + self.twin[...].astype(F32)

        def scatter(self, phase, own, n, src, dst, device):
            found = []
            for step in range(1, n):
                other = lax.rem(own + step, n)
                found.append(self.copy(phase, step, src.at[other], dst.at[own], device(other)))
                found[-1].start()
            return found

        def gather(self, phase, src):
            found = []
            for step in range(1, canvas_n):
                other = lax.rem(c + step, canvas_n)
                found.append(self.copy(phase, step, src, self.slots.at[c], (other, r)))
                found[-1].start()
            self.own = fetch(src, self.slots.at[c])
            return found

        def collect(self, copies, own, n, src, dst):
            for copy in copies:
                copy.wait_recv()
            total = src[own].astype(F32)
            for step in range(1, n):
                total = total + dst[lax.rem(own + step, n)].astype(F32)
            return total

        def second(self):
            if fused:
                self.sums[...] = self.join_core().astype(BF)
                self.z_copies = self.scatter(1, z, z_n, self.sums, self.along, lambda other: (c, other * 2 + k))

        def third(self):
            if fused:
                total = self.collect(self.z_copies, z, z_n, self.sums, self.along)
                self.total[...] = total.astype(BF)
                self.last = self.gather(2, self.total)

        def fourth(self):
            pass

        def settle_first(self):
            if fused:
                self.core.wait_send()

        def settle_z(self):
            if fused:
                for copy in self.z_copies:
                    copy.wait_send()

        def finish(self):
            if not fused:
                fetch(self.part, self.slots).wait()
                return
            self.own.wait()
            for copy in self.last:
                copy.wait()

    class WideReduction(Reduction):
        def second(self):
            if fused:
                total = self.join_core()
                quarter = total.shape[1] // canvas_n
                for place in range(canvas_n):
                    self.sums[place] = total[:, place * quarter : (place + 1) * quarter].astype(BF)
                self.c_copies = self.scatter(1, c, canvas_n, self.sums, self.along, lambda other: (other, r))

        def third(self):
            if fused:
                total = self.collect(self.c_copies, c, canvas_n, self.sums, self.along)
                self.zs, self.zl = getattr(ref, "ZS_" + self.name), getattr(ref, "ZL_" + self.name)
                self.zs[...] = total.astype(BF)
                self.z_copies = self.scatter(2, z, z_n, self.zs, self.zl, lambda other: (c, other * 2 + k))

        def fourth(self):
            if fused:
                total = self.collect(self.z_copies, z, z_n, self.zs, self.zl)
                self.total[...] = total.astype(BF)
                self.last = self.gather(3, self.total)

        def settle_first(self):
            if fused:
                self.core.wait_send()
                for copy in self.c_copies:
                    copy.wait_send()

    red = {
        name: (WideReduction if name in WIDE else Reduction)(index, name) for index, name in enumerate(GROUPS)
    }

    def put_tile(group, index, value):
        part = getattr(ref, "P_" + group)
        for owner in range(8):
            part[owner % 2, owner // 2, index] = value[16 * owner : 16 * owner + 16].astype(BF)

    def put_grad(layer, value):
        blocks, lanes = value.shape[0] // ch, value.shape[1] // 128
        for block in range(blocks):
            first = (block if layer == UP else blocks - 1 - block) * lanes
            for lane in range(lanes):
                put_tile(
                    *place_of(layer, first + lane),
                    value[block * ch : (block + 1) * ch, lane * 128 : (lane + 1) * 128],
                )

    def above_below(h, off, closed):
        above = closed + link(h) * (h - 1 + off - closed)
        below = closed + link(h + 1) * (h + 1 + off - closed)
        return jnp.where(k == 0, above, below), jnp.where(k == 0, below, above)

    def row_stack(src, h):
        above, below = above_below(h, 2, 0)
        return jnp.concatenate([src[above], src[h + 2], src[below]], axis=1)

    def weight_grad(grad3, at, src, lo=0, n=4):
        rows = grad3[at + lo : at + lo + n].reshape(n * width, 3 * ch)
        stacked = jnp.concatenate([row_stack(src, lo + h) for h in range(n)], axis=0)
        return dot_tn(rows, stacked)

    def load_wide(dst, row, src):
        put_wide(dst, row + 2, src[row + 2].astype(F32))

    def third_back(h):
        both = back_pair(G34, h + 2, KT4, h)
        for j in (0, 1):
            g = (both[:, j * ch : (j + 1) * ch] * S3[h + j + 1]).astype(BF).astype(F32)
            if 0 <= h + j < 4:
                add_sum(THIRD, g)
            put_wide(G33, h + j + 1, g)

    put_grad(FOURTH, weight_grad(G34, 2, VC))
    red[FOURTH].to_core()
    third_back(1)
    pool(0)
    pool(1)
    out_pool = [fetch(ref.POOL.at[i], ref.pooled.at[0, flip(i, 1)]) for i in (0, 1)]
    receive_far(g4_halo)
    load_wide(G34, 4, G4)
    load_wide(G34, 5, G4)
    third_back(3)
    ref.far_third[...] = weight_grad(G33, 1, VJ, 1, 3)
    red[FOURTH].second()
    receive_near(g4_halo)
    load_wide(G34, -1, G4)
    load_wide(G34, -2, G4)
    third_back(-1)

    GB, CP = ref.GB, ref.CP

    def joined_back(i, sends):
        spread = CP[i].astype(F32) * 0.25
        SB[pl.ds(0, half, stride=2), :] = spread
        SB[pl.ds(1, half, stride=2), :] = spread
        pending = []
        for a, send in enumerate(sends):
            row = 2 * i + a
            d_joined = back_row(G33, row + 1, KT3, row)
            g = ((d_joined[:, ch:] + SB[...]) * S2[row]).astype(BF)
            G2[row + 2] = g
            send()
            pending.append((a, row, d_joined[:, :ch], g))
        for a, row, d_up, g in pending:
            g_up = d_up.astype(BF).astype(F32)
            add_sum(UP, g_up)
            SA[a] = g_up
            for b in (0, 1):
                GB[i, a, :, b * ch : (b + 1) * ch] = SA[a, pl.ds(b, half, stride=2), :].astype(BF)
            g = g.astype(F32)
            add_sum(SECOND, g)
            put_wide(G32, row + 2, g)

    joined_back(0, (lambda: start_near(g2_halo), lambda: start_near(g2_second)))
    put_grad(THIRD, ref.far_third[...] + weight_grad(G33, 1, VJ, 0, 1))
    red[THIRD_B].to_core()
    red[THIRD_A].to_core()
    joined_back(1, (lambda: start_far(g2_second), lambda: start_far(g2_halo)))

    def bands(i, first, second):
        return jnp.concatenate([GB[i, first], GB[i, second]], axis=1)

    red[THIRD_B].second()
    red[THIRD_A].second()
    put_grad(SECOND, weight_grad(G32, 2, VA))
    red[SECOND].to_core()
    grad = dot_tn(
        jnp.concatenate([bands(0, k, 1 - k), bands(1, k, 1 - k)], axis=0), CO[1:3].reshape(2 * half, c_coarse)
    )
    put_grad(UP, grad)
    red[UP].to_core()

    def first_back(h):
        both = back_pair(G32, h + 2, KT2, h)
        for j in (0, 1):
            g = (both[:, j * ch : (j + 1) * ch] * S1[h + j + 1]).astype(BF).astype(F32)
            add_sum(FIRST, g)
            put_wide(G31, h + j + 1, g)

    def first_back_row(row):
        put_wide(G31, row + 1, (back_row(G32, row + 2, KT2, row) * S1[row + 1]).astype(BF).astype(F32))

    def first_grad(lo):
        stacks = []
        for h in (lo, lo + 1):
            above, below = above_below(h, 4, 12)
            stacks.append(jnp.concatenate([X[above], X[h + 4], X[below]], axis=0))
        rows = G31[lo + 1 : lo + 3].reshape(2 * width, 3 * ch)
        return dot_nn(jnp.concatenate(stacks, axis=1), rows)

    red[FOURTH].third()
    receive_far(g2_halo)
    receive_far(g2_second)
    load_wide(G32, 4, G2)
    load_wide(G32, 5, G2)
    first_back(2)
    red[SECOND].second()
    ref.far_first[...] = first_grad(2)
    red[UP].second()
    receive_near(g2_halo)
    load_wide(G32, -1, G2)
    first_back(0)

    grad = (ref.far_first[...] + first_grad(0)).T
    rest = [grad[lo : lo + ch, 128:] for lo in (2 * ch, ch, 0)]
    for tap in range(3):
        put_tile(FIRST, tap, grad[(2 - tap) * ch : (3 - tap) * ch, :128])
    put_tile(FIRST, 3, jnp.concatenate(rest[:2], axis=1))
    DB = ref.DB
    DB[...] = jnp.zeros(DB.shape, F32)
    for place, layer in enumerate(ORDER):
        total = jnp.sum(sums[layer], axis=0, keepdims=True)
        DB[place : place + 1] = total[:, : ch // 2]
        DB[5 + place : 6 + place] = total[:, ch // 2 :]
    spare = jnp.concatenate([DB[...]] * 8, axis=0)
    put_tile(FIRST, 4, jnp.concatenate([rest[2], spare], axis=1))
    red[FIRST].to_core()

    GI, GC = ref.GI, ref.GC

    def input_back(h):
        both = dot_nt(back_weights(KT1, h), band(G31, h + 1)).astype(BF)
        GI[h] = both[:c_in]
        GI[h + 1] = both[c_in:]

    red[THIRD_A].third()
    receive_near(g2_second)
    load_wide(G32, -2, G2)
    first_back_row(-1)
    red[FIRST].second()
    first_back_row(4)
    input_back(0)
    input_back(2)
    out_gi = [fetch(GI.at[row], ref.grad_inputs.at[0, flip(row, 3)]) for row in range(4)]
    red[THIRD_B].third()
    red[FOURTH].fourth()
    red[SECOND].third()
    red[UP].third()
    for i in (0, 1):
        GC[i] = dot_nt(bands(i, 0, 1), WU[...]).astype(BF)
    out_gc = [fetch(GC.at[i], ref.grad_coarse.at[0, flip(i, 1)]) for i in (0, 1)]
    for pairs in (x_halo, co_halo, g4_halo, g2_halo, g2_second):
        sent(pairs)
    wait(out_act)
    wait(out_pool)
    for name in GROUPS:
        red[name].settle_first()
    red[THIRD_A].fourth()
    red[FOURTH].settle_z()
    red[THIRD_B].settle_z()
    red[FOURTH].finish()
    red[THIRD_B].finish()
    red[FIRST].third()
    red[SECOND].fourth()
    red[UP].fourth()
    wait(out_gi)
    wait(out_gc)
    for name in (THIRD_A, FIRST, SECOND, UP):
        red[name].settle_z()
    for name in (THIRD_A, FIRST, SECOND, UP):
        red[name].finish()


def finish_kernel(names, staged, sizes, *refs):
    ref = types.SimpleNamespace(**dict(zip(names, refs)))
    held = types.SimpleNamespace(**dict(zip(staged, refs[len(names) : -1])))
    sem = refs[-1]
    ch, share = sizes
    r = lax.axis_index("rows")
    enter, leave = {}, {}
    for place, name in enumerate(staged):
        stage = getattr(held, name)
        if name in BIG or name.startswith("RC"):
            enter[name] = pltpu.make_async_copy(getattr(ref, name), stage, sem.at[0, place])
            enter[name].start()
        if not name.startswith("RC"):
            leave[name] = pltpu.make_async_copy(stage, getattr(ref, "out_" + name), sem.at[1, place])

    def tile(group, index):
        slots = getattr(held, "RC_" + group)
        if group in WIDE:
            quarter = slots.shape[1]
            return slots[index // quarter, index % quarter].astype(F32)
        value = slots[0, index].astype(F32)
        for place in range(1, slots.shape[0]):
            value = value + slots[place, index].astype(F32)
        return value

    for name in BIG:
        enter[name].wait()
        leave[name].start()
    for name in GROUPS:
        enter["RC_" + name].wait()
    for layer in ORDER:
        out = getattr(held, "w_" + layer)
        lanes = out.shape[3] // 128
        if layer == FIRST:
            part = out.shape[3]
            for col_tap in range(3):
                whole, rest = tile(FIRST, col_tap), tile(FIRST, 3 + col_tap // 2)
                lo = part * (col_tap % 2)
                out[0, col_tap] = whole[:, :part]
                out[1, col_tap] = whole[:, part:]
                out[2, col_tap] = rest[:, lo : lo + part]
        else:
            for place in range(out.shape[0] * out.shape[1]):
                col_tap, row_tap = place // out.shape[0], place % out.shape[0]
                first, second = (col_tap, row_tap) if layer == UP else (row_tap, col_tap)
                for lane in range(lanes):
                    value = tile(*place_of(layer, place * lanes + lane))
                    out[first, second, :, lane * 128 : (lane + 1) * 128] = value
        leave["w_" + layer].start()
    spare = tile(FIRST, 4)[:, ch // 2 :]
    sums = jnp.concatenate([spare[0:8], spare[5:13]], axis=1)
    sums = pltpu.roll(sums, lax.rem(ch - r * share, ch), 1)
    for place, layer in enumerate(ORDER):
        getattr(held, "b_" + layer)[...] = sums[place : place + 1, :share]
        leave["b_" + layer].start()
    for copy in leave.values():
        copy.wait()


def on_device(
    fused,
    rows_n,
    canvas_n,
    inputs,
    coarse,
    row_cuts,
    col_cuts,
    w_first,
    b_first,
    w_second,
    b_second,
    w_up,
    b_up,
    w_third,
    b_third,
    w_fourth,
    b_fourth,
    cot_out,
    cot_pool,
):
    arg = dict(
        inputs=inputs,
        coarse=coarse,
        row_cuts=row_cuts,
        col_cuts=col_cuts,
        w_first=w_first,
        b_first=b_first,
        w_second=w_second,
        b_second=b_second,
        w_up=w_up,
        b_up=b_up,
        w_third=w_third,
        b_third=b_third,
        w_fourth=w_fourth,
        b_fourth=b_fourth,
        cot_out=cot_out,
        cot_pool=cot_pool,
    )
    _, length, width, c_in = arg["inputs"].shape
    ch = arg["w_first"].shape[3]
    c_coarse = arg["coarse"].shape[3]
    half = width // 2
    assert length == 4
    arg["inputs"] = jnp.swapaxes(arg["inputs"], 2, 3)
    arg["w_first"] = arg["w_first"].reshape(3, 3 * c_in, ch)
    arg["w_second"] = arg["w_second"].reshape(3, 3 * ch, ch)
    arg["w_fourth"] = arg["w_fourth"].reshape(3, 3 * ch, ch)
    for name in ORDER:
        name = "b_" + name
        arg[name] = arg[name].reshape(1, ch)

    any_spec = pl.BlockSpec(memory_space=pl.ANY)
    vmem_spec = pl.BlockSpec(memory_space=pltpu.VMEM)
    in_specs = []
    for name in arg:
        if name == "row_cuts":
            in_specs.append(pl.BlockSpec(memory_space=pltpu.SMEM))
        elif name == "col_cuts" or name.startswith("b_"):
            in_specs.append(vmem_spec)
        else:
            in_specs.append(any_spec)

    owners, z_n = 8, 4
    share = ch // owners
    tiles = dict(fourth=12, third_a=8, third_b=10, second=8, up=8, first=6)
    outs = dict(
        activations=jax.ShapeDtypeStruct((1, 4, width, ch), BF),
        pooled=jax.ShapeDtypeStruct((1, 2, half, ch), BF),
        grad_inputs=jax.ShapeDtypeStruct((1, 4, c_in, width), BF),
        grad_coarse=jax.ShapeDtypeStruct((1, 2, half, c_coarse), BF),
    )
    scratch = dict(
        X=pltpu.VMEM((13, c_in, width), BF),
        CO=pltpu.VMEM((4, half, c_coarse), BF),
        COT=pltpu.VMEM((4, width, ch), BF),
        CP=pltpu.VMEM((2, half, ch), BF),
        WU=pltpu.VMEM((c_coarse, 4 * ch), BF),
        GL=pltpu.VMEM((width, ch), F32),
        GR=pltpu.VMEM((width, ch), F32),
        KB1=pltpu.VMEM((4, 3 * c_in, ch), BF),
        KB2=pltpu.VMEM((4, 3 * ch, ch), BF),
        KU3=pltpu.VMEM((4, 3, ch, ch), BF),
        KB3=pltpu.VMEM((4, 3, ch, ch), BF),
        KB4=pltpu.VMEM((4, 3 * ch, ch), BF),
        KT1=pltpu.VMEM((4, c_in, 3 * ch), BF),
        KT2=pltpu.VMEM((4, ch, 3 * ch), BF),
        KT3=pltpu.VMEM((4, 2 * ch, 3 * ch), BF),
        KT4=pltpu.VMEM((4, ch, 3 * ch), BF),
        V3X=pltpu.VMEM((12, 3 * c_in, width), BF),
        V3A=pltpu.VMEM((10, width, 3 * ch), BF),
        V3U=pltpu.VMEM((8, width, 3 * ch), BF),
        V3B=pltpu.VMEM((8, width, 3 * ch), BF),
        V3C=pltpu.VMEM((6, width, 3 * ch), BF),
        VA=pltpu.VMEM((7, width, ch), BF),
        VJ=pltpu.VMEM((7, width, 2 * ch), BF),
        VC=pltpu.VMEM((7, width, ch), BF),
        S1=pltpu.VMEM((6, width, ch), F32),
        S2=pltpu.VMEM((4, width, ch), F32),
        S3=pltpu.VMEM((6, width, ch), F32),
        G4=pltpu.VMEM((8, width, ch), BF),
        G2=pltpu.VMEM((8, width, ch), BF),
        G34=pltpu.VMEM((8, width, 3 * ch), BF),
        G33=pltpu.VMEM((6, width, 3 * ch), BF),
        G32=pltpu.VMEM((8, width, 3 * ch), BF),
        G31=pltpu.VMEM((6, width, 3 * ch), BF),
        far_third=pltpu.VMEM((3 * ch, 6 * ch), F32),
        far_first=pltpu.VMEM((3 * c_in, 3 * ch), F32),
        GB=pltpu.VMEM((2, 2, half, 2 * ch), BF),
        SA=pltpu.VMEM((2, width, ch), F32),
        SB=pltpu.VMEM((width, ch), F32),
        DB=pltpu.VMEM((16, ch // 2), F32),
        ACT=pltpu.VMEM((4, width, ch), BF),
        POOL=pltpu.VMEM((2, half, ch), BF),
        GI=pltpu.VMEM((4, c_in, width), BF),
        GC=pltpu.VMEM((2, half, c_coarse), BF),
        local_sem=pltpu.SemaphoreType.DMA((64,)),
        halo_send=pltpu.SemaphoreType.DMA((9, 2)),
        halo_recv=pltpu.SemaphoreType.DMA((9, 2)),
        red_send=pltpu.SemaphoreType.DMA((6, 16)),
        red_recv=pltpu.SemaphoreType.DMA((6, 16)),
    )
    for name, count in tiles.items():

        def buffer(*lead):
            return pltpu.VMEM(lead + (16, 128), BF)

        landing = (canvas_n, count, 16, 128)
        scratch["P_" + name] = buffer(2, z_n, count)
        scratch["RA_" + name] = buffer(z_n, count)
        if name in WIDE:
            quarter = count // 4
            scratch["Q_" + name] = buffer(4, z_n, quarter)
            scratch["RB_" + name] = buffer(4, z_n, quarter)
            scratch["ZS_" + name] = buffer(z_n, quarter)
            scratch["ZL_" + name] = buffer(z_n, quarter)
            scratch["T_" + name] = buffer(quarter)
            landing = (4, quarter, 16, 128)
        else:
            scratch["Q_" + name] = buffer(z_n, count)
            scratch["RB_" + name] = buffer(z_n, count)
            scratch["T_" + name] = buffer(count)
        if not fused:
            landing = (2, z_n, count, 16, 128)
        outs["RC_" + name] = jax.ShapeDtypeStruct(landing, BF)

    names = list(arg) + list(outs) + list(scratch)
    sizes = (width, ch, c_in, c_coarse, rows_n, canvas_n, fused)
    results = pl.pallas_call(
        functools.partial(level_kernel, names, sizes),
        out_shape=tuple(outs.values()),
        in_specs=in_specs,
        out_specs=tuple(any_spec for _ in outs),
        scratch_shapes=list(scratch.values()),
        compiler_params=pltpu.CompilerParams(
            collective_id=0, has_side_effects=True, vmem_limit_bytes=VMEM_BYTES
        ),
        name="level",
    )(*(arg[name] for name in arg))
    held = dict(zip(outs, results))

    if not fused:
        return unfused_tail(held, rows_n, ch, c_in, c_coarse)

    done = {"out_" + name: outs[name] for name in BIG}
    parts = dict(first=c_in, second=ch, third=2 * ch, fourth=ch)
    for name in ORDER:
        shape = (2, 2, share, c_coarse) if name == UP else (3, 3, share, parts[name])
        done["out_w_" + name] = jax.ShapeDtypeStruct(shape, F32)
    for name in ORDER:
        done["out_b_" + name] = jax.ShapeDtypeStruct((1, share), F32)
    staged = {name: outs[name] for name in outs}
    staged.update({"w_" + name: done["out_w_" + name] for name in ORDER})
    staged.update({"b_" + name: done["out_b_" + name] for name in ORDER})
    finals = pl.pallas_call(
        functools.partial(finish_kernel, list(outs) + list(done), list(staged), (ch, share)),
        out_shape=tuple(done.values()),
        in_specs=[any_spec] * len(outs),
        out_specs=(any_spec,) * len(done),
        scratch_shapes=[pltpu.VMEM(like.shape, like.dtype) for like in staged.values()]
        + [pltpu.SemaphoreType.DMA((2, len(staged)))],
        name="finish",
    )(*results)
    final = dict(zip(done, finals))
    return ordered(
        {name: final["out_" + name] for name in BIG},
        {name: final["out_w_" + name] for name in ORDER},
        {name: final["out_b_" + name].reshape(share) for name in ORDER},
    )


def ordered(big, weights, biases):
    turned = {name: jnp.swapaxes(value, 2, 3) for name, value in weights.items()}
    pairs = []
    for name in ORDER:
        pairs += [turned[name], biases[name]]
    return (
        big["activations"],
        big["pooled"],
        jnp.swapaxes(big["grad_inputs"], 2, 3),
        big["grad_coarse"],
        *pairs,
    )


def unfused_tail(held, rows_n, ch, c_in, c_coarse):
    share = ch // rows_n
    offset = lax.axis_index("rows") * share

    def whole(name):
        parts = held["RC_" + name].astype(F32)
        return jnp.transpose(parts, (2, 1, 0, 3, 4)).reshape(-1, ch, 128)

    tiles = lax.psum({name: whole(name) for name in GROUPS}, ("canvas", "rows"))
    weights = {}
    for name in ORDER:
        if name == FIRST:
            whole_taps = tiles[FIRST][:3]
            rest = jnp.stack([tiles[FIRST][3][:, :c_in], tiles[FIRST][3][:, c_in:], tiles[FIRST][4][:, :c_in]])
            value = jnp.stack([whole_taps[..., :c_in], whole_taps[..., c_in:], rest], axis=1)[:, :, None]
        else:
            lanes, shape = (2, (4, 1)) if name == UP else (2 if name == THIRD else 1, (3, 3))
            count = lanes * shape[0] * shape[1]
            found = [place_of(name, place) for place in range(count)]
            value = jnp.stack([tiles[group][index] for group, index in found]).reshape(*shape, lanes, ch, 128)
        value = jnp.transpose(value, (1, 0, 3, 2, 4)).reshape(value.shape[1], value.shape[0], ch, -1)
        if name == UP:
            value = value.reshape(2, 2, ch, c_coarse)
        weights[name] = lax.dynamic_slice_in_dim(value, offset, share, 2)
    spare = tiles[FIRST][4][:, ch // 2 :]
    biases = lax.dynamic_slice_in_dim(jnp.concatenate([spare[0:5], spare[5:10]], axis=1), offset, share, 1)
    return ordered(held, weights, {name: biases[place] for place, name in enumerate(ORDER)})


def solution(mesh):
    rows_n, canvas_n = mesh.shape["rows"], mesh.shape["canvas"]
    fused = rows_n == 8 and canvas_n == 4
    split = P("canvas", "rows", None, None)
    pairs = (P(None, None, None, "rows"), P("rows"))
    return jax.shard_map(
        functools.partial(on_device, fused, rows_n, canvas_n),
        mesh=mesh,
        in_specs=(split, split, P("canvas", None), P("canvas", None)) + (P(),) * 10 + (split, split),
        out_specs=(split,) * 4 + pairs * 5,
        check_vma=False,
    )
```

```python
import functools
import types

import jax
import jax.numpy as jnp
from jax import lax
from jax.experimental import pallas as pl
from jax.experimental.pallas import tpu as pltpu
from jax.sharding import PartitionSpec as P

MESH = pl.DeviceIdType.MESH
BF = jnp.bfloat16
F32 = jnp.float32
VMEM_BYTES = 58 * 2**20

FIRST, SECOND, UP, THIRD, FOURTH = "first", "second", "up", "third", "fourth"
THIRD_A, THIRD_B = "third_a", "third_b"
GROUPS = (FOURTH, THIRD_A, THIRD_B, SECOND, UP, FIRST)
WIDE = (FOURTH, THIRD_A, SECOND, UP)
ORDER = (FIRST, SECOND, UP, THIRD, FOURTH)
BIG = ("activations", "pooled", "grad_inputs", "grad_coarse")


def place_of(layer, tile):
    if layer == THIRD:
        return (THIRD_A, tile) if tile < 8 else (THIRD_B, tile - 8)
    if layer == SECOND and tile == 8:
        return FIRST, 5
    return layer, tile


def peer_of(own, step):
    if step == 3:
        return 3 - own
    if step == 2:
        return lax.rem(own + 2, 4)
    return own + 1 - 2 * lax.rem(own, 2)


def dot_nn(a, b):
    return lax.dot_general(a, b, (((1,), (0,)), ((), ())), preferred_element_type=F32)


def dot_tn(a, b):
    return lax.dot_general(a, b, (((0,), (0,)), ((), ())), preferred_element_type=F32)


def dot_nt(a, b):
    return lax.dot_general(a, b, (((1,), (1,)), ((), ())), preferred_element_type=F32)


def silu_and_slope(values):
    sigma = 0.5 * jnp.tanh(0.5 * values) + 0.5
    act = values * sigma
    return act, sigma + act * (1.0 - sigma)


def level_kernel(names, sizes, *refs):
    ref = types.SimpleNamespace(**dict(zip(names, refs)))
    width, ch, c_in, c_coarse, rows_n, canvas_n, fused = sizes
    half = width // 2
    c = lax.axis_index("canvas")
    r = lax.axis_index("rows")
    z, k = r // 2, lax.rem(r, 2)
    z_n = rows_n // 2

    near_id, far_id = (c, r - 1 + 2 * k), (c, r + 1 - 2 * k)
    has_near = jnp.logical_and(near_id[1] >= 0, near_id[1] < rows_n)

    def flip(index, last):
        return index + k * (last - 2 * index)

    barrier = pltpu.get_barrier_semaphore()

    def greet(device):
        pl.semaphore_signal(barrier, inc=1, device_id=device, device_id_type=MESH)

    pl.when(has_near)(lambda: greet(near_id))
    greet(far_id)
    if fused:
        for step in range(1, z_n):
            greet((c, lax.rem(z + step, z_n) * 2 + k))
        for step in range(1, canvas_n):
            greet((lax.rem(c + step, canvas_n), r))

    used = [0]

    def fetch(src, dst):
        copy = pltpu.make_async_copy(src, dst, ref.local_sem.at[used[0]])
        used[0] += 1
        assert used[0] <= ref.local_sem.shape[0]
        copy.start()
        return copy

    def fetch_taps(weights, bank):
        return [fetch(weights.at[flip(tap, 2)], bank.at[1 + tap]) for tap in range(3)]

    def wait(copies):
        for copy in copies:
            copy.wait()

    X, CO, WU = ref.X, ref.CO, ref.WU
    KB1, KB2, KU3, KB3, KB4 = ref.KB1, ref.KB2, ref.KU3, ref.KB3, ref.KB4
    KT1, KT2, KT3, KT4 = ref.KT1, ref.KT2, ref.KT3, ref.KT4
    in_x = [fetch(ref.inputs.at[0, flip(row, 3)], X.at[4 + row]) for row in range(4)]
    in_w1 = fetch_taps(ref.w_first, KB1)

    def remote(src, dst, send, recv, device):
        return pltpu.make_async_remote_copy(
            src_ref=src, dst_ref=dst, send_sem=send, recv_sem=recv, device_id=device, device_id_type=MESH
        )

    halo_count = [0]

    def exchange(src_near, dst_near, src_far, dst_far):
        place = halo_count[0]
        halo_count[0] += 1
        near = remote(src_near, dst_near, ref.halo_send.at[place, 0], ref.halo_recv.at[place, 0], near_id)
        far = remote(src_far, dst_far, ref.halo_send.at[place, 1], ref.halo_recv.at[place, 1], far_id)
        return near, far

    def start_near(pairs):
        def start():
            for pair in pairs:
                pair[0].start()

        pl.when(has_near)(start)

    def start_far(pairs):
        for pair in pairs:
            pair[1].start()

    def receive_near(pairs):
        def receive():
            for pair in pairs:
                pair[0].wait_recv()

        pl.when(has_near)(receive)

    def receive_far(pairs):
        for pair in pairs:
            pair[1].wait_recv()

    def sent(pairs):
        def near():
            for pair in pairs:
                pair[0].wait_send()

        pl.when(has_near)(near)
        for pair in pairs:
            pair[1].wait_send()

    G4, G2 = ref.G4, ref.G2

    def row_exchange(buffer, row):
        return exchange(
            buffer.at[2 + row], buffer.at[1 - row], buffer.at[5 - row], buffer.at[6 + row]
        )

    x_halo = []
    for row in range(4):
        mine, last = ref.inputs.at[0, flip(row, 3)], ref.inputs.at[0, flip(3 - row, 3)]
        x_halo.append(exchange(mine, X.at[3 - row], last, X.at[8 + row]))
    co_halo = [exchange(ref.coarse.at[0, flip(0, 1)], CO.at[0], ref.coarse.at[0, flip(1, 1)], CO.at[3])]
    g4_halo = [row_exchange(G4, 0), row_exchange(G4, 1)]
    g2_halo, g2_second = [row_exchange(G2, 0)], [row_exchange(G2, 1)]

    in_co = [fetch(ref.coarse.at[0, flip(i, 1)], CO.at[1 + i]) for i in (0, 1)]
    in_up = [
        fetch(ref.w_up.at[flip(a, 1), b], WU.at[:, pl.ds((2 * a + b) * ch, ch)]) for a in (0, 1) for b in (0, 1)
    ]
    in_w2 = fetch_taps(ref.w_second, KB2)
    in_w3 = [
        fetch(ref.w_third.at[flip(tap, 2), :, pl.ds(lo, ch)], bank.at[1 + tap])
        for bank, lo in ((KU3, 0), (KB3, ch))
        for tap in range(3)
    ]
    in_w4 = fetch_taps(ref.w_fourth, KB4)
    in_cot = [fetch(ref.cot_out.at[0, flip(row, 3)], ref.COT.at[row]) for row in range(4)]
    in_cp = [fetch(ref.cot_pool.at[0, flip(i, 1)], ref.CP.at[i]) for i in (0, 1)]

    @pl.when(jnp.logical_not(has_near))
    def _():
        X[0:4] = jnp.zeros((4,) + X.shape[1:], BF)
        CO[0] = jnp.zeros(CO.shape[1:], BF)
        G4[0:2] = jnp.zeros((2,) + G4.shape[1:], BF)
        G2[0:2] = jnp.zeros((2,) + G2.shape[1:], BF)

    first, total_rows = r * 4, rows_n * 4

    def link(h):
        row = first + flip(h, 4)
        inside = jnp.logical_and(row > 0, row < total_rows)
        cut = ref.row_cuts[0, jnp.clip(row, 0, total_rows - 1)]
        return jnp.where(inside, 1 - cut, 0)

    open_row = 1.0 - ref.col_cuts[...].astype(F32)
    open_row = jnp.where(lax.broadcasted_iota(jnp.int32, (1, width), 1) > 0, open_row, 0.0)
    left_gate = jnp.broadcast_to(open_row, (128, width))
    right_gate = pltpu.roll(left_gate, width - 1, 1)
    GL, GR = ref.GL, ref.GR
    GL[...] = left_gate.T
    GR[...] = right_gate.T
    left_row, right_row = left_gate[:c_in], right_gate[:c_in]

    for bank in (KB1, KB2, KU3, KB3, KB4, KT1, KT2, KT3, KT4, ref.VA, ref.VJ, ref.VC):
        bank[0] = jnp.zeros(bank.shape[1:], BF)
    X[12] = jnp.zeros(X.shape[1:], BF)
    ref.P_fourth[:, :, 9:] = jnp.zeros((2, ref.P_fourth.shape[1], 3, 16, 128), BF)
    peers = (z_n - 1 + canvas_n - 1) if fused else 0
    pl.semaphore_wait(barrier, peers + 1 + has_near.astype(jnp.int32))
    start_near(x_halo)
    start_far(x_halo)
    start_far(co_halo)

    def put_wide(dst, row, value, base=0, stride=ch):
        left = (pltpu.roll(value, 1, 0) * GL[...]).astype(BF)
        right = (pltpu.roll(value, width - 1, 0) * GR[...]).astype(BF)
        for place, piece in enumerate((left, value.astype(BF), right)):
            lo = base + place * stride
            dst[row, :, lo : lo + ch] = piece

    def taps(bank, h):
        ga, gb, gc = link(h), link(h + 1), link(h + 2)
        found = bank[0], bank[ga], bank[2], bank[gb * 3], bank[gb], bank[gc * 3]
        return [tap.reshape(-1, tap.shape[-1]) for tap in found]

    def forward_weights(bank, h):
        zero, up0, mid, down0, up1, down1 = taps(bank, h)
        return jnp.concatenate(
            [
                jnp.concatenate([up0, mid, down0, zero], axis=0),
                jnp.concatenate([zero, up1, mid, down1], axis=0),
            ],
            axis=1,
        )

    def back_weights(bank, h):
        zero, up0, mid, down0, up1, down1 = taps(bank, h)
        return jnp.concatenate(
            [
                jnp.concatenate([up0, mid, down0, zero], axis=1),
                jnp.concatenate([zero, up1, mid, down1], axis=1),
            ],
            axis=0,
        )

    def band(src, at, reach=(-1, 0, 1, 2)):
        return jnp.concatenate([src[at + d] for d in reach], axis=1)

    def conv_pair(src, at, bank, h):
        return dot_nn(band(src, at), forward_weights(bank, h))

    def back_pair(src, at, bank, h):
        return dot_nt(band(src, at), back_weights(bank, h))

    def back_row(src, at, bank, h):
        weights = jnp.concatenate([bank[link(h)], bank[2], bank[link(h + 1) * 3]], axis=1)
        return dot_nt(band(src, at, (-1, 0, 1)), weights)

    def bias(layer):
        return getattr(ref, "b_" + layer)[...].astype(F32).reshape(1, ch)

    b_first, b_second, b_up, b_third, b_fourth = (bias(layer) for layer in ORDER)
    V3X, V3A, V3U, V3B, V3C = ref.V3X, ref.V3A, ref.V3U, ref.V3B, ref.V3C
    VA, VJ, VC = ref.VA, ref.VJ, ref.VC
    S1, S2, S3 = ref.S1, ref.S2, ref.S3
    SA, SB = ref.SA, ref.SB

    def widen_input(row):
        value = X[row].astype(F32)
        V3X[row, 0:c_in] = (pltpu.roll(value, 1, 1) * left_row).astype(BF)
        V3X[row, c_in : 2 * c_in] = X[row]
        V3X[row, 2 * c_in : 3 * c_in] = (pltpu.roll(value, width - 1, 1) * right_row).astype(BF)

    def first_pair(h):
        rows = V3X[h + 3 : h + 7].reshape(4 * 3 * c_in, width)
        both = dot_tn(rows, forward_weights(KB1, h))
        for j in (0, 1):
            act, slope = silu_and_slope(both[:, j * ch : (j + 1) * ch] + b_first)
            if -1 <= h + j < 5:
                S1[h + j + 1] = slope
                VA[h + j + 2] = act.astype(BF)
            put_wide(V3A, h + j + 3, act)

    def up_rows(i):
        fine = dot_nn(CO[i], WU[...])
        for a in (0, 1):
            for b in (0, 1):
                lo = (2 * a + b) * ch
                SA[a, pl.ds(b, half, stride=2), :] = (fine[:, lo : lo + ch] + b_up).astype(BF).astype(F32)
        for a in (0, 1):
            value = SA[a]
            row = 2 * i + a - 2
            put_wide(V3U, row + 2, value)
            if -1 <= row < 5:
                VJ[row + 2, :, :ch] = value.astype(BF)

    def second_pair(h):
        both = conv_pair(V3A, h + 3, KB2, h)
        for j in (0, 1):
            act, slope = silu_and_slope(both[:, j * ch : (j + 1) * ch] + b_second)
            if 0 <= h + j < 4:
                S2[h + j] = slope
            put_wide(V3B, h + j + 2, act)
            if -1 <= h + j < 5:
                VJ[h + j + 2, :, ch:] = act.astype(BF)

    def pool(i):
        SB[...] = VJ[2 * i + 2, :, ch:].astype(F32) + VJ[2 * i + 3, :, ch:].astype(F32)
        ref.POOL[i] = (
            (SB[pl.ds(0, half, stride=2), :] + SB[pl.ds(1, half, stride=2), :]) * 0.25
        ).astype(BF)

    def third_pair(h):
        both = conv_pair(V3U, h + 2, KU3, h) + conv_pair(V3B, h + 2, KB3, h)
        for j in (0, 1):
            act, slope = silu_and_slope(both[:, j * ch : (j + 1) * ch] + b_third)
            S3[h + j + 1] = slope
            put_wide(V3C, h + j + 1, act)
            VC[h + j + 2] = act.astype(BF)

    def turn(bank, back, part, lo=0):
        for row_tap in range(3):
            taps_of = bank[1 + row_tap].reshape(3, part, ch)
            for col_tap in range(3):
                back[3 - row_tap, lo : lo + part, (2 - col_tap) * ch : (3 - col_tap) * ch] = taps_of[col_tap]

    wait(in_x)
    wait(in_w1)
    wait(in_co)
    wait(in_up)
    for row in (4, 5, 6, 7):
        widen_input(row)
    first_pair(1)
    up_rows(1)
    up_rows(2)
    start_near(co_halo)
    wait(in_w2)
    wait(in_w3)
    wait(in_w4)
    turn(KB4, KT4, ch)
    turn(KU3, KT3, ch)
    turn(KB3, KT3, ch, ch)
    turn(KB2, KT2, ch)
    turn(KB1, KT1, c_in)
    wait(in_cot)
    wait(in_cp)

    receive_far(x_halo)
    receive_far(co_halo)
    for row in (8, 9, 10, 11):
        widen_input(row)
    first_pair(3)
    first_pair(5)
    up_rows(3)
    second_pair(2)
    second_pair(4)
    third_pair(3)

    receive_near(x_halo)
    receive_near(co_halo)
    for row in (0, 1, 2, 3):
        widen_input(row)
    first_pair(-1)
    first_pair(-3)
    up_rows(0)
    second_pair(0)
    second_pair(-2)
    third_pair(1)
    third_pair(-1)

    G34, G33, G32, G31 = ref.G34, ref.G33, ref.G32, ref.G31
    COT, ACT = ref.COT, ref.ACT
    sums = {}

    def add_sum(layer, value):
        part = jnp.sum(value.reshape(-1, 8, ch), axis=0)
        sums[layer] = part if layer not in sums else sums[layer] + part

    def fourth_pair(h, send):
        both = conv_pair(V3C, h + 1, KB4, h)
        pending = []
        for j in (0, 1):
            act, slope = silu_and_slope(both[:, j * ch : (j + 1) * ch] + b_fourth)
            g = (COT[h + j].astype(F32) * slope).astype(BF)
            G4[h + j + 2] = g
            ACT[h + j] = act.astype(BF)
            pending.append(g)
        send(g4_halo)
        for j in (0, 1):
            g = pending[j].astype(F32)
            add_sum(FOURTH, g)
            put_wide(G34, h + j + 2, g)

    fourth_pair(0, start_near)
    fourth_pair(2, start_far)
    out_act = [fetch(ACT.at[row], ref.activations.at[0, flip(row, 3)]) for row in range(4)]

    class Reduction:
        def __init__(self, index, name):
            self.part, self.twin = getattr(ref, "P_" + name), getattr(ref, "RA_" + name)
            self.sums, self.along = getattr(ref, "Q_" + name), getattr(ref, "RB_" + name)
            self.total, self.slots = getattr(ref, "T_" + name), getattr(ref, "RC_" + name)
            self.index, self.name = index, name

        def copy(self, phase, step, src, dst, device):
            place = self.index, 4 * phase + step
            return remote(src, dst, ref.red_send.at[place], ref.red_recv.at[place], device)

        def to_core(self):
            if fused:
                self.core = self.copy(0, 0, self.part.at[1 - k], self.twin, far_id)
                self.core.start()

        def join_core(self):
            self.core.wait_recv()
            return self.part[k].astype(F32) + self.twin[...].astype(F32)

        def scatter(self, phase, own, n, src, dst, device):
            found = []
            for step in (3, 2, 1):
                other = peer_of(own, step)
                found.append(self.copy(phase, step, src.at[other], dst.at[own], device(other)))
                found[-1].start()
            return found

        def gather(self, phase, src):
            found = []
            for step in (3, 2, 1):
                other = peer_of(c, step)
                found.append(self.copy(phase, step, src, self.slots.at[c], (other, r)))
                found[-1].start()
            self.own = fetch(src, self.slots.at[c])
            return found

        def collect(self, copies, own, n, src, dst):
            for copy in copies:
                copy.wait_recv()
            total = src[own].astype(F32)
            for step in range(1, n):
                total = total + dst[lax.rem(own + step, n)].astype(F32)
            return total

        def second(self):
            if fused:
                self.sums[...] = self.join_core().astype(BF)
                self.z_copies = self.scatter(1, z, z_n, self.sums, self.along, lambda other: (c, other * 2 + k))

        def third(self):
            if fused:
                total = self.collect(self.z_copies, z, z_n, self.sums, self.along)
                self.total[...] = total.astype(BF)
                self.last = self.gather(2, self.total)

        def fourth(self):
            pass

        def settle_first(self):
            if fused:
                self.core.wait_send()

        def settle_z(self):
            if fused:
                for copy in self.z_copies:
                    copy.wait_send()

        def finish(self):
            if not fused:
                fetch(self.part, self.slots).wait()
                return
            self.own.wait()
            for copy in self.last:
                copy.wait()

    class WideReduction(Reduction):
        def second(self):
            if fused:
                total = self.join_core()
                quarter = total.shape[1] // canvas_n
                for place in range(canvas_n):
                    self.sums[place] = total[:, place * quarter : (place + 1) * quarter].astype(BF)
                self.c_copies = self.scatter(1, c, canvas_n, self.sums, self.along, lambda other: (other, r))

        def third(self):
            if fused:
                total = self.collect(self.c_copies, c, canvas_n, self.sums, self.along)
                self.zs, self.zl = getattr(ref, "ZS_" + self.name), getattr(ref, "ZL_" + self.name)
                self.zs[...] = total.astype(BF)
                self.z_copies = self.scatter(2, z, z_n, self.zs, self.zl, lambda other: (c, other * 2 + k))

        def fourth(self):
            if fused:
                total = self.collect(self.z_copies, z, z_n, self.zs, self.zl)
                self.total[...] = total.astype(BF)
                self.last = self.gather(3, self.total)

        def settle_first(self):
            if fused:
                self.core.wait_send()
                for copy in self.c_copies:
                    copy.wait_send()

    red = {
        name: (WideReduction if name in WIDE else Reduction)(index, name) for index, name in enumerate(GROUPS)
    }

    def put_tile(group, index, value):
        part = getattr(ref, "P_" + group)
        for owner in range(8):
            part[owner % 2, owner // 2, index] = value[16 * owner : 16 * owner + 16].astype(BF)

    def put_grad(layer, value):
        blocks, lanes = value.shape[0] // ch, value.shape[1] // 128
        for block in range(blocks):
            first = (block if layer == UP else blocks - 1 - block) * lanes
            for lane in range(lanes):
                put_tile(
                    *place_of(layer, first + lane),
                    value[block * ch : (block + 1) * ch, lane * 128 : (lane + 1) * 128],
                )

    def above_below(h, off, closed):
        above = closed + link(h) * (h - 1 + off - closed)
        below = closed + link(h + 1) * (h + 1 + off - closed)
        return jnp.where(k == 0, above, below), jnp.where(k == 0, below, above)

    def row_stack(src, h):
        above, below = above_below(h, 2, 0)
        return jnp.concatenate([src[above], src[h + 2], src[below]], axis=1)

    def weight_grad(grad3, at, src, lo=0, n=4):
        rows = grad3[at + lo : at + lo + n].reshape(n * width, 3 * ch)
        stacked = jnp.concatenate([row_stack(src, lo + h) for h in range(n)], axis=0)
        return dot_tn(rows, stacked)

    def load_wide(dst, row, src):
        put_wide(dst, row + 2, src[row + 2].astype(F32))

    def third_back(h):
        both = back_pair(G34, h + 2, KT4, h)
        for j in (0, 1):
            g = (both[:, j * ch : (j + 1) * ch] * S3[h + j + 1]).astype(BF).astype(F32)
            if 0 <= h + j < 4:
                add_sum(THIRD, g)
            put_wide(G33, h + j + 1, g)

    put_grad(FOURTH, weight_grad(G34, 2, VC))
    red[FOURTH].to_core()
    third_back(1)
    pool(0)
    pool(1)
    out_pool = [fetch(ref.POOL.at[i], ref.pooled.at[0, flip(i, 1)]) for i in (0, 1)]
    receive_far(g4_halo)
    load_wide(G34, 4, G4)
    load_wide(G34, 5, G4)
    third_back(3)
    ref.far_third[...] = weight_grad(G33, 1, VJ, 1, 3)
    red[FOURTH].second()
    receive_near(g4_halo)
    load_wide(G34, -1, G4)
    load_wide(G34, -2, G4)
    third_back(-1)

    GB, CP = ref.GB, ref.CP

    def joined_back(i, sends):
        spread = CP[i].astype(F32) * 0.25
        SB[pl.ds(0, half, stride=2), :] = spread
        SB[pl.ds(1, half, stride=2), :] = spread
        pending = []
        for a, send in enumerate(sends):
            row = 2 * i + a
            d_joined = back_row(G33, row + 1, KT3, row)
            g = ((d_joined[:, ch:] + SB[...]) * S2[row]).astype(BF)
            G2[row + 2] = g
            send()
            pending.append((a, row, d_joined[:, :ch], g))
        for a, row, d_up, g in pending:
            g_up = d_up.astype(BF).astype(F32)
            add_sum(UP, g_up)
            SA[a] = g_up
            for b in (0, 1):
                GB[i, a, :, b * ch : (b + 1) * ch] = SA[a, pl.ds(b, half, stride=2), :].astype(BF)
            g = g.astype(F32)
            add_sum(SECOND, g)
            put_wide(G32, row + 2, g)

    joined_back(0, (lambda: start_near(g2_halo), lambda: start_near(g2_second)))
    put_grad(THIRD, ref.far_third[...] + weight_grad(G33, 1, VJ, 0, 1))
    red[THIRD_B].to_core()
    red[THIRD_A].to_core()
    joined_back(1, (lambda: start_far(g2_second), lambda: start_far(g2_halo)))

    def bands(i, first, second):
        return jnp.concatenate([GB[i, first], GB[i, second]], axis=1)

    red[THIRD_B].second()
    red[THIRD_A].second()
    put_grad(SECOND, weight_grad(G32, 2, VA))
    red[SECOND].to_core()
    grad = dot_tn(
        jnp.concatenate([bands(0, k, 1 - k), bands(1, k, 1 - k)], axis=0), CO[1:3].reshape(2 * half, c_coarse)
    )
    put_grad(UP, grad)
    red[UP].to_core()

    def first_back(h):
        both = back_pair(G32, h + 2, KT2, h)
        for j in (0, 1):
            g = (both[:, j * ch : (j + 1) * ch] * S1[h + j + 1]).astype(BF).astype(F32)
            add_sum(FIRST, g)
            put_wide(G31, h + j + 1, g)

    def first_back_row(row):
        put_wide(G31, row + 1, (back_row(G32, row + 2, KT2, row) * S1[row + 1]).astype(BF).astype(F32))

    def first_grad(lo):
        stacks = []
        for h in (lo, lo + 1):
            above, below = above_below(h, 4, 12)
            stacks.append(jnp.concatenate([X[above], X[h + 4], X[below]], axis=0))
        rows = G31[lo + 1 : lo + 3].reshape(2 * width, 3 * ch)
        return dot_nn(jnp.concatenate(stacks, axis=1), rows)

    red[FOURTH].third()
    receive_far(g2_halo)
    receive_far(g2_second)
    load_wide(G32, 4, G2)
    load_wide(G32, 5, G2)
    first_back(2)
    red[SECOND].second()
    ref.far_first[...] = first_grad(2)
    red[UP].second()
    receive_near(g2_halo)
    load_wide(G32, -1, G2)
    first_back(0)

    grad = (ref.far_first[...] + first_grad(0)).T
    rest = [grad[lo : lo + ch, 128:] for lo in (2 * ch, ch, 0)]
    for tap in range(3):
        put_tile(FIRST, tap, grad[(2 - tap) * ch : (3 - tap) * ch, :128])
    put_tile(FIRST, 3, jnp.concatenate(rest[:2], axis=1))
    DB = ref.DB
    DB[...] = jnp.zeros(DB.shape, F32)
    for place, layer in enumerate(ORDER):
        total = jnp.sum(sums[layer], axis=0, keepdims=True)
        DB[place : place + 1] = total[:, : ch // 2]
        DB[5 + place : 6 + place] = total[:, ch // 2 :]
    spare = jnp.concatenate([DB[...]] * 8, axis=0)
    put_tile(FIRST, 4, jnp.concatenate([rest[2], spare], axis=1))
    red[FIRST].to_core()

    GI, GC = ref.GI, ref.GC

    def input_back(h):
        both = dot_nt(back_weights(KT1, h), band(G31, h + 1)).astype(BF)
        GI[h] = both[:c_in]
        GI[h + 1] = both[c_in:]

    red[THIRD_A].third()
    receive_near(g2_second)
    load_wide(G32, -2, G2)
    first_back_row(-1)
    red[FIRST].second()
    first_back_row(4)
    input_back(0)
    input_back(2)
    out_gi = [fetch(GI.at[row], ref.grad_inputs.at[0, flip(row, 3)]) for row in range(4)]
    red[THIRD_B].third()
    red[FOURTH].fourth()
    red[SECOND].third()
    red[UP].third()
    for i in (0, 1):
        GC[i] = dot_nt(bands(i, 0, 1), WU[...]).astype(BF)
    out_gc = [fetch(GC.at[i], ref.grad_coarse.at[0, flip(i, 1)]) for i in (0, 1)]
    for pairs in (x_halo, co_halo, g4_halo, g2_halo, g2_second):
        sent(pairs)
    wait(out_act)
    wait(out_pool)
    for name in GROUPS:
        red[name].settle_first()
    red[THIRD_A].fourth()
    red[FOURTH].settle_z()
    red[THIRD_B].settle_z()
    red[FOURTH].finish()
    red[THIRD_B].finish()
    red[FIRST].third()
    red[SECOND].fourth()
    red[UP].fourth()
    wait(out_gi)
    wait(out_gc)
    for name in (THIRD_A, FIRST, SECOND, UP):
        red[name].settle_z()
    for name in (THIRD_A, FIRST, SECOND, UP):
        red[name].finish()


def finish_kernel(names, staged, sizes, *refs):
    ref = types.SimpleNamespace(**dict(zip(names, refs)))
    held = types.SimpleNamespace(**dict(zip(staged, refs[len(names) : -1])))
    sem = refs[-1]
    ch, share = sizes
    r = lax.axis_index("rows")
    enter, leave = {}, {}
    for place, name in enumerate(staged):
        stage = getattr(held, name)
        if name in BIG or name.startswith("RC"):
            enter[name] = pltpu.make_async_copy(getattr(ref, name), stage, sem.at[0, place])
            enter[name].start()
        if not name.startswith("RC"):
            leave[name] = pltpu.make_async_copy(stage, getattr(ref, "out_" + name), sem.at[1, place])

    def tile(group, index):
        slots = getattr(held, "RC_" + group)
        if group in WIDE:
            quarter = slots.shape[1]
            return slots[index // quarter, index % quarter].astype(F32)
        value = slots[0, index].astype(F32)
        for place in range(1, slots.shape[0]):
            value = value + slots[place, index].astype(F32)
        return value

    for name in BIG:
        enter[name].wait()
        leave[name].start()
    for name in GROUPS:
        enter["RC_" + name].wait()
    for layer in ORDER:
        out = getattr(held, "w_" + layer)
        lanes = out.shape[3] // 128
        if layer == FIRST:
            part = out.shape[3]
            for col_tap in range(3):
                whole, rest = tile(FIRST, col_tap), tile(FIRST, 3 + col_tap // 2)
                lo = part * (col_tap % 2)
                out[0, col_tap] = whole[:, :part]
                out[1, col_tap] = whole[:, part:]
                out[2, col_tap] = rest[:, lo : lo + part]
        else:
            for place in range(out.shape[0] * out.shape[1]):
                col_tap, row_tap = place // out.shape[0], place % out.shape[0]
                first, second = (col_tap, row_tap) if layer == UP else (row_tap, col_tap)
                for lane in range(lanes):
                    value = tile(*place_of(layer, place * lanes + lane))
                    out[first, second, :, lane * 128 : (lane + 1) * 128] = value
        leave["w_" + layer].start()
    spare = tile(FIRST, 4)[:, ch // 2 :]
    sums = jnp.concatenate([spare[0:8], spare[5:13]], axis=1)
    sums = pltpu.roll(sums, lax.rem(ch - r * share, ch), 1)
    for place, layer in enumerate(ORDER):
        getattr(held, "b_" + layer)[...] = sums[place : place + 1, :share]
        leave["b_" + layer].start()
    for copy in leave.values():
        copy.wait()


def on_device(
    fused,
    rows_n,
    canvas_n,
    inputs,
    coarse,
    row_cuts,
    col_cuts,
    w_first,
    b_first,
    w_second,
    b_second,
    w_up,
    b_up,
    w_third,
    b_third,
    w_fourth,
    b_fourth,
    cot_out,
    cot_pool,
):
    arg = dict(
        inputs=inputs,
        coarse=coarse,
        row_cuts=row_cuts,
        col_cuts=col_cuts,
        w_first=w_first,
        b_first=b_first,
        w_second=w_second,
        b_second=b_second,
        w_up=w_up,
        b_up=b_up,
        w_third=w_third,
        b_third=b_third,
        w_fourth=w_fourth,
        b_fourth=b_fourth,
        cot_out=cot_out,
        cot_pool=cot_pool,
    )
    _, length, width, c_in = arg["inputs"].shape
    ch = arg["w_first"].shape[3]
    c_coarse = arg["coarse"].shape[3]
    half = width // 2
    assert length == 4
    arg["inputs"] = jnp.swapaxes(arg["inputs"], 2, 3)
    arg["w_first"] = arg["w_first"].reshape(3, 3 * c_in, ch)
    arg["w_second"] = arg["w_second"].reshape(3, 3 * ch, ch)
    arg["w_fourth"] = arg["w_fourth"].reshape(3, 3 * ch, ch)
    for name in ORDER:
        name = "b_" + name
        arg[name] = arg[name].reshape(1, ch)

    any_spec = pl.BlockSpec(memory_space=pl.ANY)
    vmem_spec = pl.BlockSpec(memory_space=pltpu.VMEM)
    in_specs = []
    for name in arg:
        if name == "row_cuts":
            in_specs.append(pl.BlockSpec(memory_space=pltpu.SMEM))
        elif name == "col_cuts" or name.startswith("b_"):
            in_specs.append(vmem_spec)
        else:
            in_specs.append(any_spec)

    owners, z_n = 8, 4
    share = ch // owners
    tiles = dict(fourth=12, third_a=8, third_b=10, second=8, up=8, first=6)
    outs = dict(
        activations=jax.ShapeDtypeStruct((1, 4, width, ch), BF),
        pooled=jax.ShapeDtypeStruct((1, 2, half, ch), BF),
        grad_inputs=jax.ShapeDtypeStruct((1, 4, c_in, width), BF),
        grad_coarse=jax.ShapeDtypeStruct((1, 2, half, c_coarse), BF),
    )
    scratch = dict(
        X=pltpu.VMEM((13, c_in, width), BF),
        CO=pltpu.VMEM((4, half, c_coarse), BF),
        COT=pltpu.VMEM((4, width, ch), BF),
        CP=pltpu.VMEM((2, half, ch), BF),
        WU=pltpu.VMEM((c_coarse, 4 * ch), BF),
        GL=pltpu.VMEM((width, ch), F32),
        GR=pltpu.VMEM((width, ch), F32),
        KB1=pltpu.VMEM((4, 3 * c_in, ch), BF),
        KB2=pltpu.VMEM((4, 3 * ch, ch), BF),
        KU3=pltpu.VMEM((4, 3, ch, ch), BF),
        KB3=pltpu.VMEM((4, 3, ch, ch), BF),
        KB4=pltpu.VMEM((4, 3 * ch, ch), BF),
        KT1=pltpu.VMEM((4, c_in, 3 * ch), BF),
        KT2=pltpu.VMEM((4, ch, 3 * ch), BF),
        KT3=pltpu.VMEM((4, 2 * ch, 3 * ch), BF),
        KT4=pltpu.VMEM((4, ch, 3 * ch), BF),
        V3X=pltpu.VMEM((12, 3 * c_in, width), BF),
        V3A=pltpu.VMEM((10, width, 3 * ch), BF),
        V3U=pltpu.VMEM((8, width, 3 * ch), BF),
        V3B=pltpu.VMEM((8, width, 3 * ch), BF),
        V3C=pltpu.VMEM((6, width, 3 * ch), BF),
        VA=pltpu.VMEM((7, width, ch), BF),
        VJ=pltpu.VMEM((7, width, 2 * ch), BF),
        VC=pltpu.VMEM((7, width, ch), BF),
        S1=pltpu.VMEM((6, width, ch), F32),
        S2=pltpu.VMEM((4, width, ch), F32),
        S3=pltpu.VMEM((6, width, ch), F32),
        G4=pltpu.VMEM((8, width, ch), BF),
        G2=pltpu.VMEM((8, width, ch), BF),
        G34=pltpu.VMEM((8, width, 3 * ch), BF),
        G33=pltpu.VMEM((6, width, 3 * ch), BF),
        G32=pltpu.VMEM((8, width, 3 * ch), BF),
        G31=pltpu.VMEM((6, width, 3 * ch), BF),
        far_third=pltpu.VMEM((3 * ch, 6 * ch), F32),
        far_first=pltpu.VMEM((3 * c_in, 3 * ch), F32),
        GB=pltpu.VMEM((2, 2, half, 2 * ch), BF),
        SA=pltpu.VMEM((2, width, ch), F32),
        SB=pltpu.VMEM((width, ch), F32),
        DB=pltpu.VMEM((16, ch // 2), F32),
        ACT=pltpu.VMEM((4, width, ch), BF),
        POOL=pltpu.VMEM((2, half, ch), BF),
        GI=pltpu.VMEM((4, c_in, width), BF),
        GC=pltpu.VMEM((2, half, c_coarse), BF),
        local_sem=pltpu.SemaphoreType.DMA((64,)),
        halo_send=pltpu.SemaphoreType.DMA((9, 2)),
        halo_recv=pltpu.SemaphoreType.DMA((9, 2)),
        red_send=pltpu.SemaphoreType.DMA((6, 16)),
        red_recv=pltpu.SemaphoreType.DMA((6, 16)),
    )
    for name, count in tiles.items():

        def buffer(*lead):
            return pltpu.VMEM(lead + (16, 128), BF)

        landing = (canvas_n, count, 16, 128)
        scratch["P_" + name] = buffer(2, z_n, count)
        scratch["RA_" + name] = buffer(z_n, count)
        if name in WIDE:
            quarter = count // 4
            scratch["Q_" + name] = buffer(4, z_n, quarter)
            scratch["RB_" + name] = buffer(4, z_n, quarter)
            scratch["ZS_" + name] = buffer(z_n, quarter)
            scratch["ZL_" + name] = buffer(z_n, quarter)
            scratch["T_" + name] = buffer(quarter)
            landing = (4, quarter, 16, 128)
        else:
            scratch["Q_" + name] = buffer(z_n, count)
            scratch["RB_" + name] = buffer(z_n, count)
            scratch["T_" + name] = buffer(count)
        if not fused:
            landing = (2, z_n, count, 16, 128)
        outs["RC_" + name] = jax.ShapeDtypeStruct(landing, BF)

    names = list(arg) + list(outs) + list(scratch)
    sizes = (width, ch, c_in, c_coarse, rows_n, canvas_n, fused)
    results = pl.pallas_call(
        functools.partial(level_kernel, names, sizes),
        out_shape=tuple(outs.values()),
        in_specs=in_specs,
        out_specs=tuple(any_spec for _ in outs),
        scratch_shapes=list(scratch.values()),
        compiler_params=pltpu.CompilerParams(
            collective_id=0, has_side_effects=True, vmem_limit_bytes=VMEM_BYTES
        ),
        name="level",
    )(*(arg[name] for name in arg))
    held = dict(zip(outs, results))

    if not fused:
        return unfused_tail(held, rows_n, ch, c_in, c_coarse)

    done = {"out_" + name: outs[name] for name in BIG}
    parts = dict(first=c_in, second=ch, third=2 * ch, fourth=ch)
    for name in ORDER:
        shape = (2, 2, share, c_coarse) if name == UP else (3, 3, share, parts[name])
        done["out_w_" + name] = jax.ShapeDtypeStruct(shape, F32)
    for name in ORDER:
        done["out_b_" + name] = jax.ShapeDtypeStruct((1, share), F32)
    staged = {name: outs[name] for name in outs}
    staged.update({"w_" + name: done["out_w_" + name] for name in ORDER})
    staged.update({"b_" + name: done["out_b_" + name] for name in ORDER})
    finals = pl.pallas_call(
        functools.partial(finish_kernel, list(outs) + list(done), list(staged), (ch, share)),
        out_shape=tuple(done.values()),
        in_specs=[any_spec] * len(outs),
        out_specs=(any_spec,) * len(done),
        scratch_shapes=[pltpu.VMEM(like.shape, like.dtype) for like in staged.values()]
        + [pltpu.SemaphoreType.DMA((2, len(staged)))],
        name="finish",
    )(*results)
    final = dict(zip(done, finals))
    return ordered(
        {name: final["out_" + name] for name in BIG},
        {name: final["out_w_" + name] for name in ORDER},
        {name: final["out_b_" + name].reshape(share) for name in ORDER},
    )


def ordered(big, weights, biases):
    turned = {name: jnp.swapaxes(value, 2, 3) for name, value in weights.items()}
    pairs = []
    for name in ORDER:
        pairs += [turned[name], biases[name]]
    return (
        big["activations"],
        big["pooled"],
        jnp.swapaxes(big["grad_inputs"], 2, 3),
        big["grad_coarse"],
        *pairs,
    )


def unfused_tail(held, rows_n, ch, c_in, c_coarse):
    share = ch // rows_n
    offset = lax.axis_index("rows") * share

    def whole(name):
        parts = held["RC_" + name].astype(F32)
        return jnp.transpose(parts, (2, 1, 0, 3, 4)).reshape(-1, ch, 128)

    tiles = lax.psum({name: whole(name) for name in GROUPS}, ("canvas", "rows"))
    weights = {}
    for name in ORDER:
        if name == FIRST:
            whole_taps = tiles[FIRST][:3]
            rest = jnp.stack([tiles[FIRST][3][:, :c_in], tiles[FIRST][3][:, c_in:], tiles[FIRST][4][:, :c_in]])
            value = jnp.stack([whole_taps[..., :c_in], whole_taps[..., c_in:], rest], axis=1)[:, :, None]
        else:
            lanes, shape = (2, (4, 1)) if name == UP else (2 if name == THIRD else 1, (3, 3))
            count = lanes * shape[0] * shape[1]
            found = [place_of(name, place) for place in range(count)]
            value = jnp.stack([tiles[group][index] for group, index in found]).reshape(*shape, lanes, ch, 128)
        value = jnp.transpose(value, (1, 0, 3, 2, 4)).reshape(value.shape[1], value.shape[0], ch, -1)
        if name == UP:
            value = value.reshape(2, 2, ch, c_coarse)
        weights[name] = lax.dynamic_slice_in_dim(value, offset, share, 2)
    spare = tiles[FIRST][4][:, ch // 2 :]
    biases = lax.dynamic_slice_in_dim(jnp.concatenate([spare[0:5], spare[5:10]], axis=1), offset, share, 1)
    return ordered(held, weights, {name: biases[place] for place, name in enumerate(ORDER)})


def solution(mesh):
    rows_n, canvas_n = mesh.shape["rows"], mesh.shape["canvas"]
    fused = rows_n == 8 and canvas_n == 4
    split = P("canvas", "rows", None, None)
    pairs = (P(None, None, None, "rows"), P("rows"))
    return jax.shard_map(
        functools.partial(on_device, fused, rows_n, canvas_n),
        mesh=mesh,
        in_specs=(split, split, P("canvas", None), P("canvas", None)) + (P(),) * 10 + (split, split),
        out_specs=(split,) * 4 + pairs * 5,
        check_vma=False,
    )
```
